32 devices in a mesh: frames: 2 (over y), gz: 16 (over z, x, core).
Axes of the slice: x: 2, y: 2, z: 4, core: 2. Of those that a mesh axis runs over, the one named last changes fastest.
Arguments:
- volume: float32 [64, 512, 1024], P('gz', 'frames'), parts along dimension 1, may hold values from -6 to 6
- tf_index: int32 [64, 512, 1024], P('gz', 'frames'), parts along dimension 1, may hold values from 0 to 7
- tf_color: float32 [3, 8], replicated, may hold values from 0.2 to 1
- tf_opacity: float32 [8], replicated, may hold values from 0.003 to 0.03
- order: int32 [32], P('frames'), parts along dimension 0, may hold values from 0 to 15, each once
Outputs:
- image: float32 [8, 256, 1024], P('frames', 'gz'), parts along dimension 0
The draws below stay inside these ranges and needn't reach their ends.
There are 2 independent parts, one for each index of `frames`. The reference program is written for one: setup_inputs(seed, part) draws one part's arguments, and reference() takes and returns one part's arrays. A program takes and returns all parts, laid end to end along the dimension named above; an argument that names none is the same for every part. Nothing has to cross between parts.
Inputs may be any that keep to these rules, and one draw needn't show every extreme that they name: `order`: each brick has a distinct rank; every rank of 0 to 15 appears once.
All inputs are finite; a program needn't handle non-finite values.
Results may differ from the reference program's by a relative error of at most 0.00076.
Values may be sent and summed in bfloat16 or wider, within the bound.
No kernel may reach another device: no remote copies, remote signals or barrier semaphores. Data moves between devices by JAX's collectives and lax.ppermute only.
A program may use at most 128 MiB of HBM per device.

```python
import math
import jax
import jax.numpy as jnp
from jax import lax

W = 1024
ROWS = 256
DZ = 4
NT = 8
DEPTH = 64
N_GZ = 16


def place_ends(entries, stream_key, smallest, top_value):
    extent = entries.shape
    index_at = [jax.random.randint(jax.random.fold_in(stream_key, axis), (), 0, extent[axis]) for axis in range(len(extent))]
    entries = entries.at[tuple(index_at)].set(smallest)
    longest = extent.index(max(extent))
    index_at[longest] = (index_at[longest] + 1) % extent[longest]
    return entries.at[tuple(index_at)].set(top_value)


def steps_of(key, extent, split, least, high):
    loudness, own = 1.0, jax.random.fold_in(key, 6)
    for axis_at, shards_of in split:
        draws = jnp.exp(jax.random.uniform(jax.random.fold_in(own, axis_at), (shards_of,), jnp.float32, least / len(split), high / len(split)))
        loudness = loudness * jnp.repeat(draws, extent[axis_at] // shards_of).reshape([-1 if axis == axis_at else 1 for axis in range(len(extent))])
    return loudness


def gaussian(stream_key, extent, width, reach, split=(), held_as=jnp.bfloat16):
    drawn = jax.random.normal(stream_key, extent, jnp.float32) * width
    if len(split) > 0:
        drawn = steps_of(stream_key, extent, split, -0.22, 0.18) * drawn
    return jnp.clip(drawn, min=-reach, max=reach).astype(held_as)


def setup_inputs(seed: int = 0, part: int = 0) -> dict:
    key_list = jax.random.split(jax.random.key(seed), 6)
    part_keys = jax.random.split(jax.random.fold_in(key_list[5], part), 6)
    return {
        "volume": gaussian(part_keys[0], (DEPTH, ROWS, W), 1.0, 6.0, ((0, 16),), jnp.float32),
        "tf_index": place_ends(jax.random.randint(part_keys[1], (DEPTH, ROWS, W), 0, NT), jax.random.fold_in(part_keys[1], 1), 0, NT - 1).astype(jnp.int32),
        "tf_color": jnp.clip(jax.random.uniform(key_list[2], (3, NT), jnp.float32, 0.2, 1.0), 0.2, 1.0),
        "tf_opacity": jnp.clip(jnp.exp(jax.random.uniform(key_list[3], (NT,), jnp.float32, math.log(0.003), math.log(0.03))), 0.003, 0.03),
        "order": jax.random.permutation(part_keys[4], N_GZ).astype(jnp.int32),
    }


def sample_brick(padded, materials_here, tf_color, tf_opacity):
    centre = padded[1:-1]
    grad_depth = 0.5 * (padded[2:] - padded[:-2])
    rows_padded = jnp.pad(centre, ((0, 0), (1, 1), (0, 0)))
    grad_row = 0.5 * (rows_padded[:, 2:] - rows_padded[:, :-2])
    cols_padded = jnp.pad(centre, ((0, 0), (0, 0), (1, 1)))
    grad_col = 0.5 * (cols_padded[:, :, 2:] - cols_padded[:, :, :-2])
    facing = jnp.abs(0.48 * grad_depth + 0.6 * grad_row + 0.64 * grad_col)
    shading = 0.35 + 0.65 * facing / jnp.sqrt(grad_depth * grad_depth + grad_row * grad_row + grad_col * grad_col + 1.0)
    opacity_cell = jnp.zeros_like(centre)
    tint_cell = jnp.zeros((3,) + centre.shape, centre.dtype)
    for material in range(tf_opacity.shape[0]):
        matches = materials_here == material
        opacity_cell = jnp.where(matches, tf_opacity[material], opacity_cell)
        tint_cell = jnp.where(matches[None], tf_color[:, material][:, None, None, None], tint_cell)
    alphas_cell = opacity_cell * (1.0 - jnp.exp(-centre * centre))
    colour = tint_cell * (shading * alphas_cell)[None]

    def advance(carry, sample_pair):
        colour_sum, transmit = carry
        alpha_slice, colour_slice = sample_pair
        return ((colour_sum + transmit[None] * colour_slice, transmit * (1.0 - alpha_slice)), None)
    initial = (jnp.zeros((3,) + centre.shape[1:], centre.dtype), jnp.ones(centre.shape[1:], centre.dtype))
    (colour_sum, transmit), _ = lax.scan(advance, initial, (alphas_cell, jnp.moveaxis(colour, 1, 0)))
    return jnp.concatenate([colour_sum, (1.0 - transmit)[None]], 0).astype(jnp.bfloat16)

def over(front_layer, back_layer):
    return front_layer + (1.0 - front_layer[3:4]) * back_layer

def reference(volume, tf_index, tf_color, tf_opacity, order):
    padded = jnp.pad(volume, ((1, 1), (0, 0), (0, 0)))
    sequence = jnp.argsort(order).astype(jnp.int32)

    def composite_step(canvas, brick_number):
        first_slice = (brick_number * DZ).astype(jnp.int32)
        window_slices = lax.dynamic_slice_in_dim(padded, first_slice, DZ + 2, 0)
        materials_here = lax.dynamic_slice_in_dim(tf_index, first_slice, DZ, 0)
        brick_image = sample_brick(window_slices, materials_here, tf_color, tf_opacity).astype(jnp.float32)
        return (over(canvas, brick_image), None)
    canvas, _ = lax.scan(composite_step, jnp.zeros((4, ROWS, W), jnp.float32), sequence)
    return canvas
```

```python
import functools

import jax
import jax.numpy as jnp
from jax import lax
from jax.experimental import pallas as pl
from jax.experimental.pallas import tpu as pltpu
from jax.sharding import PartitionSpec as P

REACH = 6.0
STEPS = 32767.0
BLOCK = 16
LANES = 128
PAD = 8
LIMIT = 40 * 1024 * 1024


def lookup(table, bits, row=None):
    b0, b1, b2 = bits
    at = (lambda m: table[m]) if row is None else (lambda m: table[row, m])
    pairs = [jnp.where(b0, at(2 * i + 1), at(2 * i)) for i in range(4)]
    low, high = jnp.where(b1, pairs[1], pairs[0]), jnp.where(b1, pairs[3], pairs[2])
    return jnp.where(b2, high, low)


def bits_of(index):
    return [(index & (1 << i)) != 0 for i in range(3)]


def alpha_of(centre, bits, opacity_ref):
    return lookup(opacity_ref, bits) * (1.0 - jnp.exp(-centre * centre))


def opacity_kernel(slices, blocks, volume_hbm, index_hbm, opacity_ref, out_ref, vol, idx, sems):
    def copies(i):
        rows = pl.ds(pl.multiple_of(i * BLOCK, BLOCK), BLOCK)
        return (
            pltpu.make_async_copy(volume_hbm.at[:, rows], vol.at[:, rows], sems.at[0, i]),
            pltpu.make_async_copy(index_hbm.at[:, rows], idx.at[:, rows], sems.at[1, i]),
        )

    @pl.loop(0, blocks)
    def _(i):
        for copy in copies(i):
            copy.start()

    @pl.loop(0, blocks)
    def _(i):
        for copy in copies(i):
            copy.wait()
        rows = pl.ds(pl.multiple_of(i * BLOCK, BLOCK), BLOCK)
        for j in range(vol.shape[2] // LANES):
            cols = pl.ds(j * LANES, LANES)
            transmit = None
            for k in range(slices):
                clear = 1.0 - alpha_of(vol[k, rows, cols], bits_of(idx[k, rows, cols]), opacity_ref)
                transmit = clear if transmit is None else transmit * clear
            out_ref[rows, cols] = (1.0 - transmit).astype(jnp.bfloat16)


def opacities(volume, tf_index, tf_opacity):
    slices, height, width = volume.shape
    blocks = height // BLOCK
    return pl.pallas_call(
        functools.partial(opacity_kernel, slices, blocks),
        out_shape=jax.ShapeDtypeStruct((height, width), jnp.bfloat16),
        in_specs=[
            pl.BlockSpec(memory_space=pl.ANY),
            pl.BlockSpec(memory_space=pl.ANY),
            pl.BlockSpec(memory_space=pltpu.SMEM),
        ],
        out_specs=pl.BlockSpec(memory_space=pltpu.VMEM),
        scratch_shapes=[
            pltpu.VMEM(volume.shape, jnp.float32),
            pltpu.VMEM(volume.shape, jnp.int32),
            pltpu.SemaphoreType.DMA((2, blocks)),
        ],
        compiler_params=pltpu.CompilerParams(vmem_limit_bytes=LIMIT),
        cost_estimate=pl.CostEstimate(
            flops=30 * volume.size, bytes_accessed=9 * volume.size, transcendentals=volume.size
        ),
        name="opacities",
    )(volume, tf_index, tf_opacity)


def colour_kernel(
    slices, blocks, first, count, volume_hbm, index_hbm, before_ref, after_ref, colour_ref, opacity_ref, out_ref, vol, idx, sems
):
    height, width = blocks * BLOCK, vol.shape[2]
    tiles = width // LANES

    def copies(i):
        start = pl.multiple_of(i * BLOCK, BLOCK)
        rows, padded = pl.ds(start, BLOCK), pl.ds(pl.multiple_of(start + PAD, PAD), BLOCK)
        return (
            pltpu.make_async_copy(volume_hbm.at[:, rows], vol.at[:, padded], sems.at[0, i]),
            pltpu.make_async_copy(index_hbm.at[:, rows], idx.at[:, rows], sems.at[1, i]),
        )

    @pl.loop(0, blocks)
    def _(i):
        for copy in copies(i):
            copy.start()

    edge = jnp.zeros((slices, PAD, width), jnp.float32)
    vol[:, pl.ds(0, PAD), :] = edge
    vol[:, pl.ds(PAD + height, PAD), :] = edge
    lane = lax.broadcasted_iota(jnp.int32, (BLOCK, LANES), 1)
    row = lax.broadcasted_iota(jnp.int32, (BLOCK, LANES), 0)
    at_left, at_right = lane == 0, lane == LANES - 1
    at_top, at_bottom = row == 0, row == BLOCK - 1
    copies(0)[0].wait()

    @pl.loop(0, blocks)
    def _(i):
        @pl.when(i + 1 < blocks)
        def _():
            copies(i + 1)[0].wait()

        copies(i)[1].wait()
        start = pl.multiple_of(i * BLOCK, BLOCK)
        rows = pl.ds(start, BLOCK)
        centre_rows = pl.ds(pl.multiple_of(start + PAD, PAD), BLOCK)
        upper_rows = pl.ds(start, PAD)
        lower_rows = pl.ds(pl.multiple_of(start + PAD + BLOCK, PAD), PAD)
        for j in range(count):
            tile = first + j
            cols = pl.ds(tile * LANES, LANES)
            halo = [
                ref[rows, cols].astype(jnp.float32) * (REACH / STEPS) for ref in (before_ref, after_ref)
            ]
            centres = [halo[0]] + [vol[k, centre_rows, cols] for k in range(slices)] + [halo[1]]
            transmit, sums = None, None
            for k in range(slices):
                centre = centres[k + 1]
                depth = centres[k + 2] - centres[k]
                upper, lower = vol[k, upper_rows, cols], vol[k, lower_rows, cols]
                up = jnp.where(
                    at_top, jnp.concatenate([pltpu.roll(upper, 1, 0)] * 2, 0), pltpu.roll(centre, 1, 0)
                )
                down = jnp.where(
                    at_bottom,
                    jnp.concatenate([pltpu.roll(lower, PAD - 1, 0)] * 2, 0),
                    pltpu.roll(centre, BLOCK - 1, 0),
                )
                across = down - up
                left_tile = vol[k, centre_rows, pl.ds((tile - 1) * LANES, LANES)] if tile > 0 else None
                right_tile = vol[k, centre_rows, pl.ds((tile + 1) * LANES, LANES)] if tile + 1 < tiles else None
                left_edge = 0.0 if left_tile is None else pltpu.roll(left_tile, 1, 1)
                right_edge = 0.0 if right_tile is None else pltpu.roll(right_tile, LANES - 1, 1)
                left = jnp.where(at_left, left_edge, pltpu.roll(centre, 1, 1))
                right = jnp.where(at_right, right_edge, pltpu.roll(centre, LANES - 1, 1))
                along = right - left
                facing = jnp.abs(0.48 * depth + 0.6 * across + 0.64 * along)
                squares = depth * depth + across * across + along * along + 4.0
                shading = 0.35 + 0.65 * facing * lax.rsqrt(squares)
                bits = bits_of(idx[k, rows, cols])
                alpha = alpha_of(centre, bits, opacity_ref)
                shown = shading * alpha
                if transmit is not None:
                    shown = transmit * shown
                terms = [lookup(colour_ref, bits, c) * shown for c in range(3)]
                sums = terms if sums is None else [s + t for s, t in zip(sums, terms)]
                if k + 1 < slices:
                    transmit = 1.0 - alpha if transmit is None else transmit * (1.0 - alpha)
            for c in range(3):
                out_ref[i, c, :, pl.ds(j * LANES, LANES)] = sums[c].astype(jnp.bfloat16)


def colours(volume, tf_index, before, after, tf_color, tf_opacity, first, count):
    slices, height, width = volume.shape
    blocks = height // BLOCK
    return pl.pallas_call(
        functools.partial(colour_kernel, slices, blocks, first, count),
        out_shape=jax.ShapeDtypeStruct((blocks, 3, BLOCK, count * LANES), jnp.bfloat16),
        in_specs=[
            pl.BlockSpec(memory_space=pl.ANY),
            pl.BlockSpec(memory_space=pl.ANY),
            pl.BlockSpec(memory_space=pltpu.VMEM),
            pl.BlockSpec(memory_space=pltpu.VMEM),
            pl.BlockSpec(memory_space=pltpu.SMEM),
            pl.BlockSpec(memory_space=pltpu.SMEM),
        ],
        out_specs=pl.BlockSpec(memory_space=pltpu.VMEM),
        scratch_shapes=[
            pltpu.VMEM((slices, height + 2 * PAD, width), jnp.float32),
            pltpu.VMEM(volume.shape, jnp.int32),
            pltpu.SemaphoreType.DMA((2, blocks)),
        ],
        compiler_params=pltpu.CompilerParams(vmem_limit_bytes=LIMIT),
        cost_estimate=pl.CostEstimate(
            flops=90 * slices * height * count * LANES,
            bytes_accessed=10 * volume.size,
            transcendentals=2 * slices * height * count * LANES,
        ),
        name="colours",
    )(volume, tf_index, before, after, tf_color, tf_opacity)


def blend_kernel(ranks, halves, order_ref, opacity_ref, *rest):
    colour_refs, out_ref, place = rest[:halves], rest[halves], rest[halves + 1]
    for b in range(ranks):
        place[order_ref[b]] = b
    for half, ref in enumerate(colour_refs):
        for j in range(ref.shape[3] // LANES):
            here = pl.ds(j * LANES, LANES)
            cols = pl.ds(half * ref.shape[3] + j * LANES, LANES)

            def step(rank, canvas):
                b = place[rank]
                opacity = opacity_ref[b, :, cols].astype(jnp.float32)
                clear = 1.0 - canvas[3]
                layers = [ref[b, c, :, here].astype(jnp.float32) for c in range(3)] + [opacity]
                return tuple(front + clear * back for front, back in zip(canvas, layers))

            canvas = lax.fori_loop(
                0, ranks, step, (jnp.zeros((opacity_ref.shape[1], LANES), jnp.float32),) * 4, unroll=True
            )
            for c in range(4):
                out_ref[c, :, cols] = canvas[c]


def blend(order, opacity, colour_parts):
    ranks, height, width = opacity.shape
    return pl.pallas_call(
        functools.partial(blend_kernel, ranks, len(colour_parts)),
        out_shape=jax.ShapeDtypeStruct((4, height, width), jnp.float32),
        in_specs=[pl.BlockSpec(memory_space=pltpu.SMEM)]
        + [pl.BlockSpec(memory_space=pltpu.VMEM)] * (1 + len(colour_parts)),
        out_specs=pl.BlockSpec(memory_space=pltpu.VMEM),
        scratch_shapes=[pltpu.SMEM((ranks,), jnp.int32)],
        compiler_params=pltpu.CompilerParams(vmem_limit_bytes=LIMIT),
        name="blend",
    )(order, opacity, *colour_parts)


def blend_plain(order, opacity, colour_parts):
    ranks = opacity.shape[0]
    place = jnp.zeros((ranks,), jnp.int32).at[order].set(jnp.arange(ranks, dtype=jnp.int32))
    layers = jnp.concatenate([jnp.concatenate(colour_parts, -1), opacity[:, None]], 1)

    def step(canvas, b):
        layer = lax.dynamic_index_in_dim(layers, b, 0, keepdims=False).astype(jnp.float32)
        return canvas + (1.0 - canvas[3:4]) * layer, None

    return lax.scan(step, jnp.zeros(layers.shape[1:], jnp.float32), place)[0]


def by_owner(blocks_first, devices):
    blocks, width = blocks_first.shape[0], blocks_first.shape[-1]
    middle = blocks_first.shape[1:-2]
    if blocks == devices:
        return blocks_first
    each = devices // blocks
    split = blocks_first.reshape((blocks,) + middle + (each, BLOCK // each, width))
    moved = jnp.moveaxis(split, len(middle) + 1, 1)
    return moved.reshape((devices,) + middle + (BLOCK // each, width))


def exchange(x):
    return lax.all_to_all(x, "gz", split_axis=0, concat_axis=0, tiled=True)


def coded(a_slice):
    return jnp.round(a_slice * (STEPS / REACH)).astype(jnp.int16)


def shards(volume, tf_index, tf_color, tf_opacity, order):
    devices = lax.axis_size("gz")
    slices, height, width = volume.shape
    up = [(i, i + 1) for i in range(devices - 1)]
    down = [(j, i) for i, j in up]
    before = lax.ppermute(coded(volume[slices - 1]), "gz", up)
    after = lax.ppermute(coded(volume[0]), "gz", down)
    opacity = opacities(volume, tf_index, tf_opacity).reshape(height // BLOCK, BLOCK, width)
    opacity = exchange(by_owner(opacity, devices))
    tiles = width // LANES
    half = tiles // 2
    parts = []
    for first in range(0, tiles, half):
        part = colours(volume, tf_index, before, after, tf_color, tf_opacity, first, half)
        parts.append(exchange(by_owner(part, devices)))
    whole_blocks = (height // devices) % BLOCK == 0
    return (blend if whole_blocks else blend_plain)(order, opacity, parts)


def solution(mesh):
    placed = (P("gz", "frames", None), P("gz", "frames", None), P(), P(), P("frames"))
    return jax.shard_map(
        shards, mesh=mesh, in_specs=placed, out_specs=P("frames", "gz", None), check_vma=False
    )
```

```python
import functools

import jax
import jax.numpy as jnp
from jax import lax
from jax.experimental import pallas as pl
from jax.experimental.pallas import tpu as pltpu
from jax.sharding import PartitionSpec as P

REACH = 6.0
STEPS = 32767.0
BLOCK = 16
LANES = 128
PAD = 8
NT = 8
LIMIT = 40 * 1024 * 1024


def spread(table_ref, *row):
    sublane = lax.broadcasted_iota(jnp.int32, (NT, LANES), 0)
    table = jnp.zeros((NT, LANES), jnp.float32)
    for m in range(NT):
        table = jnp.where(sublane == m, table_ref[(*row, m)], table)
    return table


def lookup(table, index):
    parts = [
        jnp.take_along_axis(table, index[r : r + NT], axis=0, mode="promise_in_bounds")
        for r in range(0, index.shape[0], NT)
    ]
    return jnp.concatenate(parts, 0)


def alpha_of(centre, index, table):
    return lookup(table, index) * (1.0 - jnp.exp(-centre * centre))


def fetched(source, target, sems, kind, tile, row):
    height = source.shape[1]
    return pltpu.make_async_copy(
        source.at[:, :, pl.ds(tile * LANES, LANES)], target.at[:, tile, pl.ds(row, height), :], sems.at[kind, tile]
    )


def opacity_kernel(slices, tiles, volume_hbm, index_hbm, opacity_ref, out_ref, vol, idx, sems):
    copies = [(fetched(volume_hbm, vol, sems, 0, t, 0), fetched(index_hbm, idx, sems, 1, t, 0)) for t in range(tiles)]
    for pair in copies:
        for copy in pair:
            copy.start()
    table = spread(opacity_ref)
    for t in range(tiles):
        for copy in copies[t]:
            copy.wait()

        @pl.loop(0, vol.shape[2] // BLOCK)
        def _(i):
            rows = pl.ds(pl.multiple_of(i * BLOCK, BLOCK), BLOCK)
            transmit = None
            for k in range(slices):
                clear = 1.0 - alpha_of(vol[k, t, rows, :], idx[k, t, rows, :], table)
                transmit = clear if transmit is None else transmit * clear
            out_ref[rows, pl.ds(t * LANES, LANES)] = (1.0 - transmit).astype(jnp.bfloat16)


def opacities(volume, tf_index, tf_opacity):
    slices, height, width = volume.shape
    tiles = width // LANES
    tiled = (slices, tiles, height, LANES)
    return pl.pallas_call(
        functools.partial(opacity_kernel, slices, tiles),
        out_shape=jax.ShapeDtypeStruct((height, width), jnp.bfloat16),
        in_specs=[
            pl.BlockSpec(memory_space=pltpu.HBM),
            pl.BlockSpec(memory_space=pltpu.HBM),
            pl.BlockSpec(memory_space=pltpu.SMEM),
        ],
        out_specs=pl.BlockSpec(memory_space=pltpu.VMEM),
        scratch_shapes=[
            pltpu.VMEM(tiled, jnp.float32),
            pltpu.VMEM(tiled, jnp.int32),
            pltpu.SemaphoreType.DMA((2, tiles)),
        ],
        compiler_params=pltpu.CompilerParams(vmem_limit_bytes=LIMIT),
        cost_estimate=pl.CostEstimate(
            flops=15 * volume.size, bytes_accessed=9 * volume.size, transcendentals=volume.size
        ),
        name="opacities",
    )(volume, tf_index, tf_opacity)


def colour_kernel(
    slices, tiles, first, count, volume_hbm, index_hbm, before_ref, after_ref, colour_ref, opacity_ref, out_ref, vol, idx, sems
):
    height = before_ref.shape[0]
    here = range(first, first + count)
    around = range(max(first - 1, 0), min(first + count + 1, tiles))
    volumes = {t: fetched(volume_hbm, vol, sems, 0, t, PAD) for t in around}
    indices = {t: fetched(index_hbm, idx, sems, 1, t, 0) for t in here}
    for t in around:
        volumes[t].start()
        if t in indices:
            indices[t].start()
    edge = jnp.zeros((slices, tiles, PAD, LANES), jnp.float32)
    vol[:, :, pl.ds(0, PAD), :] = edge
    vol[:, :, pl.ds(PAD + height, PAD), :] = edge
    lane = lax.broadcasted_iota(jnp.int32, (BLOCK, LANES), 1)
    at_left, at_right = lane == 0, lane == LANES - 1
    opacity_table = spread(opacity_ref)
    colour_tables = [spread(colour_ref, c) for c in range(3)]
    arrived = set()
    for t in here:
        for near in (t - 1, t, t + 1):
            if near in volumes and near not in arrived:
                volumes[near].wait()
                arrived.add(near)
        indices[t].wait()

        @pl.loop(0, height // BLOCK)
        def _(i):
            start = pl.multiple_of(i * BLOCK, BLOCK)
            rows = pl.ds(start, BLOCK)
            cols = pl.ds(t * LANES, LANES)
            halo = [ref[rows, cols].astype(jnp.float32) * (REACH / STEPS) for ref in (before_ref, after_ref)]
            inside = pl.ds(pl.multiple_of(start + PAD, PAD), BLOCK)
            centres = [halo[0]] + [vol[k, t, inside, :] for k in range(slices)] + [halo[1]]
            transmit, sums = None, None
            for k in range(slices):
                centre = centres[k + 1]
                depth = centres[k + 2] - centres[k]
                across = vol[k, t, pl.ds(start + (PAD + 1), BLOCK), :] - vol[k, t, pl.ds(start + (PAD - 1), BLOCK), :]
                left_edge = pltpu.roll(vol[k, t - 1, inside, :], 1, 1) if t > 0 else 0.0
                right_edge = pltpu.roll(vol[k, t + 1, inside, :], LANES - 1, 1) if t + 1 < tiles else 0.0
                left = jnp.where(at_left, left_edge, pltpu.roll(centre, 1, 1))
                right = jnp.where(at_right, right_edge, pltpu.roll(centre, LANES - 1, 1))
                along = right - left
                facing = jnp.abs(0.48 * depth + 0.6 * across + 0.64 * along)
                squares = depth * depth + across * across + along * along + 4.0
                shading = 0.35 + 0.65 * facing * lax.rsqrt(squares)
                index = idx[k, t, rows, :]
                alpha = alpha_of(centre, index, opacity_table)
                shown = shading * alpha
                if transmit is not None:
                    shown = transmit * shown
                terms = [lookup(table, index) * shown for table in colour_tables]
                sums = terms if sums is None else [s + add for s, add in zip(sums, terms)]
                if k + 1 < slices:
                    transmit = 1.0 - alpha if transmit is None else transmit * (1.0 - alpha)
            for c in range(3):
                out_ref[i, c, :, pl.ds((t - first) * LANES, LANES)] = sums[c].astype(jnp.bfloat16)


def colours(volume, tf_index, before, after, tf_color, tf_opacity, first, count):
    slices, height, width = volume.shape
    blocks, tiles = height // BLOCK, width // LANES
    return pl.pallas_call(
        functools.partial(colour_kernel, slices, tiles, first, count),
        out_shape=jax.ShapeDtypeStruct((blocks, 3, BLOCK, count * LANES), jnp.bfloat16),
        in_specs=[
            pl.BlockSpec(memory_space=pltpu.HBM),
            pl.BlockSpec(memory_space=pltpu.HBM),
            pl.BlockSpec(memory_space=pltpu.VMEM),
            pl.BlockSpec(memory_space=pltpu.VMEM),
            pl.BlockSpec(memory_space=pltpu.SMEM),
            pl.BlockSpec(memory_space=pltpu.SMEM),
        ],
        out_specs=pl.BlockSpec(memory_space=pltpu.VMEM),
        scratch_shapes=[
            pltpu.VMEM((slices, tiles, height + 2 * PAD, LANES), jnp.float32),
            pltpu.VMEM((slices, tiles, height, LANES), jnp.int32),
            pltpu.SemaphoreType.DMA((2, tiles)),
        ],
        compiler_params=pltpu.CompilerParams(vmem_limit_bytes=LIMIT),
        cost_estimate=pl.CostEstimate(
            flops=50 * slices * height * count * LANES,
            bytes_accessed=10 * volume.size,
            transcendentals=2 * slices * height * count * LANES,
        ),
        name="colours",
    )(volume, tf_index, before, after, tf_color, tf_opacity)


def blend_kernel(ranks, halves, order_ref, opacity_ref, *rest):
    colour_refs, out_ref, place = rest[:halves], rest[halves], rest[halves + 1]
    for b in range(ranks):
        place[order_ref[b]] = b
    for half, ref in enumerate(colour_refs):
        for j in range(ref.shape[3] // LANES):
            here = pl.ds(j * LANES, LANES)
            cols = pl.ds(half * ref.shape[3] + j * LANES, LANES)

            def step(rank, canvas):
                b = place[rank]
                opacity = opacity_ref[b, :, cols].astype(jnp.float32)
                clear = 1.0 - canvas[3]
                layers = [ref[b, c, :, here].astype(jnp.float32) for c in range(3)] + [opacity]
                return tuple(front + clear * back for front, back in zip(canvas, layers))

            canvas = lax.fori_loop(
                0, ranks, step, (jnp.zeros((opacity_ref.shape[1], LANES), jnp.float32),) * 4, unroll=True
            )
            for c in range(4):
                out_ref[c, :, cols] = canvas[c]


def blend(order, opacity, colour_parts):
    ranks, height, width = opacity.shape
    return pl.pallas_call(
        functools.partial(blend_kernel, ranks, len(colour_parts)),
        out_shape=jax.ShapeDtypeStruct((4, height, width), jnp.float32),
        in_specs=[pl.BlockSpec(memory_space=pltpu.SMEM)]
        + [pl.BlockSpec(memory_space=pltpu.VMEM)] * (1 + len(colour_parts)),
        out_specs=pl.BlockSpec(memory_space=pltpu.VMEM),
        scratch_shapes=[pltpu.SMEM((ranks,), jnp.int32)],
        compiler_params=pltpu.CompilerParams(vmem_limit_bytes=LIMIT),
        name="blend",
    )(order, opacity, *colour_parts)


def blend_plain(order, opacity, colour_parts):
    ranks = opacity.shape[0]
    place = jnp.zeros((ranks,), jnp.int32).at[order].set(jnp.arange(ranks, dtype=jnp.int32))
    layers = jnp.concatenate([jnp.concatenate(colour_parts, -1), opacity[:, None]], 1)

    def step(canvas, b):
        layer = lax.dynamic_index_in_dim(layers, b, 0, keepdims=False).astype(jnp.float32)
        return canvas + (1.0 - canvas[3:4]) * layer, None

    return lax.scan(step, jnp.zeros(layers.shape[1:], jnp.float32), place)[0]


def by_owner(blocks_first, devices):
    blocks, width = blocks_first.shape[0], blocks_first.shape[-1]
    middle = blocks_first.shape[1:-2]
    if blocks == devices:
        return blocks_first
    each = devices // blocks
    split = blocks_first.reshape((blocks,) + middle + (each, BLOCK // each, width))
    moved = jnp.moveaxis(split, len(middle) + 1, 1)
    return moved.reshape((devices,) + middle + (BLOCK // each, width))


def exchange(x):
    return lax.all_to_all(x, "gz", split_axis=0, concat_axis=0, tiled=True)


def coded(a_slice):
    return jnp.round(a_slice * (STEPS / REACH)).astype(jnp.int16)


def shards(volume, tf_index, tf_color, tf_opacity, order):
    devices = lax.axis_size("gz")
    slices, height, width = volume.shape
    up = [(i, i + 1) for i in range(devices - 1)]
    down = [(j, i) for i, j in up]
    last, initial = coded(volume[slices - 1]), coded(volume[0])
    before = lax.ppermute(last, "gz", up)
    after = lax.ppermute(initial, "gz", down)
    later, _ = lax.optimization_barrier((volume, (last, initial)))
    opacity = opacities(later, tf_index, tf_opacity).reshape(height // BLOCK, BLOCK, width)
    opacity = exchange(by_owner(opacity, devices))
    tiles = width // LANES
    half = tiles // 2
    parts = []
    for first in range(0, tiles, half):
        part = colours(volume, tf_index, before, after, tf_color, tf_opacity, first, half)
        parts.append(exchange(by_owner(part, devices)))
    whole_blocks = (height // devices) % BLOCK == 0
    return (blend if whole_blocks else blend_plain)(order, opacity, parts)


def solution(mesh):
    placed = (P("gz", "frames", None), P("gz", "frames", None), P(), P(), P("frames"))
    return jax.shard_map(
        shards, mesh=mesh, in_specs=placed, out_specs=P("frames", "gz", None), check_vma=False
    )
```

```python
import functools

import jax
import jax.numpy as jnp
from jax import lax
from jax.experimental import pallas as pl
from jax.experimental.pallas import tpu as pltpu
from jax.sharding import PartitionSpec as P

REACH = 6.0
STEPS = 32767.0
BLOCK = 16
LANES = 128
PAD = 8
NT = 8
LIMIT = 58 * 1024 * 1024
UNROLL = 4


def spread(table_ref, *row):
    sublane = lax.broadcasted_iota(jnp.int32, (NT, LANES), 0)
    table = jnp.zeros((NT, LANES), jnp.float32)
    for m in range(NT):
        table = jnp.where(sublane == m, table_ref[(*row, m)], table)
    return table


def lookup(table, index):
    parts = [
        jnp.take_along_axis(table, index[r : r + NT], axis=0, mode="promise_in_bounds")
        for r in range(0, index.shape[0], NT)
    ]
    return jnp.concatenate(parts, 0)


def alpha_of(centre, index, table):
    return lookup(table, index) * (1.0 - jnp.exp(-centre * centre))


def fetched(source, target, sems, kind, tile, row):
    height = source.shape[1]
    return pltpu.make_async_copy(
        source.at[:, :, pl.ds(tile * LANES, LANES)], target.at[:, tile, pl.ds(row, height), :], sems.at[kind, tile]
    )


def opacity_kernel(slices, tiles, volume_hbm, index_hbm, opacity_ref, out_ref, vol, idx, sems):
    copies = [(fetched(volume_hbm, vol, sems, 0, t, 0), fetched(index_hbm, idx, sems, 1, t, 0)) for t in range(tiles)]
    for pair in copies:
        for copy in pair:
            copy.start()
    table = spread(opacity_ref)
    for t in range(tiles):
        for copy in copies[t]:
            copy.wait()

        @pl.loop(0, vol.shape[2] // BLOCK, unroll=UNROLL)
        def _(i):
            rows = pl.ds(pl.multiple_of(i * BLOCK, BLOCK), BLOCK)
            transmit = None
            for k in range(slices):
                clear = 1.0 - alpha_of(vol[k, t, rows, :], idx[k, t, rows, :], table)
                transmit = clear if transmit is None else transmit * clear
            out_ref[rows, pl.ds(t * LANES, LANES)] = (1.0 - transmit).astype(jnp.bfloat16)


def opacities(volume, tf_index, tf_opacity):
    slices, height, width = volume.shape
    tiles = width // LANES
    tiled = (slices, tiles, height, LANES)
    return pl.pallas_call(
        functools.partial(opacity_kernel, slices, tiles),
        out_shape=jax.ShapeDtypeStruct((height, width), jnp.bfloat16),
        in_specs=[
            pl.BlockSpec(memory_space=pltpu.HBM),
            pl.BlockSpec(memory_space=pltpu.HBM),
            pl.BlockSpec(memory_space=pltpu.SMEM),
        ],
        out_specs=pl.BlockSpec(memory_space=pltpu.VMEM),
        scratch_shapes=[
            pltpu.VMEM(tiled, jnp.float32),
            pltpu.VMEM(tiled, jnp.int32),
            pltpu.SemaphoreType.DMA((2, tiles)),
        ],
        compiler_params=pltpu.CompilerParams(vmem_limit_bytes=LIMIT),
        cost_estimate=pl.CostEstimate(
            flops=15 * volume.size, bytes_accessed=9 * volume.size, transcendentals=volume.size
        ),
        name="opacities",
    )(volume, tf_index, tf_opacity)


def colour_kernel(
    slices, tiles, first, count, volume_hbm, index_hbm, before_ref, after_ref, colour_ref, opacity_ref, out_ref, vol, idx, sems
):
    height = before_ref.shape[0]
    here = range(first, first + count)
    around = range(max(first - 1, 0), min(first + count + 1, tiles))
    volumes = {t: fetched(volume_hbm, vol, sems, 0, t, PAD) for t in around}
    indices = {t: fetched(index_hbm, idx, sems, 1, t, 0) for t in here}
    for t in around:
        volumes[t].start()
        if t in indices:
            indices[t].start()
    edge = jnp.zeros((slices, tiles, PAD, LANES), jnp.float32)
    vol[:, :, pl.ds(0, PAD), :] = edge
    vol[:, :, pl.ds(PAD + height, PAD), :] = edge
    lane = lax.broadcasted_iota(jnp.int32, (BLOCK, LANES), 1)
    at_left, at_right = lane == 0, lane == LANES - 1
    opacity_table = spread(opacity_ref)
    colour_tables = [spread(colour_ref, c) for c in range(3)]
    arrived = set()
    for t in here:
        for near in (t - 1, t, t + 1):
            if near in volumes and near not in arrived:
                volumes[near].wait()
                arrived.add(near)
        indices[t].wait()

        @pl.loop(0, height // BLOCK, unroll=UNROLL)
        def _(i):
            start = pl.multiple_of(i * BLOCK, BLOCK)
            rows = pl.ds(start, BLOCK)
            cols = pl.ds(t * LANES, LANES)
            halo = [ref[rows, cols].astype(jnp.float32) * (REACH / STEPS) for ref in (before_ref, after_ref)]
            inside = pl.ds(pl.multiple_of(start + PAD, PAD), BLOCK)
            centres = [halo[0]] + [vol[k, t, inside, :] for k in range(slices)] + [halo[1]]
            transmit, sums = None, None
            for k in range(slices):
                centre = centres[k + 1]
                depth = centres[k + 2] - centres[k]
                across = vol[k, t, pl.ds(start + (PAD + 1), BLOCK), :] - vol[k, t, pl.ds(start + (PAD - 1), BLOCK), :]
                left_edge = pltpu.roll(vol[k, t - 1, inside, :], 1, 1) if t > 0 else 0.0
                right_edge = pltpu.roll(vol[k, t + 1, inside, :], LANES - 1, 1) if t + 1 < tiles else 0.0
                left = jnp.where(at_left, left_edge, pltpu.roll(centre, 1, 1))
                right = jnp.where(at_right, right_edge, pltpu.roll(centre, LANES - 1, 1))
                along = right - left
                facing = jnp.abs(0.48 * depth + 0.6 * across + 0.64 * along)
                squares = depth * depth + across * across + along * along + 4.0
                shading = 0.35 + 0.65 * facing * lax.rsqrt(squares)
                index = idx[k, t, rows, :]
                alpha = alpha_of(centre, index, opacity_table)
                shown = shading * alpha
                if transmit is not None:
                    shown = transmit * shown
                terms = [lookup(table, index) * shown for table in colour_tables]
                sums = terms if sums is None else [s + add for s, add in zip(sums, terms)]
                if k + 1 < slices:
                    transmit = 1.0 - alpha if transmit is None else transmit * (1.0 - alpha)
            for c in range(3):
                out_ref[i, c, :, pl.ds((t - first) * LANES, LANES)] = sums[c].astype(jnp.bfloat16)


def colours(volume, tf_index, before, after, tf_color, tf_opacity, first, count):
    slices, height, width = volume.shape
    blocks, tiles = height // BLOCK, width // LANES
    return pl.pallas_call(
        functools.partial(colour_kernel, slices, tiles, first, count),
        out_shape=jax.ShapeDtypeStruct((blocks, 3, BLOCK, count * LANES), jnp.bfloat16),
        in_specs=[
            pl.BlockSpec(memory_space=pltpu.HBM),
            pl.BlockSpec(memory_space=pltpu.HBM),
            pl.BlockSpec(memory_space=pltpu.VMEM),
            pl.BlockSpec(memory_space=pltpu.VMEM),
            pl.BlockSpec(memory_space=pltpu.SMEM),
            pl.BlockSpec(memory_space=pltpu.SMEM),
        ],
        out_specs=pl.BlockSpec(memory_space=pltpu.VMEM),
        scratch_shapes=[
            pltpu.VMEM((slices, tiles, height + 2 * PAD, LANES), jnp.float32),
            pltpu.VMEM((slices, tiles, height, LANES), jnp.int32),
            pltpu.SemaphoreType.DMA((2, tiles)),
        ],
        compiler_params=pltpu.CompilerParams(vmem_limit_bytes=LIMIT),
        cost_estimate=pl.CostEstimate(
            flops=50 * slices * height * count * LANES,
            bytes_accessed=400 * volume.size,
            transcendentals=2 * slices * height * count * LANES,
        ),
        name="colours",
    )(volume, tf_index, before, after, tf_color, tf_opacity)


def blend_kernel(ranks, halves, order_ref, opacity_ref, *rest):
    colour_refs, out_ref, place = rest[:halves], rest[halves], rest[halves + 1]
    for b in range(ranks):
        place[order_ref[b]] = b
    for half, ref in enumerate(colour_refs):
        for j in range(ref.shape[3] // LANES):
            here = pl.ds(j * LANES, LANES)
            cols = pl.ds(half * ref.shape[3] + j * LANES, LANES)

            def step(rank, canvas):
                b = place[rank]
                opacity = opacity_ref[b, :, cols].astype(jnp.float32)
                clear = 1.0 - canvas[3]
                layers = [ref[b, c, :, here].astype(jnp.float32) for c in range(3)] + [opacity]
                return tuple(front + clear * back for front, back in zip(canvas, layers))

            canvas = lax.fori_loop(
                0, ranks, step, (jnp.zeros((opacity_ref.shape[1], LANES), jnp.float32),) * 4, unroll=True
            )
            for c in range(4):
                out_ref[c, :, cols] = canvas[c]


def blend(order, opacity, colour_parts):
    ranks, height, width = opacity.shape
    return pl.pallas_call(
        functools.partial(blend_kernel, ranks, len(colour_parts)),
        out_shape=jax.ShapeDtypeStruct((4, height, width), jnp.float32),
        in_specs=[pl.BlockSpec(memory_space=pltpu.SMEM)]
        + [pl.BlockSpec(memory_space=pltpu.VMEM)] * (1 + len(colour_parts)),
        out_specs=pl.BlockSpec(memory_space=pltpu.VMEM),
        scratch_shapes=[pltpu.SMEM((ranks,), jnp.int32)],
        compiler_params=pltpu.CompilerParams(vmem_limit_bytes=LIMIT),
        name="blend",
    )(order, opacity, *colour_parts)


def blend_plain(order, opacity, colour_parts):
    ranks = opacity.shape[0]
    place = jnp.zeros((ranks,), jnp.int32).at[order].set(jnp.arange(ranks, dtype=jnp.int32))
    layers = jnp.concatenate([jnp.concatenate(colour_parts, -1), opacity[:, None]], 1)

    def step(canvas, b):
        layer = lax.dynamic_index_in_dim(layers, b, 0, keepdims=False).astype(jnp.float32)
        return canvas + (1.0 - canvas[3:4]) * layer, None

    return lax.scan(step, jnp.zeros(layers.shape[1:], jnp.float32), place)[0]


def by_owner(blocks_first, devices):
    blocks, width = blocks_first.shape[0], blocks_first.shape[-1]
    middle = blocks_first.shape[1:-2]
    if blocks == devices:
        return blocks_first
    each = devices // blocks
    split = blocks_first.reshape((blocks,) + middle + (each, BLOCK // each, width))
    moved = jnp.moveaxis(split, len(middle) + 1, 1)
    return moved.reshape((devices,) + middle + (BLOCK // each, width))


def exchange(x):
    return lax.all_to_all(x, "gz", split_axis=0, concat_axis=0, tiled=True)


def coded(a_slice):
    return jnp.round(a_slice * (STEPS / REACH)).astype(jnp.int16)


def shards(volume, tf_index, tf_color, tf_opacity, order):
    devices = lax.axis_size("gz")
    slices, height, width = volume.shape
    up = [(i, i + 1) for i in range(devices - 1)]
    down = [(j, i) for i, j in up]
    last, initial = coded(volume[slices - 1]), coded(volume[0])
    before = lax.ppermute(last, "gz", up)
    after = lax.ppermute(initial, "gz", down)
    later, _ = lax.optimization_barrier((volume, (last, initial)))
    opacity = opacities(later, tf_index, tf_opacity).reshape(height // BLOCK, BLOCK, width)
    opacity = exchange(by_owner(opacity, devices))
    colour = colours(volume, tf_index, before, after, tf_color, tf_opacity, 0, width // LANES)
    parts = [exchange(by_owner(colour, devices))]
    whole_blocks = (height // devices) % BLOCK == 0
    return (blend if whole_blocks else blend_plain)(order, opacity, parts)


def solution(mesh):
    placed = (P("gz", "frames", None), P("gz", "frames", None), P(), P(), P("frames"))
    return jax.shard_map(
        shards, mesh=mesh, in_specs=placed, out_specs=P("frames", "gz", None), check_vma=False
    )
```

```python
import functools

import jax
import jax.numpy as jnp
from jax import lax
from jax.experimental import pallas as pl
from jax.experimental.pallas import tpu as pltpu
from jax.sharding import PartitionSpec as P

REACH = 6.0
STEPS = 32767.0
BLOCK = 16
LANES = 128
PAD = 8
NT = 8
LIMIT = 58 * 1024 * 1024
BLEND_LIMIT = 16 * 1024 * 1024
UNROLL = 4


def spread(table_ref, *row):
    sublane = lax.broadcasted_iota(jnp.int32, (NT, LANES), 0)
    table = jnp.zeros((NT, LANES), jnp.float32)
    for m in range(NT):
        table = jnp.where(sublane == m, table_ref[(*row, m)], table)
    return table


def lookup(table, index):
    parts = [
        jnp.take_along_axis(table, index[r : r + NT], axis=0, mode="promise_in_bounds")
        for r in range(0, index.shape[0], NT)
    ]
    return jnp.concatenate(parts, 0)


def alpha_of(centre, index, table):
    return lookup(table, index) * (1.0 - jnp.exp(-centre * centre))


def fetched(source, target, sems, kind, tile, row):
    height = source.shape[1]
    return pltpu.make_async_copy(
        source.at[:, :, pl.ds(tile * LANES, LANES)], target.at[:, tile, pl.ds(row, height), :], sems.at[kind, tile]
    )


def opacity_kernel(slices, tiles, volume_hbm, index_hbm, opacity_ref, out_ref, vol, idx, sems):
    copies = [(fetched(volume_hbm, vol, sems, 0, t, 0), fetched(index_hbm, idx, sems, 1, t, 0)) for t in range(tiles)]
    for pair in copies:
        for copy in pair:
            copy.start()
    table = spread(opacity_ref)
    for t in range(tiles):
        for copy in copies[t]:
            copy.wait()

        @pl.loop(0, vol.shape[2] // BLOCK, unroll=UNROLL)
        def _(i):
            rows = pl.ds(pl.multiple_of(i * BLOCK, BLOCK), BLOCK)
            transmit = None
            for k in range(slices):
                clear = 1.0 - alpha_of(vol[k, t, rows, :], idx[k, t, rows, :], table)
                transmit = clear if transmit is None else transmit * clear
            out_ref[rows, pl.ds(t * LANES, LANES)] = (1.0 - transmit).astype(jnp.bfloat16)


def opacities(volume, tf_index, tf_opacity):
    slices, height, width = volume.shape
    tiles = width // LANES
    tiled = (slices, tiles, height, LANES)
    return pl.pallas_call(
        functools.partial(opacity_kernel, slices, tiles),
        out_shape=jax.ShapeDtypeStruct((height, width), jnp.bfloat16),
        in_specs=[
            pl.BlockSpec(memory_space=pltpu.HBM),
            pl.BlockSpec(memory_space=pltpu.HBM),
            pl.BlockSpec(memory_space=pltpu.SMEM),
        ],
        out_specs=pl.BlockSpec(memory_space=pltpu.VMEM),
        scratch_shapes=[
            pltpu.VMEM(tiled, jnp.float32),
            pltpu.VMEM(tiled, jnp.int32),
            pltpu.SemaphoreType.DMA((2, tiles)),
        ],
        compiler_params=pltpu.CompilerParams(vmem_limit_bytes=LIMIT),
        cost_estimate=pl.CostEstimate(
            flops=15 * volume.size, bytes_accessed=40 * volume.size, transcendentals=volume.size
        ),
        name="opacities",
    )(volume, tf_index, tf_opacity)


def colour_kernel(
    slices, tiles, first, count, volume_hbm, index_hbm, before_ref, after_ref, colour_ref, opacity_ref, out_ref, vol, idx, sems
):
    height = before_ref.shape[0]
    here = range(first, first + count)
    around = range(max(first - 1, 0), min(first + count + 1, tiles))
    volumes = {t: fetched(volume_hbm, vol, sems, 0, t, PAD) for t in around}
    indices = {t: fetched(index_hbm, idx, sems, 1, t, 0) for t in here}
    for t in around:
        volumes[t].start()
        if t in indices:
            indices[t].start()
    edge = jnp.zeros((slices, tiles, PAD, LANES), jnp.float32)
    vol[:, :, pl.ds(0, PAD), :] = edge
    vol[:, :, pl.ds(PAD + height, PAD), :] = edge
    lane = lax.broadcasted_iota(jnp.int32, (BLOCK, LANES), 1)
    at_left, at_right = lane == 0, lane == LANES - 1
    opacity_table = spread(opacity_ref)
    colour_tables = [spread(colour_ref, c) for c in range(3)]
    arrived = set()
    for t in here:
        for near in (t - 1, t, t + 1):
            if near in volumes and near not in arrived:
                volumes[near].wait()
                arrived.add(near)
        indices[t].wait()

        @pl.loop(0, height // BLOCK, unroll=UNROLL)
        def _(i):
            start = pl.multiple_of(i * BLOCK, BLOCK)
            rows = pl.ds(start, BLOCK)
            cols = pl.ds(t * LANES, LANES)
            halo = [ref[rows, cols].astype(jnp.float32) * (REACH / STEPS) for ref in (before_ref, after_ref)]
            inside = pl.ds(pl.multiple_of(start + PAD, PAD), BLOCK)
            centres = [halo[0]] + [vol[k, t, inside, :] for k in range(slices)] + [halo[1]]
            transmit, sums = None, None
            for k in range(slices):
                centre = centres[k + 1]
                depth = centres[k + 2] - centres[k]
                across = vol[k, t, pl.ds(start + (PAD + 1), BLOCK), :] - vol[k, t, pl.ds(start + (PAD - 1), BLOCK), :]
                left_edge = pltpu.roll(vol[k, t - 1, inside, :], 1, 1) if t > 0 else 0.0
                right_edge = pltpu.roll(vol[k, t + 1, inside, :], LANES - 1, 1) if t + 1 < tiles else 0.0
                left = jnp.where(at_left, left_edge, pltpu.roll(centre, 1, 1))
                right = jnp.where(at_right, right_edge, pltpu.roll(centre, LANES - 1, 1))
                along = right - left
                facing = jnp.abs(0.48 * depth + 0.6 * across + 0.64 * along)
                squares = depth * depth + across * across + along * along + 4.0
                shading = 0.35 + 0.65 * facing * lax.rsqrt(squares)
                index = idx[k, t, rows, :]
                alpha = alpha_of(centre, index, opacity_table)
                shown = shading * alpha
                if transmit is not None:
                    shown = transmit * shown
                terms = [lookup(table, index) * shown for table in colour_tables]
                sums = terms if sums is None else [s + add for s, add in zip(sums, terms)]
                if k + 1 < slices:
                    transmit = 1.0 - alpha if transmit is None else transmit * (1.0 - alpha)
            for c in range(3):
                out_ref[i, c, :, pl.ds((t - first) * LANES, LANES)] = sums[c].astype(jnp.bfloat16)


def colours(volume, tf_index, before, after, tf_color, tf_opacity, first, count):
    slices, height, width = volume.shape
    blocks, tiles = height // BLOCK, width // LANES
    return pl.pallas_call(
        functools.partial(colour_kernel, slices, tiles, first, count),
        out_shape=jax.ShapeDtypeStruct((blocks, 3, BLOCK, count * LANES), jnp.bfloat16),
        in_specs=[
            pl.BlockSpec(memory_space=pltpu.HBM),
            pl.BlockSpec(memory_space=pltpu.HBM),
            pl.BlockSpec(memory_space=pltpu.VMEM),
            pl.BlockSpec(memory_space=pltpu.VMEM),
            pl.BlockSpec(memory_space=pltpu.SMEM),
            pl.BlockSpec(memory_space=pltpu.SMEM),
        ],
        out_specs=pl.BlockSpec(memory_space=pltpu.VMEM),
        scratch_shapes=[
            pltpu.VMEM((slices, tiles, height + 2 * PAD, LANES), jnp.float32),
            pltpu.VMEM((slices, tiles, height, LANES), jnp.int32),
            pltpu.SemaphoreType.DMA((2, tiles)),
        ],
        compiler_params=pltpu.CompilerParams(vmem_limit_bytes=LIMIT),
        cost_estimate=pl.CostEstimate(
            flops=50 * slices * height * count * LANES,
            bytes_accessed=1000000 * volume.size,
            transcendentals=2 * slices * height * count * LANES,
        ),
        name="colours",
    )(volume, tf_index, before, after, tf_color, tf_opacity)


def blend_kernel(ranks, halves, order_ref, opacity_ref, *rest):
    colour_refs, out_ref, place = rest[:halves], rest[halves], rest[halves + 1]
    for b in range(ranks):
        place[order_ref[b]] = b
    for half, ref in enumerate(colour_refs):
        for j in range(ref.shape[3] // LANES):
            here = pl.ds(j * LANES, LANES)
            cols = pl.ds(half * ref.shape[3] + j * LANES, LANES)

            def step(rank, canvas):
                b = place[rank]
                opacity = opacity_ref[b, :, cols].astype(jnp.float32)
                clear = 1.0 - canvas[3]
                layers = [ref[b, c, :, here].astype(jnp.float32) for c in range(3)] + [opacity]
                return tuple(front + clear * back for front, back in zip(canvas, layers))

            canvas = lax.fori_loop(
                0, ranks, step, (jnp.zeros((opacity_ref.shape[1], LANES), jnp.float32),) * 4, unroll=True
            )
            for c in range(4):
                out_ref[c, :, cols] = canvas[c]


def blend(order, opacity, colour_parts):
    ranks, height, width = opacity.shape
    return pl.pallas_call(
        functools.partial(blend_kernel, ranks, len(colour_parts)),
        out_shape=jax.ShapeDtypeStruct((4, height, width), jnp.float32),
        in_specs=[pl.BlockSpec(memory_space=pltpu.SMEM)]
        + [pl.BlockSpec(memory_space=pltpu.VMEM)] * (1 + len(colour_parts)),
        out_specs=pl.BlockSpec(memory_space=pltpu.VMEM),
        scratch_shapes=[pltpu.SMEM((ranks,), jnp.int32)],
        compiler_params=pltpu.CompilerParams(vmem_limit_bytes=BLEND_LIMIT),
        name="blend",
    )(order, opacity, *colour_parts)


def blend_plain(order, opacity, colour_parts):
    ranks = opacity.shape[0]
    place = jnp.zeros((ranks,), jnp.int32).at[order].set(jnp.arange(ranks, dtype=jnp.int32))
    layers = jnp.concatenate([jnp.concatenate(colour_parts, -1), opacity[:, None]], 1)

    def step(canvas, b):
        layer = lax.dynamic_index_in_dim(layers, b, 0, keepdims=False).astype(jnp.float32)
        return canvas + (1.0 - canvas[3:4]) * layer, None

    return lax.scan(step, jnp.zeros(layers.shape[1:], jnp.float32), place)[0]


def by_owner(blocks_first, devices):
    blocks, width = blocks_first.shape[0], blocks_first.shape[-1]
    middle = blocks_first.shape[1:-2]
    if blocks == devices:
        return blocks_first
    each = devices // blocks
    split = blocks_first.reshape((blocks,) + middle + (each, BLOCK // each, width))
    moved = jnp.moveaxis(split, len(middle) + 1, 1)
    return moved.reshape((devices,) + middle + (BLOCK // each, width))


def exchange(x):
    return lax.all_to_all(x, "gz", split_axis=0, concat_axis=0, tiled=True)


def coded(a_slice):
    return jnp.round(a_slice * (STEPS / REACH)).astype(jnp.int16)


def shards(volume, tf_index, tf_color, tf_opacity, order):
    devices = lax.axis_size("gz")
    slices, height, width = volume.shape
    up = [(i, i + 1) for i in range(devices - 1)]
    down = [(j, i) for i, j in up]
    last, initial = coded(volume[slices - 1]), coded(volume[0])
    before = lax.ppermute(last, "gz", up)
    after = lax.ppermute(initial, "gz", down)
    later, _ = lax.optimization_barrier((volume, (last, initial)))
    opacity = opacities(later, tf_index, tf_opacity).reshape(height // BLOCK, BLOCK, width)
    opacity = exchange(by_owner(opacity, devices))
    colour = colours(volume, tf_index, before, after, tf_color, tf_opacity, 0, width // LANES)
    parts = [exchange(by_owner(colour, devices))]
    whole_blocks = (height // devices) % BLOCK == 0
    return (blend if whole_blocks else blend_plain)(order, opacity, parts)


def solution(mesh):
    placed = (P("gz", "frames", None), P("gz", "frames", None), P(), P(), P("frames"))
    return jax.shard_map(
        shards, mesh=mesh, in_specs=placed, out_specs=P("frames", "gz", None), check_vma=False
    )
```

```python
import functools

import jax
import jax.numpy as jnp
from jax import lax
from jax.experimental import pallas as pl
from jax.experimental.pallas import tpu as pltpu
from jax.sharding import PartitionSpec as P

REACH = 6.0
STEPS = 32767.0
BLOCK = 16
LANES = 128
PAD = 8
NT = 8
LIMIT = 58 * 1024 * 1024
BLEND_LIMIT = 16 * 1024 * 1024
UNROLL = 4
PLANES = 4


def spread(table_ref, *row):
    sublane = lax.broadcasted_iota(jnp.int32, (NT, LANES), 0)
    table = jnp.zeros((NT, LANES), jnp.float32)
    for m in range(NT):
        table = jnp.where(sublane == m, table_ref[(*row, m)], table)
    return table


def lookup(table, index):
    parts = [
        jnp.take_along_axis(table, index[r : r + NT], axis=0, mode="promise_in_bounds")
        for r in range(0, index.shape[0], NT)
    ]
    return jnp.concatenate(parts, 0)


def alpha_of(centre, index, table):
    return lookup(table, index) * (1.0 - jnp.exp(-centre * centre))


def fetched(source, target, sems, kind, tile, row):
    height = source.shape[1]
    return pltpu.make_async_copy(
        source.at[:, :, pl.ds(tile * LANES, LANES)], target.at[:, tile, pl.ds(row, height), :], sems.at[kind, tile]
    )


def opacity_kernel(slices, tiles, turns, volume_hbm, index_hbm, opacity_ref, *rest):
    out_refs, (vol, idx, sems) = rest[:turns], rest[turns:]
    copies = [(fetched(volume_hbm, vol, sems, 0, t, 0), fetched(index_hbm, idx, sems, 1, t, 0)) for t in range(tiles)]
    for pair in copies:
        for copy in pair:
            copy.start()
    table = spread(opacity_ref)
    height = vol.shape[2] // turns
    plane = lax.axis_index("gz") // (lax.axis_size("gz") // turns)
    for t in range(tiles):
        for copy in copies[t]:
            copy.wait()
        for turn, out_ref in enumerate(out_refs):
            base = lax.rem(plane + turn, turns) * height

            @pl.loop(0, height // BLOCK, unroll=UNROLL)
            def _(i):
                rows = pl.ds(pl.multiple_of(base + i * BLOCK, BLOCK), BLOCK)
                transmit = None
                for k in range(slices):
                    clear = 1.0 - alpha_of(vol[k, t, rows, :], idx[k, t, rows, :], table)
                    transmit = clear if transmit is None else transmit * clear
                out_ref[i, :, pl.ds(t * LANES, LANES)] = (1.0 - transmit).astype(jnp.bfloat16)


def opacities(volume, tf_index, tf_opacity, turns):
    slices, height, width = volume.shape
    tiles = width // LANES
    tiled = (slices, tiles, height, LANES)
    return pl.pallas_call(
        functools.partial(opacity_kernel, slices, tiles, turns),
        out_shape=[jax.ShapeDtypeStruct((height // BLOCK // turns, BLOCK, width), jnp.bfloat16)] * turns,
        in_specs=[
            pl.BlockSpec(memory_space=pltpu.HBM),
            pl.BlockSpec(memory_space=pltpu.HBM),
            pl.BlockSpec(memory_space=pltpu.SMEM),
        ],
        out_specs=[pl.BlockSpec(memory_space=pltpu.VMEM)] * turns,
        scratch_shapes=[
            pltpu.VMEM(tiled, jnp.float32),
            pltpu.VMEM(tiled, jnp.int32),
            pltpu.SemaphoreType.DMA((2, tiles)),
        ],
        compiler_params=pltpu.CompilerParams(vmem_limit_bytes=LIMIT),
        cost_estimate=pl.CostEstimate(
            flops=15 * volume.size, bytes_accessed=9 * volume.size, transcendentals=volume.size
        ),
        name="opacities",
    )(volume, tf_index, tf_opacity)


def colour_kernel(
    slices, tiles, volume_hbm, index_hbm, before_hbm, after_hbm, colour_ref, opacity_ref, out_hbm,
    vol, idx, before_ref, after_ref, out_ref, sems, halo_sems, out_sems,
):
    height = before_ref.shape[0]
    halos = [
        pltpu.make_async_copy(source, target, halo_sems.at[n])
        for n, (source, target) in enumerate([(before_hbm, before_ref), (after_hbm, after_ref)])
    ]
    volumes = [fetched(volume_hbm, vol, sems, 0, t, PAD) for t in range(tiles)]
    indices = [fetched(index_hbm, idx, sems, 1, t, 0) for t in range(tiles)]
    volumes[0].start()
    indices[0].start()
    for copy in halos:
        copy.start()
    for t in range(1, tiles):
        volumes[t].start()
        indices[t].start()
    edge = jnp.zeros((slices, tiles, PAD, LANES), jnp.float32)
    vol[:, :, pl.ds(0, PAD), :] = edge
    vol[:, :, pl.ds(PAD + height, PAD), :] = edge
    lane = lax.broadcasted_iota(jnp.int32, (BLOCK, LANES), 1)
    first_lane, last_lane = lane == 0, lane == LANES - 1
    opacity_table = spread(opacity_ref)
    colour_tables = [spread(colour_ref, c) for c in range(3)]
    volumes[0].wait()
    for copy in halos:
        copy.wait()
    for t in range(tiles):
        if t + 1 < tiles:
            volumes[t + 1].wait()
        indices[t].wait()
        cols = pl.ds(t * LANES, LANES)

        @pl.loop(0, height // BLOCK, unroll=UNROLL)
        def _(i):
            start = pl.multiple_of(i * BLOCK, BLOCK)
            rows = pl.ds(start, BLOCK)
            halo = [ref[rows, cols].astype(jnp.float32) * (REACH / STEPS) for ref in (before_ref, after_ref)]
            inside = pl.ds(pl.multiple_of(start + PAD, PAD), BLOCK)
            centres = [halo[0]] + [vol[k, t, inside, :] for k in range(slices)] + [halo[1]]
            transmit, sums = None, None
            for k in range(slices):
                centre = centres[k + 1]
                depth = centres[k + 2] - centres[k]
                across = vol[k, t, pl.ds(start + (PAD + 1), BLOCK), :] - vol[k, t, pl.ds(start + (PAD - 1), BLOCK), :]
                beside_left = vol[k, t - 1, inside, :] if t > 0 else 0.0
                beside_right = vol[k, t + 1, inside, :] if t + 1 < tiles else 0.0
                left = pltpu.roll(jnp.where(last_lane, beside_left, centre), 1, 1)
                right = pltpu.roll(jnp.where(first_lane, beside_right, centre), LANES - 1, 1)
                along = right - left
                facing = jnp.abs((0.65 * 0.48) * depth + (0.65 * 0.6) * across + (0.65 * 0.64) * along)
                squares = depth * depth + across * across + along * along + 4.0
                shading = 0.35 + facing * lax.rsqrt(squares)
                index = idx[k, t, rows, :]
                alpha = alpha_of(centre, index, opacity_table)
                shown = shading * alpha
                if transmit is not None:
                    shown = transmit * shown
                terms = [lookup(table, index) * shown for table in colour_tables]
                sums = terms if sums is None else [s + add for s, add in zip(sums, terms)]
                if k + 1 < slices:
                    transmit = 1.0 - alpha if transmit is None else transmit * (1.0 - alpha)
            for c in range(3):
                out_ref[i, c, :, cols] = sums[c].astype(jnp.bfloat16)

        pltpu.make_async_copy(out_ref.at[:, :, :, cols], out_hbm.at[:, :, :, cols], out_sems.at[t]).start()
    for t in range(tiles):
        cols = pl.ds(t * LANES, LANES)
        pltpu.make_async_copy(out_ref.at[:, :, :, cols], out_hbm.at[:, :, :, cols], out_sems.at[t]).wait()


def colours(volume, tf_index, before, after, tf_color, tf_opacity):
    slices, height, width = volume.shape
    tiles = width // LANES
    shape = (height // BLOCK, 3, BLOCK, width)
    return pl.pallas_call(
        functools.partial(colour_kernel, slices, tiles),
        out_shape=jax.ShapeDtypeStruct(shape, jnp.bfloat16),
        in_specs=[pl.BlockSpec(memory_space=pltpu.HBM)] * 4 + [pl.BlockSpec(memory_space=pltpu.SMEM)] * 2,
        out_specs=pl.BlockSpec(memory_space=pltpu.HBM),
        scratch_shapes=[
            pltpu.VMEM((slices, tiles, height + 2 * PAD, LANES), jnp.float32),
            pltpu.VMEM((slices, tiles, height, LANES), jnp.int32),
            pltpu.VMEM((height, width), jnp.int16),
            pltpu.VMEM((height, width), jnp.int16),
            pltpu.VMEM(shape, jnp.bfloat16),
            pltpu.SemaphoreType.DMA((2, tiles)),
            pltpu.SemaphoreType.DMA((2,)),
            pltpu.SemaphoreType.DMA((tiles,)),
        ],
        compiler_params=pltpu.CompilerParams(vmem_limit_bytes=LIMIT),
        cost_estimate=pl.CostEstimate(
            flops=50 * volume.size, bytes_accessed=40 * volume.size, transcendentals=2 * volume.size
        ),
        name="colours",
    )(volume, tf_index, before, after, tf_color, tf_opacity)


def regroup_kernel(turns, *refs):
    here = lax.rem(lax.axis_index("gz"), turns)
    for s, ref in enumerate(refs[:turns]):
        for m, out_ref in enumerate(refs[turns:]):
            out_ref[s] = ref[here ^ m]


def regroup(parts):
    turns = len(parts)
    return pl.pallas_call(
        functools.partial(regroup_kernel, turns),
        out_shape=[jax.ShapeDtypeStruct(parts[0].shape, parts[0].dtype)] * turns,
        in_specs=[pl.BlockSpec(memory_space=pltpu.VMEM)] * turns,
        out_specs=[pl.BlockSpec(memory_space=pltpu.VMEM)] * turns,
        compiler_params=pltpu.CompilerParams(vmem_limit_bytes=BLEND_LIMIT),
        name="regroup",
    )(*parts)


def blend_kernel(ranks, turns, order_ref, colour_ref, *rest):
    opacity_refs, (out_ref, place, opacity_ref) = rest[:turns], rest[turns:]
    device = lax.axis_index("gz")
    plane, member = device // turns, lax.rem(device, turns)
    for b in range(ranks):
        place[order_ref[b]] = b
    for m, ref in enumerate(opacity_refs):
        for s in range(turns):
            brick = lax.rem(plane + turns - s, turns) * turns + (member ^ m)
            opacity_ref[brick] = ref[s]
    for j in range(colour_ref.shape[3] // LANES):
        cols = pl.ds(j * LANES, LANES)
        canvas = (jnp.zeros((colour_ref.shape[2], LANES), jnp.float32),) * 4
        for rank in range(ranks):
            b = place[rank]
            clear = 1.0 - canvas[3]
            layers = [colour_ref[b, c, :, cols] for c in range(3)] + [opacity_ref[b, :, cols]]
            canvas = tuple(front + clear * back.astype(jnp.float32) for front, back in zip(canvas, layers))
        for c in range(4):
            out_ref[c, :, cols] = canvas[c]


def blend(order, colour, opacity_parts):
    ranks, channels, height, width = colour.shape
    turns = len(opacity_parts)
    return pl.pallas_call(
        functools.partial(blend_kernel, ranks, turns),
        out_shape=jax.ShapeDtypeStruct((4, height, width), jnp.float32),
        in_specs=[pl.BlockSpec(memory_space=pltpu.SMEM)] + [pl.BlockSpec(memory_space=pltpu.VMEM)] * (1 + turns),
        out_specs=pl.BlockSpec(memory_space=pltpu.VMEM),
        scratch_shapes=[pltpu.SMEM((ranks,), jnp.int32), pltpu.VMEM((ranks, height, width), colour.dtype)],
        compiler_params=pltpu.CompilerParams(vmem_limit_bytes=BLEND_LIMIT),
        name="blend",
    )(order, colour, *opacity_parts)


def blend_plain(order, colour, opacity):
    ranks = opacity.shape[0]
    place = jnp.zeros((ranks,), jnp.int32).at[order].set(jnp.arange(ranks, dtype=jnp.int32))
    layers = jnp.concatenate([colour, opacity[:, None]], 1)

    def step(canvas, b):
        layer = lax.dynamic_index_in_dim(layers, b, 0, keepdims=False).astype(jnp.float32)
        return canvas + (1.0 - canvas[3:4]) * layer, None

    return lax.scan(step, jnp.zeros(layers.shape[1:], jnp.float32), place)[0]


def by_owner(blocks_first, devices):
    blocks, width = blocks_first.shape[0], blocks_first.shape[-1]
    middle = blocks_first.shape[1:-2]
    if blocks == devices:
        return blocks_first
    each = devices // blocks
    split = blocks_first.reshape((blocks,) + middle + (each, BLOCK // each, width))
    moved = jnp.moveaxis(split, len(middle) + 1, 1)
    return moved.reshape((devices,) + middle + (BLOCK // each, width))


def exchange(x):
    return lax.all_to_all(x, "gz", split_axis=0, concat_axis=0, tiled=True)


def coded(a_slice):
    return jnp.round(a_slice * (STEPS / REACH)).astype(jnp.int16)


def shards(volume, tf_index, tf_color, tf_opacity, order):
    devices = lax.axis_size("gz")
    slices, height, width = volume.shape
    up = [(i, i + 1) for i in range(devices - 1)]
    down = [(j, i) for i, j in up]
    last, initial = coded(volume[slices - 1]), coded(volume[0])
    before = lax.ppermute(last, "gz", up)
    after = lax.ppermute(initial, "gz", down)
    later, _ = lax.optimization_barrier((volume, (last, initial)))
    turns = PLANES if devices == PLANES * PLANES and height // devices == BLOCK else 1
    own, *others = opacities(later, tf_index, tf_opacity, turns)
    colour = by_owner(colours(volume, tf_index, before, after, tf_color, tf_opacity), devices)
    if turns == 1:
        return blend_plain(order, exchange(colour), exchange(by_owner(own, devices)))
    shifted = [
        lax.ppermute(part, "gz", [(i, (i + s * turns) % devices) for i in range(devices)])
        for s, part in enumerate(others, 1)
    ]
    shifted, colour = lax.optimization_barrier((shifted, colour))
    mine, *swapped = regroup([own] + shifted)
    swapped = [lax.ppermute(part, "gz", [(i, i ^ m) for i in range(devices)]) for m, part in enumerate(swapped, 1)]
    return blend(order, exchange(colour), [mine] + swapped)


def solution(mesh):
    placed = (P("gz", "frames", None), P("gz", "frames", None), P(), P(), P("frames"))
    return jax.shard_map(
        shards, mesh=mesh, in_specs=placed, out_specs=P("frames", "gz", None), check_vma=False
    )
```

```python
import functools

import jax
import jax.numpy as jnp
from jax import lax
from jax.experimental import pallas as pl
from jax.experimental.pallas import tpu as pltpu
from jax.sharding import PartitionSpec as P

REACH = 6.0
STEPS = 32767.0
BLOCK = 16
LANES = 128
PAD = 8
NT = 8
LIMIT = 24 * 1024 * 1024
BLEND_LIMIT = 16 * 1024 * 1024
UNROLL = 4
PLANES = 4


def spread(table_ref, *row):
    sublane = lax.broadcasted_iota(jnp.int32, (NT, LANES), 0)
    table = jnp.zeros((NT, LANES), jnp.float32)
    for m in range(NT):
        table = jnp.where(sublane == m, table_ref[(*row, m)], table)
    return table


def lookup(table, index):
    parts = [
        jnp.take_along_axis(table, index[r : r + NT], axis=0, mode="promise_in_bounds")
        for r in range(0, index.shape[0], NT)
    ]
    return jnp.concatenate(parts, 0)


def alpha_of(centre, index, table):
    return lookup(table, index) * (1.0 - jnp.exp(-centre * centre))


def opacity_kernel(slices, tiles, turns, vol, idx, opacity_ref, *out_refs):
    table = spread(opacity_ref)
    height = vol.shape[1] // turns
    plane = lax.axis_index("gz") // (lax.axis_size("gz") // turns)
    for turn, out_ref in enumerate(out_refs):
        base = lax.rem(plane + turn, turns) * height

        @pl.loop(0, height // BLOCK)
        def _(i):
            rows = pl.ds(pl.multiple_of(base + i * BLOCK, BLOCK), BLOCK)
            for t in range(tiles):
                cols = pl.ds(t * LANES, LANES)
                transmit = None
                for k in range(slices):
                    clear = 1.0 - alpha_of(vol[k, rows, cols], idx[k, rows, cols], table)
                    transmit = clear if transmit is None else transmit * clear
                out_ref[i, :, cols] = (1.0 - transmit).astype(jnp.bfloat16)


def opacities(volume, tf_index, tf_opacity, turns):
    slices, height, width = volume.shape
    return pl.pallas_call(
        functools.partial(opacity_kernel, slices, width // LANES, turns),
        out_shape=[jax.ShapeDtypeStruct((height // BLOCK // turns, BLOCK, width), jnp.bfloat16)] * turns,
        in_specs=[pl.BlockSpec(memory_space=pltpu.VMEM)] * 2 + [pl.BlockSpec(memory_space=pltpu.SMEM)],
        out_specs=[pl.BlockSpec(memory_space=pltpu.VMEM)] * turns,
        compiler_params=pltpu.CompilerParams(vmem_limit_bytes=LIMIT),
        cost_estimate=pl.CostEstimate(
            flops=15 * volume.size, bytes_accessed=9 * volume.size, transcendentals=volume.size
        ),
        name="opacities",
    )(volume, tf_index, tf_opacity)


def colour_kernel(
    slices, tiles, vol, idx, before_ref, after_ref, colour_ref, opacity_ref, out_hbm, out_ref, out_sems
):
    height = before_ref.shape[0]
    blocks = height // BLOCK
    lane = lax.broadcasted_iota(jnp.int32, (BLOCK, LANES), 1)
    first_lane, last_lane = lane == 0, lane == LANES - 1
    sublane = lax.broadcasted_iota(jnp.int32, (PAD, LANES), 0)
    first_row, last_row = sublane == 0, sublane == PAD - 1
    opacity_table = spread(opacity_ref)
    colour_tables = [spread(colour_ref, c) for c in range(3)]
    steps = blocks // UNROLL

    def shade(i):
        start = pl.multiple_of(i * BLOCK, BLOCK)
        rows = pl.ds(start, BLOCK)
        above = pl.ds(pl.multiple_of(jnp.maximum(start - PAD, 0), PAD), PAD)
        below = pl.ds(pl.multiple_of(jnp.minimum(start + BLOCK, height - PAD), PAD), PAD)
        for t in range(tiles):
            cols = pl.ds(t * LANES, LANES)
            halo = [ref[rows, cols].astype(jnp.float32) * (REACH / STEPS) for ref in (before_ref, after_ref)]
            centres = [halo[0]] + [vol[k, rows, cols] for k in range(slices)] + [halo[1]]
            transmit, sums = None, None
            for k in range(slices):
                centre = centres[k + 1]
                depth = centres[k + 2] - centres[k]
                upper = jnp.where(i > 0, vol[k, above, cols], 0.0)
                lower = jnp.where(i + 1 < blocks, vol[k, below, cols], 0.0)
                eights = [upper] + [centre[r : r + PAD] for r in range(0, BLOCK, PAD)] + [lower]
                across = jnp.concatenate(
                    [
                        pltpu.roll(jnp.where(first_row, eights[e + 1], eights[e]), PAD - 1, 0)
                        - pltpu.roll(jnp.where(last_row, eights[e - 1], eights[e]), 1, 0)
                        for e in range(1, len(eights) - 1)
                    ],
                    0,
                )
                beside_left = vol[k, rows, pl.ds((t - 1) * LANES, LANES)] if t > 0 else 0.0
                beside_right = vol[k, rows, pl.ds((t + 1) * LANES, LANES)] if t + 1 < tiles else 0.0
                left = pltpu.roll(jnp.where(last_lane, beside_left, centre), 1, 1)
                right = pltpu.roll(jnp.where(first_lane, beside_right, centre), LANES - 1, 1)
                along = right - left
                facing = jnp.abs((0.65 * 0.48) * depth + (0.65 * 0.6) * across + (0.65 * 0.64) * along)
                squares = depth * depth + across * across + along * along + 4.0
                shading = 0.35 + facing * lax.rsqrt(squares)
                index = idx[k, rows, cols]
                alpha = alpha_of(centre, index, opacity_table)
                shown = shading * alpha
                if transmit is not None:
                    shown = transmit * shown
                terms = [lookup(table, index) * shown for table in colour_tables]
                sums = terms if sums is None else [s + add for s, add in zip(sums, terms)]
                if k + 1 < slices:
                    transmit = 1.0 - alpha if transmit is None else transmit * (1.0 - alpha)
            for c in range(3):
                out_ref[i, c, :, cols] = sums[c].astype(jnp.bfloat16)

    def sent(step):
        some = pl.ds(step * UNROLL, UNROLL)
        return pltpu.make_async_copy(out_ref.at[some], out_hbm.at[some], out_sems.at[step])

    for step in range(steps):
        @pl.loop(step * UNROLL, (step + 1) * UNROLL)
        def _(i):
            shade(i)

        sent(step).start()
    for step in range(steps):
        sent(step).wait()


def colours(volume, tf_index, before, after, tf_color, tf_opacity):
    slices, height, width = volume.shape
    blocks = height // BLOCK
    shape = (blocks, 3, BLOCK, width)
    return pl.pallas_call(
        functools.partial(colour_kernel, slices, width // LANES),
        out_shape=jax.ShapeDtypeStruct(shape, jnp.bfloat16),
        in_specs=[pl.BlockSpec(memory_space=pltpu.VMEM)] * 4 + [pl.BlockSpec(memory_space=pltpu.SMEM)] * 2,
        out_specs=pl.BlockSpec(memory_space=pltpu.HBM),
        scratch_shapes=[pltpu.VMEM(shape, jnp.bfloat16), pltpu.SemaphoreType.DMA((blocks // UNROLL,))],
        compiler_params=pltpu.CompilerParams(vmem_limit_bytes=LIMIT),
        cost_estimate=pl.CostEstimate(
            flops=50 * volume.size, bytes_accessed=40 * volume.size, transcendentals=2 * volume.size
        ),
        name="colours",
    )(volume, tf_index, before, after, tf_color, tf_opacity)


def regroup_kernel(turns, *refs):
    here = lax.rem(lax.axis_index("gz"), turns)
    for s, ref in enumerate(refs[:turns]):
        for m, out_ref in enumerate(refs[turns:]):
            out_ref[s] = ref[here ^ m]


def regroup(parts):
    turns = len(parts)
    return pl.pallas_call(
        functools.partial(regroup_kernel, turns),
        out_shape=[jax.ShapeDtypeStruct(parts[0].shape, parts[0].dtype)] * turns,
        in_specs=[pl.BlockSpec(memory_space=pltpu.VMEM)] * turns,
        out_specs=[pl.BlockSpec(memory_space=pltpu.VMEM)] * turns,
        compiler_params=pltpu.CompilerParams(vmem_limit_bytes=BLEND_LIMIT),
        name="regroup",
    )(*parts)


def blend_kernel(ranks, turns, order_ref, colour_ref, *rest):
    opacity_refs, (out_ref, place, opacity_ref) = rest[:turns], rest[turns:]
    device = lax.axis_index("gz")
    plane, member = device // turns, lax.rem(device, turns)
    for b in range(ranks):
        place[order_ref[b]] = b
    for m, ref in enumerate(opacity_refs):
        for s in range(turns):
            brick = lax.rem(plane + turns - s, turns) * turns + (member ^ m)
            opacity_ref[brick] = ref[s]
    for j in range(colour_ref.shape[3] // LANES):
        cols = pl.ds(j * LANES, LANES)
        canvas = (jnp.zeros((colour_ref.shape[2], LANES), jnp.float32),) * 4
        for rank in range(ranks):
            b = place[rank]
            clear = 1.0 - canvas[3]
            layers = [colour_ref[b, c, :, cols] for c in range(3)] + [opacity_ref[b, :, cols]]
            canvas = tuple(front + clear * back.astype(jnp.float32) for front, back in zip(canvas, layers))
        for c in range(4):
            out_ref[c, :, cols] = canvas[c]


def blend(order, colour, opacity_parts):
    ranks, channels, height, width = colour.shape
    turns = len(opacity_parts)
    return pl.pallas_call(
        functools.partial(blend_kernel, ranks, turns),
        out_shape=jax.ShapeDtypeStruct((4, height, width), jnp.float32),
        in_specs=[pl.BlockSpec(memory_space=pltpu.SMEM)] + [pl.BlockSpec(memory_space=pltpu.VMEM)] * (1 + turns),
        out_specs=pl.BlockSpec(memory_space=pltpu.VMEM),
        scratch_shapes=[pltpu.SMEM((ranks,), jnp.int32), pltpu.VMEM((ranks, height, width), colour.dtype)],
        compiler_params=pltpu.CompilerParams(vmem_limit_bytes=BLEND_LIMIT),
        name="blend",
    )(order, colour, *opacity_parts)


def blend_plain(order, colour, opacity):
    ranks = opacity.shape[0]
    place = jnp.zeros((ranks,), jnp.int32).at[order].set(jnp.arange(ranks, dtype=jnp.int32))
    layers = jnp.concatenate([colour, opacity[:, None]], 1)

    def step(canvas, b):
        layer = lax.dynamic_index_in_dim(layers, b, 0, keepdims=False).astype(jnp.float32)
        return canvas + (1.0 - canvas[3:4]) * layer, None

    return lax.scan(step, jnp.zeros(layers.shape[1:], jnp.float32), place)[0]


def by_owner(blocks_first, devices):
    blocks, width = blocks_first.shape[0], blocks_first.shape[-1]
    middle = blocks_first.shape[1:-2]
    if blocks == devices:
        return blocks_first
    each = devices // blocks
    split = blocks_first.reshape((blocks,) + middle + (each, BLOCK // each, width))
    moved = jnp.moveaxis(split, len(middle) + 1, 1)
    return moved.reshape((devices,) + middle + (BLOCK // each, width))


def exchange(x):
    return lax.all_to_all(x, "gz", split_axis=0, concat_axis=0, tiled=True)


def coded(a_slice):
    return jnp.round(a_slice * (STEPS / REACH)).astype(jnp.int16)


def shards(volume, tf_index, tf_color, tf_opacity, order):
    devices = lax.axis_size("gz")
    slices, height, width = volume.shape
    up = [(i, i + 1) for i in range(devices - 1)]
    down = [(j, i) for i, j in up]
    last, initial = coded(volume[slices - 1]), coded(volume[0])
    before = lax.ppermute(last, "gz", up)
    after = lax.ppermute(initial, "gz", down)
    turns = PLANES if devices == PLANES * PLANES and height // devices == BLOCK else 1
    own, *others = opacities(volume, tf_index, tf_opacity, turns)
    colour = by_owner(colours(volume, tf_index, before, after, tf_color, tf_opacity), devices)
    if turns == 1:
        return blend_plain(order, exchange(colour), exchange(by_owner(own, devices)))
    shifted = [
        lax.ppermute(part, "gz", [(i, (i + s * turns) % devices) for i in range(devices)])
        for s, part in enumerate(others, 1)
    ]
    shifted, colour = lax.optimization_barrier((shifted, colour))
    mine, *swapped = regroup([own] + shifted)
    swapped = [lax.ppermute(part, "gz", [(i, i ^ m) for i in range(devices)]) for m, part in enumerate(swapped, 1)]
    return blend(order, exchange(colour), [mine] + swapped)


def solution(mesh):
    placed = (P("gz", "frames", None), P("gz", "frames", None), P(), P(), P("frames"))
    return jax.shard_map(
        shards, mesh=mesh, in_specs=placed, out_specs=P("frames", "gz", None), check_vma=False
    )
```

```python
import functools

import jax
import jax.numpy as jnp
from jax import lax
from jax.experimental import pallas as pl
from jax.experimental.pallas import tpu as pltpu
from jax.sharding import PartitionSpec as P

REACH = 6.0
STEPS = 32767.0
BLOCK = 16
LANES = 128
PAD = 8
NT = 8
LIMIT = 24 * 1024 * 1024
FETCH_LIMIT = 43 * 1024 * 1024
BLEND_LIMIT = 16 * 1024 * 1024
UNROLL = 4
PLANES = 4


def spread(table_ref, *row):
    sublane = lax.broadcasted_iota(jnp.int32, (NT, LANES), 0)
    table = jnp.zeros((NT, LANES), jnp.float32)
    for m in range(NT):
        table = jnp.where(sublane == m, table_ref[(*row, m)], table)
    return table


def lookup(table, index):
    parts = [
        jnp.take_along_axis(table, index[r : r + NT], axis=0, mode="promise_in_bounds")
        for r in range(0, index.shape[0], NT)
    ]
    return jnp.concatenate(parts, 0)


def alpha_of(centre, index, table):
    return lookup(table, index) * (1.0 - jnp.exp(-centre * centre))


def opacity_kernel(slices, tiles, turns, volume_hbm, index_hbm, opacity_ref, *rest):
    out_refs, (vol, idx, sems) = rest[:turns], rest[turns:]
    height = vol.shape[1] // turns
    plane = lax.axis_index("gz") // (lax.axis_size("gz") // turns)
    bases = [pl.multiple_of(lax.rem(plane + turn, turns) * height, height) for turn in range(turns)]
    copies = []
    for turn, base in enumerate(bases):
        some = pl.ds(base, height)
        pair = [
            pltpu.make_async_copy(source.at[:, some, :], target.at[:, some, :], sems.at[kind, turn])
            for kind, (source, target) in enumerate([(volume_hbm, vol), (index_hbm, idx)])
        ]
        for copy in pair:
            copy.start()
        copies.append(pair)
    table = spread(opacity_ref)
    for base, pair, out_ref in zip(bases, copies, out_refs):
        for copy in pair:
            copy.wait()

        @pl.loop(0, height // BLOCK)
        def _(i):
            rows = pl.ds(pl.multiple_of(base + i * BLOCK, BLOCK), BLOCK)
            for t in range(tiles):
                cols = pl.ds(t * LANES, LANES)
                transmit = None
                for k in range(slices):
                    clear = 1.0 - alpha_of(vol[k, rows, cols], idx[k, rows, cols], table)
                    transmit = clear if transmit is None else transmit * clear
                out_ref[i, :, cols] = (1.0 - transmit).astype(jnp.bfloat16)


def opacities(volume, tf_index, tf_opacity, turns):
    slices, height, width = volume.shape
    part = jax.ShapeDtypeStruct((height // BLOCK // turns, BLOCK, width), jnp.bfloat16)
    held = [jax.ShapeDtypeStruct(x.shape, x.dtype) for x in (volume, tf_index)]
    return pl.pallas_call(
        functools.partial(opacity_kernel, slices, width // LANES, turns),
        out_shape=[part] * turns + held,
        in_specs=[pl.BlockSpec(memory_space=pltpu.HBM)] * 2 + [pl.BlockSpec(memory_space=pltpu.SMEM)],
        out_specs=[pl.BlockSpec(memory_space=pltpu.VMEM)] * (turns + 2),
        scratch_shapes=[pltpu.SemaphoreType.DMA((2, turns))],
        compiler_params=pltpu.CompilerParams(vmem_limit_bytes=FETCH_LIMIT),
        cost_estimate=pl.CostEstimate(
            flops=15 * volume.size, bytes_accessed=9 * volume.size, transcendentals=volume.size
        ),
        name="opacities",
    )(volume, tf_index, tf_opacity)


def colour_kernel(slices, span, vol, idx, before_ref, after_ref, colour_ref, opacity_ref, *out_refs):
    height, width = before_ref.shape
    blocks, tiles = height // BLOCK, width // LANES
    turns = len(out_refs)
    each = blocks // turns
    plane = lax.axis_index("gz") // (lax.axis_size("gz") // turns)
    lane = lax.broadcasted_iota(jnp.int32, (BLOCK, LANES), 1)
    first_lane, last_lane = lane == 0, lane == LANES - 1
    sublane = lax.broadcasted_iota(jnp.int32, (PAD, LANES), 0)
    first_row, last_row = sublane == 0, sublane == PAD - 1
    opacity_table = spread(opacity_ref)
    colour_tables = [spread(colour_ref, c) for c in range(3)]

    def shade(i, out_ref, j):
        start = pl.multiple_of(i * BLOCK, BLOCK)
        rows = pl.ds(start, BLOCK)
        above = pl.ds(pl.multiple_of(jnp.maximum(start - PAD, 0), PAD), PAD)
        below = pl.ds(pl.multiple_of(jnp.minimum(start + BLOCK, height - PAD), PAD), PAD)
        for t in range(*span):
            cols = pl.ds(t * LANES, LANES)
            halo = [ref[rows, cols].astype(jnp.float32) * (REACH / STEPS) for ref in (before_ref, after_ref)]
            centres = [halo[0]] + [vol[k, rows, cols] for k in range(slices)] + [halo[1]]
            transmit, sums = None, None
            for k in range(slices):
                centre = centres[k + 1]
                depth = centres[k + 2] - centres[k]
                upper = jnp.where(i > 0, vol[k, above, cols], 0.0)
                lower = jnp.where(i + 1 < blocks, vol[k, below, cols], 0.0)
                eights = [upper] + [centre[r : r + PAD] for r in range(0, BLOCK, PAD)] + [lower]
                across = jnp.concatenate(
                    [
                        pltpu.roll(jnp.where(first_row, eights[e + 1], eights[e]), PAD - 1, 0)
                        - pltpu.roll(jnp.where(last_row, eights[e - 1], eights[e]), 1, 0)
                        for e in range(1, len(eights) - 1)
                    ],
                    0,
                )
                beside_left = vol[k, rows, pl.ds((t - 1) * LANES, LANES)] if t > 0 else 0.0
                beside_right = vol[k, rows, pl.ds((t + 1) * LANES, LANES)] if t + 1 < tiles else 0.0
                left = pltpu.roll(jnp.where(last_lane, beside_left, centre), 1, 1)
                right = pltpu.roll(jnp.where(first_lane, beside_right, centre), LANES - 1, 1)
                along = right - left
                facing = jnp.abs((0.65 * 0.48) * depth + (0.65 * 0.6) * across + (0.65 * 0.64) * along)
                squares = depth * depth + across * across + along * along + 4.0
                shading = 0.35 + facing * lax.rsqrt(squares)
                index = idx[k, rows, cols]
                alpha = alpha_of(centre, index, opacity_table)
                shown = shading * alpha
                if transmit is not None:
                    shown = transmit * shown
                terms = [lookup(table, index) * shown for table in colour_tables]
                sums = terms if sums is None else [s + add for s, add in zip(sums, terms)]
                if k + 1 < slices:
                    transmit = 1.0 - alpha if transmit is None else transmit * (1.0 - alpha)
            for c in range(3):
                out_ref[j, c, :, pl.ds((t - span[0]) * LANES, LANES)] = sums[c].astype(jnp.bfloat16)

    for turn, out_ref in enumerate(out_refs):
        base = lax.rem(plane + turn, turns) * each

        @pl.loop(0, each)
        def _(j):
            shade(base + j, out_ref, j)


def colours(volume, tf_index, before, after, tf_color, tf_opacity, span, turns):
    slices, height, _ = volume.shape
    part = jax.ShapeDtypeStruct((height // BLOCK // turns, 3, BLOCK, (span[1] - span[0]) * LANES), jnp.bfloat16)
    cells = slices * height * (span[1] - span[0]) * LANES
    return pl.pallas_call(
        functools.partial(colour_kernel, slices, span),
        out_shape=[part] * turns,
        in_specs=[pl.BlockSpec(memory_space=pltpu.VMEM)] * 4 + [pl.BlockSpec(memory_space=pltpu.SMEM)] * 2,
        out_specs=[pl.BlockSpec(memory_space=pltpu.VMEM)] * turns,
        compiler_params=pltpu.CompilerParams(vmem_limit_bytes=LIMIT),
        cost_estimate=pl.CostEstimate(flops=50 * cells, bytes_accessed=40 * cells, transcendentals=2 * cells),
        name="colours",
    )(volume, tf_index, before, after, tf_color, tf_opacity)


def regroup_kernel(turns, *refs):
    here = lax.rem(lax.axis_index("gz"), turns)
    for s, ref in enumerate(refs[:turns]):
        for m, out_ref in enumerate(refs[turns:]):
            out_ref[s] = ref[here ^ m]


def regroup(parts):
    turns = len(parts)
    return pl.pallas_call(
        functools.partial(regroup_kernel, turns),
        out_shape=[jax.ShapeDtypeStruct(parts[0].shape, parts[0].dtype)] * turns,
        in_specs=[pl.BlockSpec(memory_space=pltpu.VMEM)] * turns,
        out_specs=[pl.BlockSpec(memory_space=pltpu.VMEM)] * turns,
        compiler_params=pltpu.CompilerParams(vmem_limit_bytes=BLEND_LIMIT),
        name="regroup",
    )(*parts)


def blend_kernel(ranks, turns, colour_count, start, order_ref, *rest):
    opacity_refs, rest = rest[:turns], rest[turns:]
    colour_refs, (out_hbm, place, opacity_ref, out_ref, sem) = rest[:colour_count], rest[-5:]
    device = lax.axis_index("gz")
    plane, member = device // turns, lax.rem(device, turns)
    width = out_ref.shape[2]
    for b in range(ranks):
        place[order_ref[b]] = b
    for m, ref in enumerate(opacity_refs):
        for s in range(turns):
            brick = lax.rem(plane + turns - s, turns) * turns + (member ^ m)
            opacity_ref[brick, 3] = ref[s, :, pl.ds(start, width)]
            if len(colour_refs) > 1:
                for c in range(3):
                    opacity_ref[brick, c] = colour_refs[m][s, c]
    colour_ref = opacity_ref if len(colour_refs) > 1 else colour_refs[0]
    for j in range(width // LANES):
        cols = pl.ds(j * LANES, LANES)
        canvas = (jnp.zeros((out_ref.shape[1], LANES), jnp.float32),) * 4
        for rank in range(ranks):
            b = place[rank]
            clear = 1.0 - canvas[3]
            layers = [colour_ref[b, c, :, cols] for c in range(3)] + [opacity_ref[b, 3, :, cols]]
            canvas = tuple(front + clear * back.astype(jnp.float32) for front, back in zip(canvas, layers))
        for c in range(4):
            out_ref[c, :, cols] = canvas[c]
    copy = pltpu.make_async_copy(out_ref, out_hbm.at[:, :, pl.ds(start, width)], sem)
    copy.start()
    copy.wait()


def blend(order, opacity_parts, colours_here, start, total, image=()):
    turns, ranks = len(opacity_parts), order.shape[0]
    height, width = colours_here[0].shape[-2:]
    operands = [order, *opacity_parts, *colours_here]
    return pl.pallas_call(
        functools.partial(blend_kernel, ranks, turns, len(colours_here), start),
        out_shape=jax.ShapeDtypeStruct((4, height, total), jnp.float32),
        in_specs=[pl.BlockSpec(memory_space=pltpu.SMEM)]
        + [pl.BlockSpec(memory_space=pltpu.VMEM)] * (len(operands) - 1)
        + [pl.BlockSpec(memory_space=pltpu.HBM)] * len(image),
        out_specs=pl.BlockSpec(memory_space=pltpu.HBM),
        scratch_shapes=[
            pltpu.SMEM((ranks,), jnp.int32),
            pltpu.VMEM((ranks, 4, height, width), jnp.bfloat16),
            pltpu.VMEM((4, height, width), jnp.float32),
            pltpu.SemaphoreType.DMA,
        ],
        input_output_aliases={len(operands): 0} if image else {},
        compiler_params=pltpu.CompilerParams(vmem_limit_bytes=BLEND_LIMIT),
        name="blend",
    )(*operands, *image)


def blend_plain(order, colour, opacity):
    ranks = opacity.shape[0]
    place = jnp.zeros((ranks,), jnp.int32).at[order].set(jnp.arange(ranks, dtype=jnp.int32))
    layers = jnp.concatenate([colour, opacity[:, None]], 1)

    def step(canvas, b):
        layer = lax.dynamic_index_in_dim(layers, b, 0, keepdims=False).astype(jnp.float32)
        return canvas + (1.0 - canvas[3:4]) * layer, None

    return lax.scan(step, jnp.zeros(layers.shape[1:], jnp.float32), place)[0]


def by_owner(blocks_first, devices):
    blocks, width = blocks_first.shape[0], blocks_first.shape[-1]
    middle = blocks_first.shape[1:-2]
    if blocks == devices:
        return blocks_first
    each = devices // blocks
    split = blocks_first.reshape((blocks,) + middle + (each, BLOCK // each, width))
    moved = jnp.moveaxis(split, len(middle) + 1, 1)
    return moved.reshape((devices,) + middle + (BLOCK // each, width))


def exchange(x):
    return lax.all_to_all(x, "gz", split_axis=0, concat_axis=0, tiled=True)


def coded(a_slice):
    return jnp.round(a_slice * (STEPS / REACH)).astype(jnp.int16)


def across_planes(parts, turns, devices):
    return [parts[0]] + [
        lax.ppermute(part, "gz", [(i, (i + s * turns) % devices) for i in range(devices)])
        for s, part in enumerate(parts[1:], 1)
    ]


def in_plane(parts, devices):
    return [parts[0]] + [
        lax.ppermute(part, "gz", [(i, i ^ m) for i in range(devices)]) for m, part in enumerate(parts[1:], 1)
    ]


def shards(volume, tf_index, tf_color, tf_opacity, order):
    devices = lax.axis_size("gz")
    slices, height, width = volume.shape
    up = [(i, i + 1) for i in range(devices - 1)]
    down = [(j, i) for i, j in up]
    last, initial = coded(volume[slices - 1]), coded(volume[0])
    before = lax.ppermute(last, "gz", up)
    after = lax.ppermute(initial, "gz", down)
    turns = PLANES if devices == PLANES * PLANES and height // devices == BLOCK else 1
    *opacity, volume, tf_index = opacities(volume, tf_index, tf_opacity, turns)
    tiles = width // LANES
    held = (volume, tf_index, before, after, tf_color, tf_opacity)
    if turns == 1:
        colour = by_owner(colours(*held, (0, tiles), 1)[0], devices)
        return blend_plain(order, exchange(colour), exchange(by_owner(opacity[0], devices)))
    opacity = across_planes(opacity, turns, devices)
    first = colours(*held, (0, tiles // 2), turns)
    first, held = lax.optimization_barrier((first, held))
    first = across_planes(first, turns, devices)
    (second,) = colours(*held, (tiles // 2, tiles), 1)
    opacity, second = lax.optimization_barrier((opacity, second))
    second = exchange(second)
    opacity = in_plane(regroup(opacity), devices)
    first = in_plane(regroup(first), devices)
    image = blend(order, opacity, first, 0, width)
    return blend(order, opacity, [second], width // 2, width, (image,))


def solution(mesh):
    placed = (P("gz", "frames", None), P("gz", "frames", None), P(), P(), P("frames"))
    return jax.shard_map(
        shards, mesh=mesh, in_specs=placed, out_specs=P("frames", "gz", None), check_vma=False
    )
```

```python
import functools

import jax
import jax.numpy as jnp
from jax import lax
from jax.experimental import pallas as pl
from jax.experimental.pallas import tpu as pltpu
from jax.sharding import PartitionSpec as P

REACH = 6.0
STEPS = 32767.0
BLOCK = 16
LANES = 128
PAD = 8
NT = 8
LIMIT = 24 * 1024 * 1024
FETCH_LIMIT = 43 * 1024 * 1024
BLEND_LIMIT = 16 * 1024 * 1024
FIRST = 4
PLANES = 4


def spread(table_ref, *row):
    sublane = lax.broadcasted_iota(jnp.int32, (NT, LANES), 0)
    table = jnp.zeros((NT, LANES), jnp.float32)
    for m in range(NT):
        table = jnp.where(sublane == m, table_ref[(*row, m)], table)
    return table


def lookup(table, index):
    parts = [
        jnp.take_along_axis(table, index[r : r + NT], axis=0, mode="promise_in_bounds")
        for r in range(0, index.shape[0], NT)
    ]
    return jnp.concatenate(parts, 0)


def alpha_of(centre, index, table):
    return lookup(table, index) * (1.0 - jnp.exp(-centre * centre))


def opacity_kernel(slices, tiles, turns, volume_hbm, index_hbm, opacity_ref, *rest):
    out_refs, (vol, idx, sems) = rest[:turns], rest[turns:]
    height = vol.shape[1] // turns
    plane = lax.axis_index("gz") // (lax.axis_size("gz") // turns)
    bases = [pl.multiple_of(lax.rem(plane + turn, turns) * height, height) for turn in range(turns)]
    copies = []
    for turn, base in enumerate(bases):
        some = pl.ds(base, height)
        pair = [
            pltpu.make_async_copy(source.at[:, some, :], target.at[:, some, :], sems.at[kind, turn])
            for kind, (source, target) in enumerate([(volume_hbm, vol), (index_hbm, idx)])
        ]
        for copy in pair:
            copy.start()
        copies.append(pair)
    table = spread(opacity_ref)
    for base, pair, out_ref in zip(bases, copies, out_refs):
        for copy in pair:
            copy.wait()

        @pl.loop(0, height // BLOCK)
        def _(i):
            rows = pl.ds(pl.multiple_of(base + i * BLOCK, BLOCK), BLOCK)
            for t in range(tiles):
                cols = pl.ds(t * LANES, LANES)
                transmit = None
                for k in range(slices):
                    clear = 1.0 - alpha_of(vol[k, rows, cols], idx[k, rows, cols], table)
                    transmit = clear if transmit is None else transmit * clear
                out_ref[i, :, cols] = (1.0 - transmit).astype(jnp.bfloat16)


def opacities(volume, tf_index, tf_opacity, turns):
    slices, height, width = volume.shape
    part = jax.ShapeDtypeStruct((height // BLOCK // turns, BLOCK, width), jnp.bfloat16)
    held = [jax.ShapeDtypeStruct(x.shape, x.dtype) for x in (volume, tf_index)]
    return pl.pallas_call(
        functools.partial(opacity_kernel, slices, width // LANES, turns),
        out_shape=[part] * turns + held,
        in_specs=[pl.BlockSpec(memory_space=pltpu.HBM)] * 2 + [pl.BlockSpec(memory_space=pltpu.SMEM)],
        out_specs=[pl.BlockSpec(memory_space=pltpu.VMEM)] * (turns + 2),
        scratch_shapes=[pltpu.SemaphoreType.DMA((2, turns))],
        compiler_params=pltpu.CompilerParams(vmem_limit_bytes=FETCH_LIMIT),
        cost_estimate=pl.CostEstimate(
            flops=15 * volume.size, bytes_accessed=9 * volume.size, transcendentals=volume.size
        ),
        name="opacities",
    )(volume, tf_index, tf_opacity)


def colour_kernel(slices, span, turns, by_member, vol, idx, before_ref, after_ref, colour_ref, opacity_ref, *rest):
    out_refs = rest[-turns:]
    height, width = before_ref.shape
    blocks, tiles = height // BLOCK, width // LANES
    each = blocks // turns
    device, members = lax.axis_index("gz"), lax.axis_size("gz") // turns
    plane, member = device // members, lax.rem(device, members)
    lane = lax.broadcasted_iota(jnp.int32, (BLOCK, LANES), 1)
    first_lane, last_lane = lane == 0, lane == LANES - 1
    sublane = lax.broadcasted_iota(jnp.int32, (PAD, LANES), 0)
    first_row, last_row = sublane == 0, sublane == PAD - 1
    opacity_table = spread(opacity_ref)
    colour_tables = [spread(colour_ref, c) for c in range(3)]

    def shade(i, out_ref, j):
        start = pl.multiple_of(i * BLOCK, BLOCK)
        rows = pl.ds(start, BLOCK)
        above = pl.ds(pl.multiple_of(jnp.maximum(start - PAD, 0), PAD), PAD)
        below = pl.ds(pl.multiple_of(jnp.minimum(start + BLOCK, height - PAD), PAD), PAD)
        for t in range(*span):
            cols = pl.ds(t * LANES, LANES)
            halo = [ref[rows, cols].astype(jnp.float32) * (REACH / STEPS) for ref in (before_ref, after_ref)]
            centres = [halo[0]] + [vol[k, rows, cols] for k in range(slices)] + [halo[1]]
            transmit, sums = None, None
            for k in range(slices):
                centre = centres[k + 1]
                depth = centres[k + 2] - centres[k]
                upper = jnp.where(i > 0, vol[k, above, cols], 0.0)
                lower = jnp.where(i + 1 < blocks, vol[k, below, cols], 0.0)
                eights = [upper] + [centre[r : r + PAD] for r in range(0, BLOCK, PAD)] + [lower]
                across = jnp.concatenate(
                    [
                        pltpu.roll(jnp.where(first_row, eights[e + 1], eights[e]), PAD - 1, 0)
                        - pltpu.roll(jnp.where(last_row, eights[e - 1], eights[e]), 1, 0)
                        for e in range(1, len(eights) - 1)
                    ],
                    0,
                )
                beside_left = vol[k, rows, pl.ds((t - 1) * LANES, LANES)] if t > 0 else 0.0
                beside_right = vol[k, rows, pl.ds((t + 1) * LANES, LANES)] if t + 1 < tiles else 0.0
                left = pltpu.roll(jnp.where(last_lane, beside_left, centre), 1, 1)
                right = pltpu.roll(jnp.where(first_lane, beside_right, centre), LANES - 1, 1)
                along = right - left
                facing = jnp.abs((0.65 * 0.48) * depth + (0.65 * 0.6) * across + (0.65 * 0.64) * along)
                squares = depth * depth + across * across + along * along + 4.0
                shading = 0.35 + facing * lax.rsqrt(squares)
                index = idx[k, rows, cols]
                alpha = alpha_of(centre, index, opacity_table)
                shown = shading * alpha
                if transmit is not None:
                    shown = transmit * shown
                terms = [lookup(table, index) * shown for table in colour_tables]
                sums = terms if sums is None else [s + add for s, add in zip(sums, terms)]
                if k + 1 < slices:
                    transmit = 1.0 - alpha if transmit is None else transmit * (1.0 - alpha)
            for c in range(3):
                out_ref[j, c, :, pl.ds((t - span[0]) * LANES, LANES)] = sums[c].astype(jnp.bfloat16)

    if not by_member:
        for turn, out_ref in enumerate(out_refs):
            base = lax.rem(plane + turn, turns) * each

            @pl.loop(0, each)
            def _(j):
                shade(base + j, out_ref, j)

        return
    for m, out_ref in enumerate(out_refs):
        @pl.loop(0, turns)
        def _(j):
            shade(lax.rem(plane + j, turns) * members + (member ^ m), out_ref, j)


def colours(volume, tf_index, before, after, tf_color, tf_opacity, span, turns, earlier=()):
    slices, height, _ = volume.shape
    part = jax.ShapeDtypeStruct((height // BLOCK // turns, 3, BLOCK, (span[1] - span[0]) * LANES), jnp.bfloat16)
    cells = slices * height * (span[1] - span[0]) * LANES
    return pl.pallas_call(
        functools.partial(colour_kernel, slices, span, turns, bool(earlier)),
        out_shape=[part] * turns,
        in_specs=[pl.BlockSpec(memory_space=pltpu.VMEM)] * 4
        + [pl.BlockSpec(memory_space=pltpu.SMEM)] * 2
        + [pl.BlockSpec(memory_space=pl.ANY)] * len(earlier),
        out_specs=[pl.BlockSpec(memory_space=pltpu.VMEM)] * turns,
        compiler_params=pltpu.CompilerParams(vmem_limit_bytes=LIMIT),
        cost_estimate=pl.CostEstimate(flops=50 * cells, bytes_accessed=40 * cells, transcendentals=2 * cells),
        name="colours",
    )(volume, tf_index, before, after, tf_color, tf_opacity, *earlier)


def on_chip(kernel, out_shapes, operands, earlier=()):
    return pl.pallas_call(
        kernel,
        out_shape=out_shapes,
        in_specs=[pl.BlockSpec(memory_space=pltpu.VMEM)] * len(operands)
        + [pl.BlockSpec(memory_space=pl.ANY)] * len(earlier),
        out_specs=[pl.BlockSpec(memory_space=pltpu.VMEM)] * len(out_shapes),
        compiler_params=pltpu.CompilerParams(vmem_limit_bytes=BLEND_LIMIT),
        name=kernel.func.__name__.removesuffix("_kernel"),
    )(*operands, *earlier)


def hold_kernel(count, *refs):
    for ref, out_ref in zip(refs[:count], refs[-count:]):
        out_ref[...] = ref[...]


def hold(parts, earlier):
    shapes = [jax.ShapeDtypeStruct(part.shape, part.dtype) for part in parts]
    return list(on_chip(functools.partial(hold_kernel, len(parts)), shapes, parts, earlier))


def to_core_kernel(turns, *refs):
    here = lax.rem(lax.axis_index("gz"), turns)
    colour_refs, opacity_refs, second_refs = refs[:turns], refs[turns : 2 * turns], refs[2 * turns :][:2]
    own_ref, far_ref, passed_ref = refs[-3:]
    width, total = colour_refs[0].shape[-1], opacity_refs[0].shape[-1]
    for s, (colour_ref, opacity_ref) in enumerate(zip(colour_refs, opacity_refs)):
        for m, (out_ref, at) in enumerate([(own_ref, s), (passed_ref, s), (far_ref, s), (passed_ref, turns + s)]):
            for c in range(3):
                out_ref[at, :, pl.ds(c * width, width)] = colour_ref[here ^ m, c]
            out_ref[at, :, pl.ds(3 * width, total)] = opacity_ref[here ^ m]
    width, start = second_refs[0].shape[-1], 3 * width + total
    for x, ref in enumerate(second_refs):
        for s in range(turns):
            for c in range(3):
                passed_ref[x * turns + s, :, pl.ds(start + c * width, width)] = ref[s, c]


def to_core(first, opacity, second, earlier):
    turns, (_, _, height, width) = len(first), first[0].shape
    wide = 3 * width + opacity[0].shape[-1]
    part = jax.ShapeDtypeStruct((turns, height, wide), jnp.bfloat16)
    passed = jax.ShapeDtypeStruct((2 * turns, height, wide + 3 * second[0].shape[-1]), jnp.bfloat16)
    operands = [*first, *opacity, *second]
    return on_chip(functools.partial(to_core_kernel, turns), [part, part, passed], operands, earlier)


def to_rest_kernel(turns, far_ref, passed_ref, own_ref, other_ref, out_ref, *plane_refs):
    wide, width = far_ref.shape[2], own_ref.shape[-1]
    out_ref[pl.ds(0, turns)] = far_ref[...]
    out_ref[pl.ds(turns, turns)] = passed_ref[pl.ds(turns, turns), :, pl.ds(0, wide)]
    for s, plane_ref in enumerate(plane_refs):
        plane_ref[0] = own_ref[s]
        plane_ref[2] = other_ref[s]
        for c in range(3):
            cols = pl.ds(wide + c * width, width)
            plane_ref[1, c] = passed_ref[s, :, cols]
            plane_ref[3, c] = passed_ref[turns + s, :, cols]


def to_rest(far, passed, own, other):
    turns = far.shape[0]
    shapes = [jax.ShapeDtypeStruct((2 * turns,) + far.shape[1:], far.dtype)]
    shapes += [jax.ShapeDtypeStruct(own.shape, own.dtype)] * turns
    return on_chip(functools.partial(to_rest_kernel, turns), shapes, [far, passed, own, other])


def swap(part, devices, stride):
    return lax.ppermute(part, "gz", [(i, i ^ stride) for i in range(devices)])


def blend_kernel(ranks, turns, side, order_ref, *rest):
    (own_ref, passed_ref, far_ref), second_refs = rest[:3], rest[3:-6]
    out_hbm, place, colour_ref, opacity_ref, out_ref, sem = rest[-6:]
    device = lax.axis_index("gz")
    plane, member = device // turns, lax.rem(device, turns)
    width, total = out_ref.shape[2], out_hbm.shape[2]
    start = total - width if side else 0
    before = own_ref.shape[2] - total
    for b in range(ranks):
        place[order_ref[b]] = b
    for m in range(turns):
        for s in range(turns):
            brick = lax.rem(plane + turns - s, turns) * turns + (member ^ m)
            ref, at = [(own_ref, s), (passed_ref, s), (far_ref, s), (far_ref, turns + s)][m]
            for c in range(3):
                colour_ref[brick, c] = second_refs[s][m, c] if side else ref[at, :, pl.ds(c * width, width)]
            opacity_ref[brick] = ref[at, :, pl.ds(before + start, width)]
    for j in range(width // LANES):
        cols = pl.ds(j * LANES, LANES)
        canvas = (jnp.zeros((out_ref.shape[1], LANES), jnp.float32),) * 4
        for rank in range(ranks):
            b = place[rank]
            clear = 1.0 - canvas[3]
            layers = [colour_ref[b, c, :, cols] for c in range(3)] + [opacity_ref[b, :, cols]]
            canvas = tuple(front + clear * back.astype(jnp.float32) for front, back in zip(canvas, layers))
        for c in range(4):
            out_ref[c, :, cols] = canvas[c]
    copy = pltpu.make_async_copy(out_ref, out_hbm.at[:, :, pl.ds(start, width)], sem)
    copy.start()
    copy.wait()


def blend(order, turns, total, first, second=(), image=()):
    ranks, height = order.shape[0], first[0].shape[1]
    width = second[0].shape[-1] if second else (first[0].shape[2] - total) // 3
    operands = [order, *first, *second]
    return pl.pallas_call(
        functools.partial(blend_kernel, ranks, turns, 1 if second else 0),
        out_shape=jax.ShapeDtypeStruct((4, height, total), jnp.float32),
        in_specs=[pl.BlockSpec(memory_space=pltpu.SMEM)]
        + [pl.BlockSpec(memory_space=pltpu.VMEM)] * (len(operands) - 1)
        + [pl.BlockSpec(memory_space=pltpu.HBM)] * len(image),
        out_specs=pl.BlockSpec(memory_space=pltpu.HBM),
        scratch_shapes=[
            pltpu.SMEM((ranks,), jnp.int32),
            pltpu.VMEM((ranks, 3, height, width), jnp.bfloat16),
            pltpu.VMEM((ranks, height, width), jnp.bfloat16),
            pltpu.VMEM((4, height, width), jnp.float32),
            pltpu.SemaphoreType.DMA,
        ],
        input_output_aliases={len(operands): 0} if image else {},
        compiler_params=pltpu.CompilerParams(vmem_limit_bytes=BLEND_LIMIT),
        name="blend",
    )(*operands, *image)


def blend_plain(order, colour, opacity):
    ranks = opacity.shape[0]
    place = jnp.zeros((ranks,), jnp.int32).at[order].set(jnp.arange(ranks, dtype=jnp.int32))
    layers = jnp.concatenate([colour, opacity[:, None]], 1)

    def step(canvas, b):
        layer = lax.dynamic_index_in_dim(layers, b, 0, keepdims=False).astype(jnp.float32)
        return canvas + (1.0 - canvas[3:4]) * layer, None

    return lax.scan(step, jnp.zeros(layers.shape[1:], jnp.float32), place)[0]


def by_owner(blocks_first, devices):
    blocks, width = blocks_first.shape[0], blocks_first.shape[-1]
    middle = blocks_first.shape[1:-2]
    if blocks == devices:
        return blocks_first
    each = devices // blocks
    split = blocks_first.reshape((blocks,) + middle + (each, BLOCK // each, width))
    moved = jnp.moveaxis(split, len(middle) + 1, 1)
    return moved.reshape((devices,) + middle + (BLOCK // each, width))


def exchange(x):
    return lax.all_to_all(x, "gz", split_axis=0, concat_axis=0, tiled=True)


def coded(a_slice):
    return jnp.round(a_slice * (STEPS / REACH)).astype(jnp.int16)


def across_planes(parts, turns, devices):
    return [parts[0]] + [
        lax.ppermute(part, "gz", [(i, (i + s * turns) % devices) for i in range(devices)])
        for s, part in enumerate(parts[1:], 1)
    ]


def shards(volume, tf_index, tf_color, tf_opacity, order):
    devices = lax.axis_size("gz")
    slices, height, width = volume.shape
    up = [(i, i + 1) for i in range(devices - 1)]
    down = [(j, i) for i, j in up]
    last, initial = coded(volume[slices - 1]), coded(volume[0])
    before = lax.ppermute(last, "gz", up)
    after = lax.ppermute(initial, "gz", down)
    turns = PLANES if devices == PLANES * PLANES and height // devices == BLOCK else 1
    *opacity, volume, tf_index = opacities(volume, tf_index, tf_opacity, turns)
    tiles = width // LANES
    held = (volume, tf_index, before, after, tf_color, tf_opacity)
    if turns == 1:
        colour = by_owner(colours(*held, (0, tiles), 1)[0], devices)
        return blend_plain(order, exchange(colour), exchange(by_owner(opacity[0], devices)))
    split = tiles * FIRST // 8
    opacity = across_planes(opacity, turns, devices)
    own, *others = colours(*held, (0, split), turns)
    second = colours(*held, (split, tiles), turns, (own,))
    first = across_planes([own] + hold(others, opacity[1:]), turns, devices)
    near, core, *far = second
    far = [swap(part, devices, 2) for part in far]
    own, other, passed = to_core(first, opacity, [core, far[1]], far[:1])
    passed = swap(passed, devices, 1)
    other, *second = to_rest(other, passed, near, far[0])
    second = across_planes(second, turns, devices)
    first = [own, passed, swap(other, devices, 2)]
    return blend(order, turns, width, first, second, (blend(order, turns, width, first),))


def solution(mesh):
    placed = (P("gz", "frames", None), P("gz", "frames", None), P(), P(), P("frames"))
    return jax.shard_map(
        shards, mesh=mesh, in_specs=placed, out_specs=P("frames", "gz", None), check_vma=False
    )
```

```python
import functools

import jax
import jax.numpy as jnp
from jax import lax
from jax.experimental import pallas as pl
from jax.experimental.pallas import tpu as pltpu
from jax.sharding import PartitionSpec as P

REACH = 6.0
STEPS = 32767.0
BLOCK = 16
LANES = 128
PAD = 8
NT = 8
LIMIT = 24 * 1024 * 1024
FETCH_LIMIT = 43 * 1024 * 1024
BLEND_LIMIT = 16 * 1024 * 1024
FIRST = 4
PLANES = 4


def spread(table_ref, *row):
    sublane = lax.broadcasted_iota(jnp.int32, (NT, LANES), 0)
    table = jnp.zeros((NT, LANES), jnp.float32)
    for m in range(NT):
        table = jnp.where(sublane == m, table_ref[(*row, m)], table)
    return table


def lookup(table, index):
    parts = [
        jnp.take_along_axis(table, index[r : r + NT], axis=0, mode="promise_in_bounds")
        for r in range(0, index.shape[0], NT)
    ]
    return jnp.concatenate(parts, 0)


def alpha_of(centre, index, table):
    return lookup(table, index) * (1.0 - jnp.exp(-centre * centre))


def opacity_kernel(slices, tiles, turns, volume_hbm, index_hbm, opacity_ref, *rest):
    out_refs, (vol, idx, sems) = rest[:turns], rest[turns:]
    height = vol.shape[1] // turns
    plane = lax.axis_index("gz") // (lax.axis_size("gz") // turns)
    bases = [pl.multiple_of(lax.rem(plane + turn, turns) * height, height) for turn in range(turns)]
    copies = []
    for turn, base in enumerate(bases):
        some = pl.ds(base, height)
        pair = [
            pltpu.make_async_copy(source.at[:, some, :], target.at[:, some, :], sems.at[kind, turn])
            for kind, (source, target) in enumerate([(volume_hbm, vol), (index_hbm, idx)])
        ]
        for copy in pair:
            copy.start()
        copies.append(pair)
    table = spread(opacity_ref)
    for base, pair, out_ref in zip(bases, copies, out_refs):
        for copy in pair:
            copy.wait()

        @pl.loop(0, height // BLOCK)
        def _(i):
            rows = pl.ds(pl.multiple_of(base + i * BLOCK, BLOCK), BLOCK)
            for t in range(tiles):
                cols = pl.ds(t * LANES, LANES)
                transmit = None
                for k in range(slices):
                    clear = 1.0 - alpha_of(vol[k, rows, cols], idx[k, rows, cols], table)
                    transmit = clear if transmit is None else transmit * clear
                out_ref[i, :, cols] = (1.0 - transmit).astype(jnp.bfloat16)


def opacities(volume, tf_index, tf_opacity, turns):
    slices, height, width = volume.shape
    part = jax.ShapeDtypeStruct((height // BLOCK // turns, BLOCK, width), jnp.bfloat16)
    held = [jax.ShapeDtypeStruct(x.shape, x.dtype) for x in (volume, tf_index)]
    return pl.pallas_call(
        functools.partial(opacity_kernel, slices, width // LANES, turns),
        out_shape=[part] * turns + held,
        in_specs=[pl.BlockSpec(memory_space=pltpu.HBM)] * 2 + [pl.BlockSpec(memory_space=pltpu.SMEM)],
        out_specs=[pl.BlockSpec(memory_space=pltpu.VMEM)] * (turns + 2),
        scratch_shapes=[pltpu.SemaphoreType.DMA((2, turns))],
        compiler_params=pltpu.CompilerParams(vmem_limit_bytes=FETCH_LIMIT),
        cost_estimate=pl.CostEstimate(
            flops=15 * volume.size, bytes_accessed=9 * volume.size, transcendentals=volume.size
        ),
        name="opacities",
    )(volume, tf_index, tf_opacity)


def colour_kernel(slices, span, turns, by_member, vol, idx, before_ref, after_ref, colour_ref, opacity_ref, *rest):
    out_refs = rest[-turns:]
    height, width = before_ref.shape
    blocks, tiles = height // BLOCK, width // LANES
    each = blocks // turns
    device, members = lax.axis_index("gz"), lax.axis_size("gz") // turns
    plane, member = device // members, lax.rem(device, members)
    lane = lax.broadcasted_iota(jnp.int32, (BLOCK, LANES), 1)
    first_lane, last_lane = lane == 0, lane == LANES - 1
    sublane = lax.broadcasted_iota(jnp.int32, (PAD, LANES), 0)
    first_row, last_row = sublane == 0, sublane == PAD - 1
    opacity_table = spread(opacity_ref)
    colour_tables = [spread(colour_ref, c) for c in range(3)]

    def shade(i, out_ref, j):
        start = pl.multiple_of(i * BLOCK, BLOCK)
        rows = pl.ds(start, BLOCK)
        above = pl.ds(pl.multiple_of(jnp.maximum(start - PAD, 0), PAD), PAD)
        below = pl.ds(pl.multiple_of(jnp.minimum(start + BLOCK, height - PAD), PAD), PAD)
        for t in range(*span):
            cols = pl.ds(t * LANES, LANES)
            halo = [ref[rows, cols].astype(jnp.float32) * (REACH / STEPS) for ref in (before_ref, after_ref)]
            centres = [halo[0]] + [vol[k, rows, cols] for k in range(slices)] + [halo[1]]
            transmit, sums = None, None
            for k in range(slices):
                centre = centres[k + 1]
                depth = centres[k + 2] - centres[k]
                upper = jnp.where(i > 0, vol[k, above, cols], 0.0)
                lower = jnp.where(i + 1 < blocks, vol[k, below, cols], 0.0)
                eights = [upper] + [centre[r : r + PAD] for r in range(0, BLOCK, PAD)] + [lower]
                across = jnp.concatenate(
                    [
                        pltpu.roll(jnp.where(first_row, eights[e + 1], eights[e]), PAD - 1, 0)
                        - pltpu.roll(jnp.where(last_row, eights[e - 1], eights[e]), 1, 0)
                        for e in range(1, len(eights) - 1)
                    ],
                    0,
                )
                beside_left = vol[k, rows, pl.ds((t - 1) * LANES, LANES)] if t > 0 else 0.0
                beside_right = vol[k, rows, pl.ds((t + 1) * LANES, LANES)] if t + 1 < tiles else 0.0
                left = pltpu.roll(jnp.where(last_lane, beside_left, centre), 1, 1)
                right = pltpu.roll(jnp.where(first_lane, beside_right, centre), LANES - 1, 1)
                along = right - left
                facing = jnp.abs((0.65 * 0.48) * depth + (0.65 * 0.6) * across + (0.65 * 0.64) * along)
                squares = depth * depth + across * across + along * along + 4.0
                shading = 0.35 + facing * lax.rsqrt(squares)
                index = idx[k, rows, cols]
                alpha = alpha_of(centre, index, opacity_table)
                shown = shading * alpha
                if transmit is not None:
                    shown = transmit * shown
                terms = [lookup(table, index) * shown for table in colour_tables]
                sums = terms if sums is None else [s + add for s, add in zip(sums, terms)]
                if k + 1 < slices:
                    transmit = 1.0 - alpha if transmit is None else transmit * (1.0 - alpha)
            for c in range(3):
                out_ref[j, c, :, pl.ds((t - span[0]) * LANES, LANES)] = sums[c].astype(jnp.bfloat16)

    if not by_member:
        for turn, out_ref in enumerate(out_refs):
            base = lax.rem(plane + turn, turns) * each

            @pl.loop(0, each)
            def _(j):
                shade(base + j, out_ref, j)

        return
    for m, out_ref in enumerate(out_refs):
        @pl.loop(0, turns)
        def _(j):
            shade(lax.rem(plane + j, turns) * members + (member ^ m), out_ref, j)


def colours(volume, tf_index, before, after, tf_color, tf_opacity, span, turns, earlier=()):
    slices, height, _ = volume.shape
    part = jax.ShapeDtypeStruct((height // BLOCK // turns, 3, BLOCK, (span[1] - span[0]) * LANES), jnp.bfloat16)
    cells = slices * height * (span[1] - span[0]) * LANES
    return pl.pallas_call(
        functools.partial(colour_kernel, slices, span, turns, bool(earlier)),
        out_shape=[part] * turns,
        in_specs=[pl.BlockSpec(memory_space=pltpu.VMEM)] * 4
        + [pl.BlockSpec(memory_space=pltpu.SMEM)] * 2
        + [pl.BlockSpec(memory_space=pl.ANY)] * len(earlier),
        out_specs=[pl.BlockSpec(memory_space=pltpu.VMEM)] * turns,
        compiler_params=pltpu.CompilerParams(vmem_limit_bytes=LIMIT),
        cost_estimate=pl.CostEstimate(flops=50 * cells, bytes_accessed=40 * cells, transcendentals=2 * cells),
        name="colours",
    )(volume, tf_index, before, after, tf_color, tf_opacity, *earlier)


def on_chip(kernel, out_shapes, operands, earlier=()):
    return pl.pallas_call(
        kernel,
        out_shape=out_shapes,
        in_specs=[pl.BlockSpec(memory_space=pltpu.VMEM)] * len(operands)
        + [pl.BlockSpec(memory_space=pl.ANY)] * len(earlier),
        out_specs=[pl.BlockSpec(memory_space=pltpu.VMEM)] * len(out_shapes),
        compiler_params=pltpu.CompilerParams(vmem_limit_bytes=BLEND_LIMIT),
        name=kernel.func.__name__.removesuffix("_kernel"),
    )(*operands, *earlier)


def hold_kernel(count, *refs):
    for ref, out_ref in zip(refs[:count], refs[-count:]):
        out_ref[...] = ref[...]


def hold(parts, earlier):
    shapes = [jax.ShapeDtypeStruct(part.shape, part.dtype) for part in parts]
    return list(on_chip(functools.partial(hold_kernel, len(parts)), shapes, parts, earlier))


def turn_over_kernel(turns, *refs):
    here = lax.rem(lax.axis_index("gz"), turns)
    colour_refs, opacity_refs, second_refs, member_refs, plane_refs = (
        refs[turns * n : turns * (n + 1)] for n in range(5)
    )
    width, total = colour_refs[0].shape[-1], opacity_refs[0].shape[-1]
    for s, (colour_ref, opacity_ref, plane_ref) in enumerate(zip(colour_refs, opacity_refs, plane_refs)):
        for m, (second_ref, member_ref) in enumerate(zip(second_refs, member_refs)):
            plane_ref[m] = second_ref[s]
            for c in range(3):
                member_ref[s, :, pl.ds(c * width, width)] = colour_ref[here ^ m, c]
            member_ref[s, :, pl.ds(3 * width, total)] = opacity_ref[here ^ m]


def turn_over(first, opacity, second):
    turns, (_, _, height, width) = len(first), first[0].shape
    member = jax.ShapeDtypeStruct((turns, height, 3 * width + opacity[0].shape[-1]), jnp.bfloat16)
    plane = jax.ShapeDtypeStruct(second[0].shape, jnp.bfloat16)
    operands = [*first, *opacity, *second]
    done = on_chip(functools.partial(turn_over_kernel, turns), [member] * turns + [plane] * turns, operands)
    return done[:turns], done[turns:]


def in_plane(parts, devices):
    return [parts[0]] + [
        lax.ppermute(part, "gz", [(i, i ^ m) for i in range(devices)]) for m, part in enumerate(parts[1:], 1)
    ]


def blend_kernel(ranks, turns, side, order_ref, *rest):
    first_refs, second_refs = rest[:turns], rest[turns:-6]
    out_hbm, place, colour_ref, opacity_ref, out_ref, sem = rest[-6:]
    device = lax.axis_index("gz")
    plane, member = device // turns, lax.rem(device, turns)
    width, total = out_ref.shape[2], out_hbm.shape[2]
    start = total - width if side else 0
    before = first_refs[0].shape[2] - total
    for b in range(ranks):
        place[order_ref[b]] = b
    for m in range(turns):
        for s in range(turns):
            brick = lax.rem(plane + turns - s, turns) * turns + (member ^ m)
            for c in range(3):
                colour_ref[brick, c] = second_refs[s][m, c] if side else first_refs[m][s, :, pl.ds(c * width, width)]
            opacity_ref[brick] = first_refs[m][s, :, pl.ds(before + start, width)]
    for j in range(width // LANES):
        cols = pl.ds(j * LANES, LANES)
        canvas = (jnp.zeros((out_ref.shape[1], LANES), jnp.float32),) * 4
        for rank in range(ranks):
            b = place[rank]
            clear = 1.0 - canvas[3]
            layers = [colour_ref[b, c, :, cols] for c in range(3)] + [opacity_ref[b, :, cols]]
            canvas = tuple(front + clear * back.astype(jnp.float32) for front, back in zip(canvas, layers))
        for c in range(4):
            out_ref[c, :, cols] = canvas[c]
    copy = pltpu.make_async_copy(out_ref, out_hbm.at[:, :, pl.ds(start, width)], sem)
    copy.start()
    copy.wait()


def blend(order, turns, total, first, second=(), image=()):
    ranks, height = order.shape[0], first[0].shape[1]
    width = second[0].shape[-1] if second else (first[0].shape[2] - total) // 3
    operands = [order, *first, *second]
    return pl.pallas_call(
        functools.partial(blend_kernel, ranks, turns, 1 if second else 0),
        out_shape=jax.ShapeDtypeStruct((4, height, total), jnp.float32),
        in_specs=[pl.BlockSpec(memory_space=pltpu.SMEM)]
        + [pl.BlockSpec(memory_space=pltpu.VMEM)] * (len(operands) - 1)
        + [pl.BlockSpec(memory_space=pltpu.HBM)] * len(image),
        out_specs=pl.BlockSpec(memory_space=pltpu.HBM),
        scratch_shapes=[
            pltpu.SMEM((ranks,), jnp.int32),
            pltpu.VMEM((ranks, 3, height, width), jnp.bfloat16),
            pltpu.VMEM((ranks, height, width), jnp.bfloat16),
            pltpu.VMEM((4, height, width), jnp.float32),
            pltpu.SemaphoreType.DMA,
        ],
        input_output_aliases={len(operands): 0} if image else {},
        compiler_params=pltpu.CompilerParams(vmem_limit_bytes=BLEND_LIMIT),
        name="blend",
    )(*operands, *image)


def blend_plain(order, colour, opacity):
    ranks = opacity.shape[0]
    place = jnp.zeros((ranks,), jnp.int32).at[order].set(jnp.arange(ranks, dtype=jnp.int32))
    layers = jnp.concatenate([colour, opacity[:, None]], 1)

    def step(canvas, b):
        layer = lax.dynamic_index_in_dim(layers, b, 0, keepdims=False).astype(jnp.float32)
        return canvas + (1.0 - canvas[3:4]) * layer, None

    return lax.scan(step, jnp.zeros(layers.shape[1:], jnp.float32), place)[0]


def by_owner(blocks_first, devices):
    blocks, width = blocks_first.shape[0], blocks_first.shape[-1]
    middle = blocks_first.shape[1:-2]
    if blocks == devices:
        return blocks_first
    each = devices // blocks
    split = blocks_first.reshape((blocks,) + middle + (each, BLOCK // each, width))
    moved = jnp.moveaxis(split, len(middle) + 1, 1)
    return moved.reshape((devices,) + middle + (BLOCK // each, width))


def exchange(x):
    return lax.all_to_all(x, "gz", split_axis=0, concat_axis=0, tiled=True)


def coded(a_slice):
    return jnp.round(a_slice * (STEPS / REACH)).astype(jnp.int16)


def across_planes(parts, turns, devices):
    return [parts[0]] + [
        lax.ppermute(part, "gz", [(i, (i + s * turns) % devices) for i in range(devices)])
        for s, part in enumerate(parts[1:], 1)
    ]


def shards(volume, tf_index, tf_color, tf_opacity, order):
    devices = lax.axis_size("gz")
    slices, height, width = volume.shape
    up = [(i, i + 1) for i in range(devices - 1)]
    down = [(j, i) for i, j in up]
    last, initial = coded(volume[slices - 1]), coded(volume[0])
    before = lax.ppermute(last, "gz", up)
    after = lax.ppermute(initial, "gz", down)
    turns = PLANES if devices == PLANES * PLANES and height // devices == BLOCK else 1
    *opacity, volume, tf_index = opacities(volume, tf_index, tf_opacity, turns)
    tiles = width // LANES
    held = (volume, tf_index, before, after, tf_color, tf_opacity)
    if turns == 1:
        colour = by_owner(colours(*held, (0, tiles), 1)[0], devices)
        return blend_plain(order, exchange(colour), exchange(by_owner(opacity[0], devices)))
    split = tiles * FIRST // 8
    opacity = across_planes(opacity, turns, devices)
    own, *others = colours(*held, (0, split), turns)
    second = in_plane(colours(*held, (split, tiles), turns, (own,)), devices)
    first = across_planes([own] + hold(others, opacity[1:]), turns, devices)
    first, second = turn_over(first, opacity, second)
    first, second = in_plane(first, devices), across_planes(second, turns, devices)
    return blend(order, turns, width, first, second, (blend(order, turns, width, first),))


def solution(mesh):
    placed = (P("gz", "frames", None), P("gz", "frames", None), P(), P(), P("frames"))
    return jax.shard_map(
        shards, mesh=mesh, in_specs=placed, out_specs=P("frames", "gz", None), check_vma=False
    )
```

```python
import functools

import jax
import jax.numpy as jnp
from jax import lax
from jax.experimental import pallas as pl
from jax.experimental.pallas import tpu as pltpu
from jax.sharding import PartitionSpec as P

REACH = 6.0
STEPS = 32767.0
BLOCK = 16
LANES = 128
PAD = 8
NT = 8
LIMIT = 24 * 1024 * 1024
FETCH_LIMIT = 43 * 1024 * 1024
REFETCH_LIMIT = 50 * 1024 * 1024
BLEND_LIMIT = 16 * 1024 * 1024
FIRST = 5
PLANES = 4


def spread(table_ref, *row):
    sublane = lax.broadcasted_iota(jnp.int32, (NT, LANES), 0)
    table = jnp.zeros((NT, LANES), jnp.float32)
    for m in range(NT):
        table = jnp.where(sublane == m, table_ref[(*row, m)], table)
    return table


def lookup(table, index):
    parts = [
        jnp.take_along_axis(table, index[r : r + NT], axis=0, mode="promise_in_bounds")
        for r in range(0, index.shape[0], NT)
    ]
    return jnp.concatenate(parts, 0)


def alpha_of(centre, index, table):
    return lookup(table, index) * (1.0 - jnp.exp(-centre * centre))


def opacity_kernel(slices, tiles, turns, volume_hbm, index_hbm, opacity_ref, *rest):
    out_refs, (vol, idx, sems) = rest[:-3], rest[-3:]
    height = vol.shape[1] // turns
    plane = lax.axis_index("gz") // (lax.axis_size("gz") // turns)
    bases = [pl.multiple_of((plane ^ turn) * height, height) for turn in range(turns)]
    copies = []
    for turn, base in enumerate(bases):
        some = pl.ds(base, height)
        pair = [
            pltpu.make_async_copy(source.at[:, some, :], target.at[:, some, :], sems.at[kind, turn])
            for kind, (source, target) in enumerate([(volume_hbm, vol), (index_hbm, idx)])
        ]
        for copy in pair:
            copy.start()
        copies.append(pair)
    table = spread(opacity_ref)
    shared = turns // len(out_refs)
    blocks = height // BLOCK
    for turn, (base, pair) in enumerate(zip(bases, copies)):
        out_ref, at = out_refs[turn // shared], turn % shared * blocks
        for copy in pair:
            copy.wait()

        @pl.loop(0, blocks)
        def _(i):
            rows = pl.ds(pl.multiple_of(base + i * BLOCK, BLOCK), BLOCK)
            for t in range(tiles):
                cols = pl.ds(t * LANES, LANES)
                transmit = None
                for k in range(slices):
                    clear = 1.0 - alpha_of(vol[k, rows, cols], idx[k, rows, cols], table)
                    transmit = clear if transmit is None else transmit * clear
                out_ref[at + i, :, cols] = (1.0 - transmit).astype(jnp.bfloat16)


def opacities(volume, tf_index, tf_opacity, turns):
    slices, height, width = volume.shape
    parts = min(turns, 2)
    part = jax.ShapeDtypeStruct((height // BLOCK // parts, BLOCK, width), jnp.bfloat16)
    held = [jax.ShapeDtypeStruct(x.shape, x.dtype) for x in (volume, tf_index)]
    return pl.pallas_call(
        functools.partial(opacity_kernel, slices, width // LANES, turns),
        out_shape=[part] * parts + held,
        in_specs=[pl.BlockSpec(memory_space=pltpu.HBM)] * 2 + [pl.BlockSpec(memory_space=pltpu.SMEM)],
        out_specs=[pl.BlockSpec(memory_space=pltpu.VMEM)] * (parts + 2),
        scratch_shapes=[pltpu.SemaphoreType.DMA((2, turns))],
        compiler_params=pltpu.CompilerParams(vmem_limit_bytes=FETCH_LIMIT),
        cost_estimate=pl.CostEstimate(
            flops=15 * volume.size, bytes_accessed=9 * volume.size, transcendentals=volume.size
        ),
        name="opacities",
    )(volume, tf_index, tf_opacity)


def colour_kernel(slices, span, turns, by_member, vol, idx, before_ref, after_ref, colour_ref, opacity_ref, *rest):
    out_refs, skipped = rest[-turns:], 0
    if by_member:
        out_refs, (volume_here, index_here, sems) = rest[-turns - 3 : -3], rest[-3:]
        skipped = span[0] - 1
        some = pl.ds(skipped * LANES, volume_here.shape[2])
        copies = [
            pltpu.make_async_copy(source.at[:, :, some], target, sems.at[n])
            for n, (source, target) in enumerate([(vol, volume_here), (idx, index_here)])
        ]
        for copy in copies:
            copy.start()
        for copy in copies:
            copy.wait()
        vol, idx = volume_here, index_here
    height, width = before_ref.shape
    blocks, tiles = height // BLOCK, width // LANES
    each = blocks // turns
    device, members = lax.axis_index("gz"), lax.axis_size("gz") // turns
    plane, member = device // members, lax.rem(device, members)
    lane = lax.broadcasted_iota(jnp.int32, (BLOCK, LANES), 1)
    first_lane, last_lane = lane == 0, lane == LANES - 1
    sublane = lax.broadcasted_iota(jnp.int32, (PAD, LANES), 0)
    first_row, last_row = sublane == 0, sublane == PAD - 1
    opacity_table = spread(opacity_ref)
    colour_tables = [spread(colour_ref, c) for c in range(3)]

    def shade(i, out_ref, j):
        start = pl.multiple_of(i * BLOCK, BLOCK)
        rows = pl.ds(start, BLOCK)
        above = pl.ds(pl.multiple_of(jnp.maximum(start - PAD, 0), PAD), PAD)
        below = pl.ds(pl.multiple_of(jnp.minimum(start + BLOCK, height - PAD), PAD), PAD)
        for t in range(*span):
            u = t - skipped
            cols = pl.ds(u * LANES, LANES)
            halo = [ref[rows, pl.ds(t * LANES, LANES)].astype(jnp.float32) * (REACH / STEPS) for ref in (before_ref, after_ref)]
            centres = [halo[0]] + [vol[k, rows, cols] for k in range(slices)] + [halo[1]]
            transmit, sums = None, None
            for k in range(slices):
                centre = centres[k + 1]
                depth = centres[k + 2] - centres[k]
                upper = jnp.where(i > 0, vol[k, above, cols], 0.0)
                lower = jnp.where(i + 1 < blocks, vol[k, below, cols], 0.0)
                eights = [upper] + [centre[r : r + PAD] for r in range(0, BLOCK, PAD)] + [lower]
                across = jnp.concatenate(
                    [
                        pltpu.roll(jnp.where(first_row, eights[e + 1], eights[e]), PAD - 1, 0)
                        - pltpu.roll(jnp.where(last_row, eights[e - 1], eights[e]), 1, 0)
                        for e in range(1, len(eights) - 1)
                    ],
                    0,
                )
                beside_left = vol[k, rows, pl.ds((u - 1) * LANES, LANES)] if t > 0 else 0.0
                beside_right = vol[k, rows, pl.ds((u + 1) * LANES, LANES)] if t + 1 < tiles else 0.0
                left = pltpu.roll(jnp.where(last_lane, beside_left, centre), 1, 1)
                right = pltpu.roll(jnp.where(first_lane, beside_right, centre), LANES - 1, 1)
                along = right - left
                facing = jnp.abs((0.65 * 0.48) * depth + (0.65 * 0.6) * across + (0.65 * 0.64) * along)
                squares = depth * depth + across * across + along * along + 4.0
                shading = 0.35 + facing * lax.rsqrt(squares)
                index = idx[k, rows, cols]
                alpha = alpha_of(centre, index, opacity_table)
                shown = shading * alpha
                if transmit is not None:
                    shown = transmit * shown
                terms = [lookup(table, index) * shown for table in colour_tables]
                sums = terms if sums is None else [s + add for s, add in zip(sums, terms)]
                if k + 1 < slices:
                    transmit = 1.0 - alpha if transmit is None else transmit * (1.0 - alpha)
            for c in range(3):
                out_ref[j, c, :, pl.ds((t - span[0]) * LANES, LANES)] = sums[c].astype(jnp.bfloat16)

    if not by_member:
        for turn, out_ref in enumerate(out_refs):
            base = lax.rem(plane + turn, turns) * each

            @pl.loop(0, each)
            def _(j):
                shade(base + j, out_ref, j)

        return
    for m, out_ref in enumerate(out_refs):
        @pl.loop(0, turns)
        def _(j):
            shade(lax.rem(plane + j, turns) * members + (member ^ m), out_ref, j)


def colours(volume, tf_index, before, after, tf_color, tf_opacity, span, turns, earlier=()):
    slices, height, _ = volume.shape
    part = jax.ShapeDtypeStruct((height // BLOCK // turns, 3, BLOCK, (span[1] - span[0]) * LANES), jnp.bfloat16)
    held = []
    if earlier:
        near = (slices, height, volume.shape[2] - (span[0] - 1) * LANES)
        held = [pltpu.VMEM(near, volume.dtype), pltpu.VMEM(near, tf_index.dtype), pltpu.SemaphoreType.DMA((2,))]
    cells = slices * height * (span[1] - span[0]) * LANES
    return pl.pallas_call(
        functools.partial(colour_kernel, slices, span, turns, bool(earlier)),
        out_shape=[part] * turns,
        in_specs=[pl.BlockSpec(memory_space=pltpu.HBM if earlier else pltpu.VMEM)] * 2
        + [pl.BlockSpec(memory_space=pltpu.VMEM)] * 2
        + [pl.BlockSpec(memory_space=pltpu.SMEM)] * 2
        + [pl.BlockSpec(memory_space=pl.ANY)] * len(earlier),
        out_specs=[pl.BlockSpec(memory_space=pltpu.VMEM)] * turns,
        scratch_shapes=held,
        compiler_params=pltpu.CompilerParams(vmem_limit_bytes=REFETCH_LIMIT if earlier else LIMIT),
        cost_estimate=pl.CostEstimate(flops=50 * cells, bytes_accessed=40 * cells, transcendentals=2 * cells),
        name="colours",
    )(volume, tf_index, before, after, tf_color, tf_opacity, *earlier)


def on_chip(kernel, out_shapes, operands, earlier=()):
    return pl.pallas_call(
        kernel,
        out_shape=out_shapes,
        in_specs=[pl.BlockSpec(memory_space=pltpu.VMEM)] * len(operands)
        + [pl.BlockSpec(memory_space=pl.ANY)] * len(earlier),
        out_specs=[pl.BlockSpec(memory_space=pltpu.VMEM)] * len(out_shapes),
        compiler_params=pltpu.CompilerParams(vmem_limit_bytes=BLEND_LIMIT),
        name=kernel.func.__name__.removesuffix("_kernel"),
    )(*operands, *earlier)


def to_planes_kernel(turns, *refs):
    for m, ref in enumerate(refs[:turns]):
        for s, out_ref in enumerate(refs[turns:]):
            out_ref[m] = ref[s]


def to_planes(parts):
    turns = len(parts)
    shapes = [jax.ShapeDtypeStruct(parts[0].shape, parts[0].dtype)] * turns
    return on_chip(functools.partial(to_planes_kernel, turns), shapes, parts)


def to_others(parts, devices):
    return [parts[0]] + [
        lax.ppermute(part, "gz", [(i, i ^ m) for i in range(devices)]) for m, part in enumerate(parts[1:], 1)
    ]


def to_members_kernel(turns, *refs):
    here = lax.rem(lax.axis_index("gz"), turns)
    for t in range(turns):
        for m in range(turns):
            refs[m // 2 - 2][m % 2 * turns + t] = swapped_in(refs[:3], turns, t, here ^ m)


def to_members(arrived, turns, earlier=()):
    part = jax.ShapeDtypeStruct(arrived[0].shape, jnp.bfloat16)
    return on_chip(functools.partial(to_members_kernel, turns), [part] * 2, arrived, earlier)


def hold_kernel(ref, *rest):
    rest[-1][...] = ref[...]


def hold(part, earlier):
    shape = jax.ShapeDtypeStruct(part.shape, part.dtype)
    return on_chip(functools.partial(hold_kernel), [shape], [part], earlier)[0]


def to_near_kernel(turns, near_ref, far_ref, *rest):
    rest[-1][pl.ds(0, turns)] = near_ref[pl.ds(turns, turns)]
    rest[-1][pl.ds(turns, turns)] = far_ref[pl.ds(turns, turns)]


def swap(part, devices, stride):
    return lax.ppermute(part, "gz", [(i, i ^ stride) for i in range(devices)])


def swap_near(near, far, devices, stride, earlier=()):
    shape = jax.ShapeDtypeStruct(near.shape, near.dtype)
    kernel = functools.partial(to_near_kernel, near.shape[0] // 2)
    (passed,) = on_chip(kernel, [shape], [near, far], earlier)
    return [near, far, swap(passed, devices, stride)]


def swapped_in(refs, turns, m, entry):
    near_ref, far_ref, passed_ref = refs
    return [near_ref, passed_ref, far_ref, passed_ref][m][entry if m < 3 else turns + entry]


def blend_kernel(ranks, turns, start, order_ref, *rest):
    opacity_refs, colour_refs = rest[:3], rest[3:-6]
    out_hbm, place, colour_ref, opacity_ref, out_ref, sem = rest[-6:]
    device = lax.axis_index("gz")
    plane, member = device // turns, lax.rem(device, turns)
    width = out_ref.shape[2]
    for b in range(ranks):
        place[order_ref[b]] = b
    for m in range(turns):
        for s in range(turns):
            brick = lax.rem(plane + turns - s, turns) * turns + (member ^ m)
            at = (plane ^ s) * turns + (member ^ m)
            opacity_ref[at] = swapped_in(opacity_refs, turns, m, s)[:, start : start + width]
            if start > 0:
                colour_ref[brick] = colour_refs[s][m]
    if start == 0:
        colour_ref = colour_refs[0]
    for j in range(width // LANES):
        cols = pl.ds(j * LANES, LANES)
        canvas = (jnp.zeros((out_ref.shape[1], LANES), jnp.float32),) * 4
        for rank in range(ranks):
            b = place[rank]
            clear = 1.0 - canvas[3]
            layers = [colour_ref[b, c, :, cols] for c in range(3)] + [opacity_ref[b, :, cols]]
            canvas = tuple(front + clear * back.astype(jnp.float32) for front, back in zip(canvas, layers))
        for c in range(4):
            out_ref[c, :, cols] = canvas[c]
    copy = pltpu.make_async_copy(out_ref, out_hbm.at[:, :, pl.ds(start, width)], sem)
    copy.start()
    copy.wait()


def blend(order, turns, total, start, opacity, colour, image=()):
    ranks = order.shape[0]
    height, width = colour[0].shape[-2:]
    operands = [order, *opacity, *colour]
    return pl.pallas_call(
        functools.partial(blend_kernel, ranks, turns, start),
        out_shape=jax.ShapeDtypeStruct((4, height, total), jnp.float32),
        in_specs=[pl.BlockSpec(memory_space=pltpu.SMEM)]
        + [pl.BlockSpec(memory_space=pltpu.VMEM)] * (len(operands) - 1)
        + [pl.BlockSpec(memory_space=pltpu.HBM)] * len(image),
        out_specs=pl.BlockSpec(memory_space=pltpu.HBM),
        scratch_shapes=[
            pltpu.SMEM((ranks,), jnp.int32),
            pltpu.VMEM((ranks, 3, height, width), jnp.bfloat16),
            pltpu.VMEM((ranks, height, width), jnp.bfloat16),
            pltpu.VMEM((4, height, width), jnp.float32),
            pltpu.SemaphoreType.DMA,
        ],
        input_output_aliases={len(operands): 0} if image else {},
        compiler_params=pltpu.CompilerParams(vmem_limit_bytes=BLEND_LIMIT),
        name="blend",
    )(*operands, *image)


def blend_plain(order, colour, opacity):
    ranks = opacity.shape[0]
    place = jnp.zeros((ranks,), jnp.int32).at[order].set(jnp.arange(ranks, dtype=jnp.int32))
    layers = jnp.concatenate([colour, opacity[:, None]], 1)

    def step(canvas, b):
        layer = lax.dynamic_index_in_dim(layers, b, 0, keepdims=False).astype(jnp.float32)
        return canvas + (1.0 - canvas[3:4]) * layer, None

    return lax.scan(step, jnp.zeros(layers.shape[1:], jnp.float32), place)[0]


def by_owner(blocks_first, devices):
    blocks, width = blocks_first.shape[0], blocks_first.shape[-1]
    middle = blocks_first.shape[1:-2]
    if blocks == devices:
        return blocks_first
    each = devices // blocks
    split = blocks_first.reshape((blocks,) + middle + (each, BLOCK // each, width))
    moved = jnp.moveaxis(split, len(middle) + 1, 1)
    return moved.reshape((devices,) + middle + (BLOCK // each, width))


def exchange(x):
    return lax.all_to_all(x, "gz", split_axis=0, concat_axis=0, tiled=True)


def coded(a_slice):
    return jnp.round(a_slice * (STEPS / REACH)).astype(jnp.int16)


def across_planes(parts, turns, devices):
    return [parts[0]] + [
        lax.ppermute(part, "gz", [(i, (i + s * turns) % devices) for i in range(devices)])
        for s, part in enumerate(parts[1:], 1)
    ]


def shards(volume, tf_index, tf_color, tf_opacity, order):
    devices = lax.axis_size("gz")
    slices, height, width = volume.shape
    up = [(i, i + 1) for i in range(devices - 1)]
    down = [(j, i) for i, j in up]
    last, initial = coded(volume[slices - 1]), coded(volume[0])
    before = lax.ppermute(last, "gz", up)
    after = lax.ppermute(initial, "gz", down)
    turns = PLANES if devices == PLANES * PLANES and height // devices == BLOCK else 1
    whole, tiles = (volume, tf_index), width // LANES
    *opacity, volume, tf_index = opacities(volume, tf_index, tf_opacity, turns)
    others = (before, after, tf_color, tf_opacity)
    held = (volume, tf_index, *others)
    if turns == 1:
        colour = by_owner(colours(*held, (0, tiles), 1)[0], devices)
        return blend_plain(order, exchange(colour), exchange(by_owner(opacity[0], devices)))
    split = tiles * FIRST // 8
    near, far = opacity
    far = swap(far, devices, 2 * turns)
    (first,) = colours(*held, (0, split), 1)
    second = colours(*whole, *others, (split, tiles), turns, (first,))
    opacity = swap_near(near, far, devices, turns, (first,))
    first = exchange(hold(first, (far,)))
    near, far = to_members(opacity, turns, second[:1])
    opacity = swap_near(near, swap(far, devices, 2), devices, 1)
    second = across_planes(to_planes(to_others(second, devices)), turns, devices)
    image = blend(order, turns, width, 0, opacity, [first])
    return blend(order, turns, width, split * LANES, opacity, second, (image,))


def solution(mesh):
    placed = (P("gz", "frames", None), P("gz", "frames", None), P(), P(), P("frames"))
    return jax.shard_map(
        shards, mesh=mesh, in_specs=placed, out_specs=P("frames", "gz", None), check_vma=False
    )
```

```python
import functools

import jax
import jax.numpy as jnp
from jax import lax
from jax.experimental import pallas as pl
from jax.experimental.pallas import tpu as pltpu
from jax.sharding import PartitionSpec as P

REACH = 6.0
STEPS = 32767.0
BLOCK = 16
LANES = 128
PAD = 8
NT = 8
LIMIT = 24 * 1024 * 1024
FETCH_LIMIT = 43 * 1024 * 1024
BLEND_LIMIT = 16 * 1024 * 1024
PLANES = 4


def spread(table_ref, *row):
    sublane = lax.broadcasted_iota(jnp.int32, (NT, LANES), 0)
    table = jnp.zeros((NT, LANES), jnp.float32)
    for m in range(NT):
        table = jnp.where(sublane == m, table_ref[(*row, m)], table)
    return table


def lookup(table, index):
    parts = [
        jnp.take_along_axis(table, index[r : r + NT], axis=0, mode="promise_in_bounds")
        for r in range(0, index.shape[0], NT)
    ]
    return jnp.concatenate(parts, 0)


def alpha_of(centre, index, table):
    return lookup(table, index) * (1.0 - jnp.exp(-centre * centre))


def opacity_kernel(slices, tiles, turns, volume_hbm, index_hbm, opacity_ref, *rest):
    out_refs, (vol, idx, sems) = rest[:turns], rest[turns:]
    height = vol.shape[1] // turns
    plane = lax.axis_index("gz") // (lax.axis_size("gz") // turns)
    bases = [pl.multiple_of(lax.rem(plane + turn, turns) * height, height) for turn in range(turns)]
    copies = []
    for turn, base in enumerate(bases):
        some = pl.ds(base, height)
        pair = [
            pltpu.make_async_copy(source.at[:, some, :], target.at[:, some, :], sems.at[kind, turn])
            for kind, (source, target) in enumerate([(volume_hbm, vol), (index_hbm, idx)])
        ]
        for copy in pair:
            copy.start()
        copies.append(pair)
    table = spread(opacity_ref)
    for base, pair, out_ref in zip(bases, copies, out_refs):
        for copy in pair:
            copy.wait()

        @pl.loop(0, height // BLOCK)
        def _(i):
            rows = pl.ds(pl.multiple_of(base + i * BLOCK, BLOCK), BLOCK)
            for t in range(tiles):
                cols = pl.ds(t * LANES, LANES)
                transmit = None
                for k in range(slices):
                    clear = 1.0 - alpha_of(vol[k, rows, cols], idx[k, rows, cols], table)
                    transmit = clear if transmit is None else transmit * clear
                out_ref[i, :, cols] = (1.0 - transmit).astype(jnp.bfloat16)


def opacities(volume, tf_index, tf_opacity, turns):
    slices, height, width = volume.shape
    part = jax.ShapeDtypeStruct((height // BLOCK // turns, BLOCK, width), jnp.bfloat16)
    held = [jax.ShapeDtypeStruct(x.shape, x.dtype) for x in (volume, tf_index)]
    return pl.pallas_call(
        functools.partial(opacity_kernel, slices, width // LANES, turns),
        out_shape=[part] * turns + held,
        in_specs=[pl.BlockSpec(memory_space=pltpu.HBM)] * 2 + [pl.BlockSpec(memory_space=pltpu.SMEM)],
        out_specs=[pl.BlockSpec(memory_space=pltpu.VMEM)] * (turns + 2),
        scratch_shapes=[pltpu.SemaphoreType.DMA((2, turns))],
        compiler_params=pltpu.CompilerParams(vmem_limit_bytes=FETCH_LIMIT),
        cost_estimate=pl.CostEstimate(
            flops=15 * volume.size, bytes_accessed=9 * volume.size, transcendentals=volume.size
        ),
        name="opacities",
    )(volume, tf_index, tf_opacity)


def colour_kernel(
    slices, tiles, vol, idx, before_ref, after_ref, colour_ref, opacity_ref, out_ref
):
    height = before_ref.shape[0]
    blocks = height // BLOCK
    lane = lax.broadcasted_iota(jnp.int32, (BLOCK, LANES), 1)
    first_lane, last_lane = lane == 0, lane == LANES - 1
    sublane = lax.broadcasted_iota(jnp.int32, (PAD, LANES), 0)
    first_row, last_row = sublane == 0, sublane == PAD - 1
    opacity_table = spread(opacity_ref)
    colour_tables = [spread(colour_ref, c) for c in range(3)]

    def shade(i):
        start = pl.multiple_of(i * BLOCK, BLOCK)
        rows = pl.ds(start, BLOCK)
        above = pl.ds(pl.multiple_of(jnp.maximum(start - PAD, 0), PAD), PAD)
        below = pl.ds(pl.multiple_of(jnp.minimum(start + BLOCK, height - PAD), PAD), PAD)
        for t in range(tiles):
            cols = pl.ds(t * LANES, LANES)
            halo = [ref[rows, cols].astype(jnp.float32) * (REACH / STEPS) for ref in (before_ref, after_ref)]
            centres = [halo[0]] + [vol[k, rows, cols] for k in range(slices)] + [halo[1]]
            transmit, sums = None, None
            for k in range(slices):
                centre = centres[k + 1]
                depth = centres[k + 2] - centres[k]
                upper = jnp.where(i > 0, vol[k, above, cols], 0.0)
                lower = jnp.where(i + 1 < blocks, vol[k, below, cols], 0.0)
                eights = [upper] + [centre[r : r + PAD] for r in range(0, BLOCK, PAD)] + [lower]
                across = jnp.concatenate(
                    [
                        pltpu.roll(jnp.where(first_row, eights[e + 1], eights[e]), PAD - 1, 0)
                        - pltpu.roll(jnp.where(last_row, eights[e - 1], eights[e]), 1, 0)
                        for e in range(1, len(eights) - 1)
                    ],
                    0,
                )
                beside_left = vol[k, rows, pl.ds((t - 1) * LANES, LANES)] if t > 0 else 0.0
                beside_right = vol[k, rows, pl.ds((t + 1) * LANES, LANES)] if t + 1 < tiles else 0.0
                left = pltpu.roll(jnp.where(last_lane, beside_left, centre), 1, 1)
                right = pltpu.roll(jnp.where(first_lane, beside_right, centre), LANES - 1, 1)
                along = right - left
                facing = jnp.abs((0.65 * 0.48) * depth + (0.65 * 0.6) * across + (0.65 * 0.64) * along)
                squares = depth * depth + across * across + along * along + 4.0
                shading = 0.35 + facing * lax.rsqrt(squares)
                index = idx[k, rows, cols]
                alpha = alpha_of(centre, index, opacity_table)
                shown = shading * alpha
                if transmit is not None:
                    shown = transmit * shown
                terms = [lookup(table, index) * shown for table in colour_tables]
                sums = terms if sums is None else [s + add for s, add in zip(sums, terms)]
                if k + 1 < slices:
                    transmit = 1.0 - alpha if transmit is None else transmit * (1.0 - alpha)
            for c in range(3):
                out_ref[i, c, :, cols] = sums[c].astype(jnp.bfloat16)

    @pl.loop(0, blocks)
    def _(i):
        shade(i)


def colours(volume, tf_index, before, after, tf_color, tf_opacity):
    slices, height, width = volume.shape
    blocks = height // BLOCK
    shape = (blocks, 3, BLOCK, width)
    return pl.pallas_call(
        functools.partial(colour_kernel, slices, width // LANES),
        out_shape=jax.ShapeDtypeStruct(shape, jnp.bfloat16),
        in_specs=[pl.BlockSpec(memory_space=pltpu.VMEM)] * 4 + [pl.BlockSpec(memory_space=pltpu.SMEM)] * 2,
        out_specs=pl.BlockSpec(memory_space=pltpu.VMEM),
        compiler_params=pltpu.CompilerParams(vmem_limit_bytes=LIMIT),
        cost_estimate=pl.CostEstimate(
            flops=50 * volume.size, bytes_accessed=40 * volume.size, transcendentals=2 * volume.size
        ),
        name="colours",
    )(volume, tf_index, before, after, tf_color, tf_opacity)


def regroup_kernel(turns, *refs):
    here = lax.rem(lax.axis_index("gz"), turns)
    for s, ref in enumerate(refs[:turns]):
        for m, out_ref in enumerate(refs[turns:]):
            out_ref[s] = ref[here ^ m]


def regroup(parts):
    turns = len(parts)
    return pl.pallas_call(
        functools.partial(regroup_kernel, turns),
        out_shape=[jax.ShapeDtypeStruct(parts[0].shape, parts[0].dtype)] * turns,
        in_specs=[pl.BlockSpec(memory_space=pltpu.VMEM)] * turns,
        out_specs=[pl.BlockSpec(memory_space=pltpu.VMEM)] * turns,
        compiler_params=pltpu.CompilerParams(vmem_limit_bytes=BLEND_LIMIT),
        name="regroup",
    )(*parts)


def blend_kernel(ranks, turns, order_ref, colour_ref, *rest):
    opacity_refs, (out_ref, place, opacity_ref) = rest[:turns], rest[turns:]
    device = lax.axis_index("gz")
    plane, member = device // turns, lax.rem(device, turns)
    for b in range(ranks):
        place[order_ref[b]] = b
    for m, ref in enumerate(opacity_refs):
        for s in range(turns):
            brick = lax.rem(plane + turns - s, turns) * turns + (member ^ m)
            opacity_ref[brick] = ref[s]
    for j in range(colour_ref.shape[3] // LANES):
        cols = pl.ds(j * LANES, LANES)
        canvas = (jnp.zeros((colour_ref.shape[2], LANES), jnp.float32),) * 4
        for rank in range(ranks):
            b = place[rank]
            clear = 1.0 - canvas[3]
            layers = [colour_ref[b, c, :, cols] for c in range(3)] + [opacity_ref[b, :, cols]]
            canvas = tuple(front + clear * back.astype(jnp.float32) for front, back in zip(canvas, layers))
        for c in range(4):
            out_ref[c, :, cols] = canvas[c]


def blend(order, colour, opacity_parts):
    ranks, channels, height, width = colour.shape
    turns = len(opacity_parts)
    return pl.pallas_call(
        functools.partial(blend_kernel, ranks, turns),
        out_shape=jax.ShapeDtypeStruct((4, height, width), jnp.float32),
        in_specs=[pl.BlockSpec(memory_space=pltpu.SMEM)] + [pl.BlockSpec(memory_space=pltpu.VMEM)] * (1 + turns),
        out_specs=pl.BlockSpec(memory_space=pltpu.VMEM),
        scratch_shapes=[pltpu.SMEM((ranks,), jnp.int32), pltpu.VMEM((ranks, height, width), colour.dtype)],
        compiler_params=pltpu.CompilerParams(vmem_limit_bytes=BLEND_LIMIT),
        name="blend",
    )(order, colour, *opacity_parts)


def blend_plain(order, colour, opacity):
    ranks = opacity.shape[0]
    place = jnp.zeros((ranks,), jnp.int32).at[order].set(jnp.arange(ranks, dtype=jnp.int32))
    layers = jnp.concatenate([colour, opacity[:, None]], 1)

    def step(canvas, b):
        layer = lax.dynamic_index_in_dim(layers, b, 0, keepdims=False).astype(jnp.float32)
        return canvas + (1.0 - canvas[3:4]) * layer, None

    return lax.scan(step, jnp.zeros(layers.shape[1:], jnp.float32), place)[0]


def by_owner(blocks_first, devices):
    blocks, width = blocks_first.shape[0], blocks_first.shape[-1]
    middle = blocks_first.shape[1:-2]
    if blocks == devices:
        return blocks_first
    each = devices // blocks
    split = blocks_first.reshape((blocks,) + middle + (each, BLOCK // each, width))
    moved = jnp.moveaxis(split, len(middle) + 1, 1)
    return moved.reshape((devices,) + middle + (BLOCK // each, width))


def exchange(x):
    return lax.all_to_all(x, "gz", split_axis=0, concat_axis=0, tiled=True)


def coded(a_slice):
    return jnp.round(a_slice * (STEPS / REACH)).astype(jnp.int16)


def shards(volume, tf_index, tf_color, tf_opacity, order):
    devices = lax.axis_size("gz")
    slices, height, width = volume.shape
    up = [(i, i + 1) for i in range(devices - 1)]
    down = [(j, i) for i, j in up]
    last, initial = coded(volume[slices - 1]), coded(volume[0])
    before = lax.ppermute(last, "gz", up)
    after = lax.ppermute(initial, "gz", down)
    turns = PLANES if devices == PLANES * PLANES and height // devices == BLOCK else 1
    own, *others, volume, tf_index = opacities(volume, tf_index, tf_opacity, turns)
    colour = by_owner(colours(volume, tf_index, before, after, tf_color, tf_opacity), devices)
    if turns == 1:
        return blend_plain(order, exchange(colour), exchange(by_owner(own, devices)))
    shifted = [
        lax.ppermute(part, "gz", [(i, (i + s * turns) % devices) for i in range(devices)])
        for s, part in enumerate(others, 1)
    ]
    shifted, colour = lax.optimization_barrier((shifted, colour))
    mine, *swapped = regroup([own] + shifted)
    swapped = [lax.ppermute(part, "gz", [(i, i ^ m) for i in range(devices)]) for m, part in enumerate(swapped, 1)]
    return blend(order, exchange(colour), [mine] + swapped)


def solution(mesh):
    placed = (P("gz", "frames", None), P("gz", "frames", None), P(), P(), P("frames"))
    return jax.shard_map(
        shards, mesh=mesh, in_specs=placed, out_specs=P("frames", "gz", None), check_vma=False
    )
```

```python
import functools

import jax
import jax.numpy as jnp
from jax import lax
from jax.experimental import pallas as pl
from jax.experimental.pallas import tpu as pltpu
from jax.sharding import PartitionSpec as P

REACH = 6.0
STEPS = 32767.0
BLOCK = 16
LANES = 128
PAD = 8
NT = 8
LIMIT = 24 * 1024 * 1024
FETCH_LIMIT = 43 * 1024 * 1024
CODED_LIMIT = 51 * 1024 * 1024
BLEND_LIMIT = 16 * 1024 * 1024
PLANES = 4


def spread(table_ref, *row):
    sublane = lax.broadcasted_iota(jnp.int32, (NT, LANES), 0)
    table = jnp.zeros((NT, LANES), jnp.float32)
    for m in range(NT):
        table = jnp.where(sublane == m, table_ref[(*row, m)], table)
    return table


def lookup(table, index):
    parts = [
        jnp.take_along_axis(table, index[r : r + NT], axis=0, mode="promise_in_bounds")
        for r in range(0, index.shape[0], NT)
    ]
    return jnp.concatenate(parts, 0)


def alpha_of(centre, index, table):
    return lookup(table, index) * (1.0 - jnp.exp(-centre * centre))


def opacity_kernel(slices, tiles, turns, volume_hbm, index_hbm, opacity_ref, *rest):
    out_refs, (vol, idx, sems) = rest[:turns], rest[turns:]
    height = vol.shape[1] // turns
    plane = lax.axis_index("gz") // (lax.axis_size("gz") // turns)
    bases = [pl.multiple_of(lax.rem(plane + turn, turns) * height, height) for turn in range(turns)]
    copies = []
    for turn, base in enumerate(bases):
        some = pl.ds(base, height)
        pair = [
            pltpu.make_async_copy(source.at[:, some, :], target.at[:, some, :], sems.at[kind, turn])
            for kind, (source, target) in enumerate([(volume_hbm, vol), (index_hbm, idx)])
        ]
        for copy in pair:
            copy.start()
        copies.append(pair)
    table = spread(opacity_ref)
    for base, pair, out_ref in zip(bases, copies, out_refs):
        for copy in pair:
            copy.wait()

        @pl.loop(0, height // BLOCK)
        def _(i):
            rows = pl.ds(pl.multiple_of(base + i * BLOCK, BLOCK), BLOCK)
            for t in range(tiles):
                cols = pl.ds(t * LANES, LANES)
                transmit = None
                for k in range(slices):
                    clear = 1.0 - alpha_of(vol[k, rows, cols], idx[k, rows, cols], table)
                    transmit = clear if transmit is None else transmit * clear
                out_ref[i, :, cols] = (1.0 - transmit).astype(jnp.bfloat16)


def opacities(volume, tf_index, tf_opacity, turns):
    slices, height, width = volume.shape
    part = jax.ShapeDtypeStruct((height // BLOCK // turns, BLOCK, width), jnp.bfloat16)
    held = [jax.ShapeDtypeStruct(x.shape, x.dtype) for x in (volume, tf_index)]
    return pl.pallas_call(
        functools.partial(opacity_kernel, slices, width // LANES, turns),
        out_shape=[part] * turns + held,
        in_specs=[pl.BlockSpec(memory_space=pltpu.HBM)] * 2 + [pl.BlockSpec(memory_space=pltpu.SMEM)],
        out_specs=[pl.BlockSpec(memory_space=pltpu.VMEM)] * (turns + 2),
        scratch_shapes=[pltpu.SemaphoreType.DMA((2, turns))],
        compiler_params=pltpu.CompilerParams(vmem_limit_bytes=FETCH_LIMIT),
        cost_estimate=pl.CostEstimate(
            flops=15 * volume.size, bytes_accessed=9 * volume.size, transcendentals=volume.size
        ),
        name="opacities",
    )(volume, tf_index, tf_opacity)


def colour_kernel(
    slices, tiles, vol, idx, before_ref, after_ref, colour_ref, opacity_ref, out_ref
):
    height = before_ref.shape[0]
    blocks = height // BLOCK
    lane = lax.broadcasted_iota(jnp.int32, (BLOCK, LANES), 1)
    first_lane, last_lane = lane == 0, lane == LANES - 1
    sublane = lax.broadcasted_iota(jnp.int32, (PAD, LANES), 0)
    first_row, last_row = sublane == 0, sublane == PAD - 1
    opacity_table = spread(opacity_ref)
    colour_tables = [spread(colour_ref, c) for c in range(3)]

    def shade(i):
        start = pl.multiple_of(i * BLOCK, BLOCK)
        rows = pl.ds(start, BLOCK)
        above = pl.ds(pl.multiple_of(jnp.maximum(start - PAD, 0), PAD), PAD)
        below = pl.ds(pl.multiple_of(jnp.minimum(start + BLOCK, height - PAD), PAD), PAD)
        for t in range(tiles):
            cols = pl.ds(t * LANES, LANES)
            halo = [ref[rows, cols].astype(jnp.float32) * (REACH / STEPS) for ref in (before_ref, after_ref)]
            centres = [halo[0]] + [vol[k, rows, cols] for k in range(slices)] + [halo[1]]
            transmit, sums = None, None
            for k in range(slices):
                centre = centres[k + 1]
                depth = centres[k + 2] - centres[k]
                upper = jnp.where(i > 0, vol[k, above, cols], 0.0)
                lower = jnp.where(i + 1 < blocks, vol[k, below, cols], 0.0)
                eights = [upper] + [centre[r : r + PAD] for r in range(0, BLOCK, PAD)] + [lower]
                across = jnp.concatenate(
                    [
                        pltpu.roll(jnp.where(first_row, eights[e + 1], eights[e]), PAD - 1, 0)
                        - pltpu.roll(jnp.where(last_row, eights[e - 1], eights[e]), 1, 0)
                        for e in range(1, len(eights) - 1)
                    ],
                    0,
                )
                beside_left = vol[k, rows, pl.ds((t - 1) * LANES, LANES)] if t > 0 else 0.0
                beside_right = vol[k, rows, pl.ds((t + 1) * LANES, LANES)] if t + 1 < tiles else 0.0
                left = pltpu.roll(jnp.where(last_lane, beside_left, centre), 1, 1)
                right = pltpu.roll(jnp.where(first_lane, beside_right, centre), LANES - 1, 1)
                along = right - left
                facing = jnp.abs((0.65 * 0.48) * depth + (0.65 * 0.6) * across + (0.65 * 0.64) * along)
                squares = depth * depth + across * across + along * along + 4.0
                shading = 0.35 + facing * lax.rsqrt(squares)
                index = idx[k, rows, cols]
                alpha = alpha_of(centre, index, opacity_table)
                shown = shading * alpha
                if transmit is not None:
                    shown = transmit * shown
                terms = [lookup(table, index) * shown for table in colour_tables]
                sums = terms if sums is None else [s + add for s, add in zip(sums, terms)]
                if k + 1 < slices:
                    transmit = 1.0 - alpha if transmit is None else transmit * (1.0 - alpha)
            for c in range(3):
                out_ref[i, c, :, cols] = sums[c].astype(jnp.bfloat16)

    @pl.loop(0, blocks)
    def _(i):
        shade(i)


def colours(volume, tf_index, before, after, tf_color, tf_opacity):
    slices, height, width = volume.shape
    blocks = height // BLOCK
    shape = (blocks, 3, BLOCK, width)
    return pl.pallas_call(
        functools.partial(colour_kernel, slices, width // LANES),
        out_shape=jax.ShapeDtypeStruct(shape, jnp.bfloat16),
        in_specs=[pl.BlockSpec(memory_space=pltpu.VMEM)] * 4 + [pl.BlockSpec(memory_space=pltpu.SMEM)] * 2,
        out_specs=pl.BlockSpec(memory_space=pltpu.VMEM),
        compiler_params=pltpu.CompilerParams(vmem_limit_bytes=LIMIT),
        cost_estimate=pl.CostEstimate(
            flops=50 * volume.size, bytes_accessed=40 * volume.size, transcendentals=2 * volume.size
        ),
        name="colours",
    )(volume, tf_index, before, after, tf_color, tf_opacity)


def regroup_kernel(turns, *refs):
    here = lax.rem(lax.axis_index("gz"), turns)
    for s, ref in enumerate(refs[:turns]):
        for m, out_ref in enumerate(refs[turns:]):
            out_ref[s] = ref[here ^ m]


def regroup(parts):
    turns = len(parts)
    return pl.pallas_call(
        functools.partial(regroup_kernel, turns),
        out_shape=[jax.ShapeDtypeStruct(parts[0].shape, parts[0].dtype)] * turns,
        in_specs=[pl.BlockSpec(memory_space=pltpu.VMEM)] * turns,
        out_specs=[pl.BlockSpec(memory_space=pltpu.VMEM)] * turns,
        compiler_params=pltpu.CompilerParams(vmem_limit_bytes=BLEND_LIMIT),
        name="regroup",
    )(*parts)


def blend_kernel(ranks, turns, order_ref, colour_ref, *rest):
    opacity_refs, (out_ref, place, opacity_ref) = rest[:turns], rest[turns:]
    device = lax.axis_index("gz")
    plane, member = device // turns, lax.rem(device, turns)
    for b in range(ranks):
        place[order_ref[b]] = b
    for m, ref in enumerate(opacity_refs):
        for s in range(turns):
            brick = lax.rem(plane + turns - s, turns) * turns + (member ^ m)
            opacity_ref[brick] = ref[s]
    for j in range(colour_ref.shape[3] // LANES):
        cols = pl.ds(j * LANES, LANES)
        canvas = (jnp.zeros((colour_ref.shape[2], LANES), jnp.float32),) * 4
        for rank in range(ranks):
            b = place[rank]
            clear = 1.0 - canvas[3]
            layers = [colour_ref[b, c, :, cols] for c in range(3)] + [opacity_ref[b, :, cols]]
            canvas = tuple(front + clear * back.astype(jnp.float32) for front, back in zip(canvas, layers))
        for c in range(4):
            out_ref[c, :, cols] = canvas[c]


def blend(order, colour, opacity_parts):
    ranks, channels, height, width = colour.shape
    turns = len(opacity_parts)
    return pl.pallas_call(
        functools.partial(blend_kernel, ranks, turns),
        out_shape=jax.ShapeDtypeStruct((4, height, width), jnp.float32),
        in_specs=[pl.BlockSpec(memory_space=pltpu.SMEM)] + [pl.BlockSpec(memory_space=pltpu.VMEM)] * (1 + turns),
        out_specs=pl.BlockSpec(memory_space=pltpu.VMEM),
        scratch_shapes=[pltpu.SMEM((ranks,), jnp.int32), pltpu.VMEM((ranks, height, width), colour.dtype)],
        compiler_params=pltpu.CompilerParams(vmem_limit_bytes=BLEND_LIMIT),
        name="blend",
    )(order, colour, *opacity_parts)


def blend_plain(order, colour, opacity):
    ranks = opacity.shape[0]
    place = jnp.zeros((ranks,), jnp.int32).at[order].set(jnp.arange(ranks, dtype=jnp.int32))
    layers = jnp.concatenate([colour, opacity[:, None]], 1)

    def step(canvas, b):
        layer = lax.dynamic_index_in_dim(layers, b, 0, keepdims=False).astype(jnp.float32)
        return canvas + (1.0 - canvas[3:4]) * layer, None

    return lax.scan(step, jnp.zeros(layers.shape[1:], jnp.float32), place)[0]


def by_owner(blocks_first, devices):
    blocks, width = blocks_first.shape[0], blocks_first.shape[-1]
    middle = blocks_first.shape[1:-2]
    if blocks == devices:
        return blocks_first
    each = devices // blocks
    split = blocks_first.reshape((blocks,) + middle + (each, BLOCK // each, width))
    moved = jnp.moveaxis(split, len(middle) + 1, 1)
    return moved.reshape((devices,) + middle + (BLOCK // each, width))


def exchange(x):
    return lax.all_to_all(x, "gz", split_axis=0, concat_axis=0, tiled=True)


def coded_kernel(pieces, volume_hbm, *rest):
    out_refs, (here, sems) = rest[:2], rest[2:]
    height = here.shape[1] // pieces
    copies = [
        pltpu.make_async_copy(
            volume_hbm.at[k, pl.ds(p * height, height), :], here.at[n, pl.ds(p * height, height), :], sems.at[n, p]
        )
        for n, k in enumerate([0, volume_hbm.shape[0] - 1])
        for p in range(pieces)
    ]
    for copy in copies:
        copy.start()
    for n, out_ref in enumerate(out_refs):
        for p in range(pieces):
            copies[n * pieces + p].wait()

            @pl.loop(0, height // BLOCK)
            def _(i):
                rows = pl.ds(pl.multiple_of(p * height + i * BLOCK, BLOCK), BLOCK)
                out_ref[rows, :] = jnp.round(here[n, rows, :] * (STEPS / REACH)).astype(jnp.int32).astype(jnp.int16)


def coded(volume):
    _, height, width = volume.shape
    part = jax.ShapeDtypeStruct((height, width), jnp.int16)
    return pl.pallas_call(
        functools.partial(coded_kernel, PLANES),
        out_shape=[part] * 2,
        in_specs=[pl.BlockSpec(memory_space=pltpu.HBM)],
        out_specs=[pl.BlockSpec(memory_space=pltpu.VMEM)] * 2,
        scratch_shapes=[pltpu.VMEM((2, height, width), volume.dtype), pltpu.SemaphoreType.DMA((2, PLANES))],
        compiler_params=pltpu.CompilerParams(vmem_limit_bytes=CODED_LIMIT),
        name="coded",
    )(volume)


def shards(volume, tf_index, tf_color, tf_opacity, order):
    devices = lax.axis_size("gz")
    slices, height, width = volume.shape
    up = [(i, i + 1) for i in range(devices - 1)]
    down = [(j, i) for i, j in up]
    initial, last = coded(volume)
    before = lax.ppermute(last, "gz", up)
    after = lax.ppermute(initial, "gz", down)
    turns = PLANES if devices == PLANES * PLANES and height // devices == BLOCK else 1
    own, *others, volume, tf_index = opacities(volume, tf_index, tf_opacity, turns)
    colour = by_owner(colours(volume, tf_index, before, after, tf_color, tf_opacity), devices)
    if turns == 1:
        return blend_plain(order, exchange(colour), exchange(by_owner(own, devices)))
    shifted = [
        lax.ppermute(part, "gz", [(i, (i + s * turns) % devices) for i in range(devices)])
        for s, part in enumerate(others, 1)
    ]
    shifted, colour = lax.optimization_barrier((shifted, colour))
    mine, *swapped = regroup([own] + shifted)
    swapped = [lax.ppermute(part, "gz", [(i, i ^ m) for i in range(devices)]) for m, part in enumerate(swapped, 1)]
    return blend(order, exchange(colour), [mine] + swapped)


def solution(mesh):
    placed = (P("gz", "frames", None), P("gz", "frames", None), P(), P(), P("frames"))
    return jax.shard_map(
        shards, mesh=mesh, in_specs=placed, out_specs=P("frames", "gz", None), check_vma=False
    )
```

```python
import functools

import jax
import jax.numpy as jnp
from jax import lax
from jax.experimental import pallas as pl
from jax.experimental.pallas import tpu as pltpu
from jax.sharding import PartitionSpec as P

REACH = 6.0
STEPS = 32767.0
BLOCK = 16
LANES = 128
PAD = 8
NT = 8
LIMIT = 24 * 1024 * 1024
FETCH_LIMIT = 43 * 1024 * 1024
CODED_LIMIT = 51 * 1024 * 1024
BLEND_LIMIT = 16 * 1024 * 1024
PLANES = 4


def spread(table_ref, *row):
    sublane = lax.broadcasted_iota(jnp.int32, (NT, LANES), 0)
    table = jnp.zeros((NT, LANES), jnp.float32)
    for m in range(NT):
        table = jnp.where(sublane == m, table_ref[(*row, m)], table)
    return table


def lookup(table, index):
    parts = [
        jnp.take_along_axis(table, index[r : r + NT], axis=0, mode="promise_in_bounds")
        for r in range(0, index.shape[0], NT)
    ]
    return jnp.concatenate(parts, 0)


def alpha_of(centre, index, table):
    return lookup(table, index) * (1.0 - jnp.exp(-centre * centre))


def opacity_kernel(slices, tiles, turns, volume_hbm, index_hbm, opacity_ref, *rest):
    out_refs, (vol, idx, sems) = rest[:turns], rest[turns:]
    height = vol.shape[1] // turns
    plane = lax.axis_index("gz") // (lax.axis_size("gz") // turns)
    bases = [pl.multiple_of(lax.rem(plane + turn, turns) * height, height) for turn in range(turns)]
    copies = []
    for turn, base in enumerate(bases):
        some = pl.ds(base, height)
        pair = [
            pltpu.make_async_copy(source.at[:, some, :], target.at[:, some, :], sems.at[kind, turn])
            for kind, (source, target) in enumerate([(volume_hbm, vol), (index_hbm, idx)])
        ]
        for copy in pair:
            copy.start()
        copies.append(pair)
    table = spread(opacity_ref)
    for base, pair, out_ref in zip(bases, copies, out_refs):
        for copy in pair:
            copy.wait()

        @pl.loop(0, height // BLOCK)
        def _(i):
            rows = pl.ds(pl.multiple_of(base + i * BLOCK, BLOCK), BLOCK)
            for t in range(tiles):
                cols = pl.ds(t * LANES, LANES)
                transmit = None
                for k in range(slices):
                    clear = 1.0 - alpha_of(vol[k, rows, cols], idx[k, rows, cols], table)
                    transmit = clear if transmit is None else transmit * clear
                out_ref[i, :, cols] = (1.0 - transmit).astype(jnp.bfloat16)


def opacities(volume, tf_index, tf_opacity, turns):
    slices, height, width = volume.shape
    part = jax.ShapeDtypeStruct((height // BLOCK // turns, BLOCK, width), jnp.bfloat16)
    held = [jax.ShapeDtypeStruct(x.shape, x.dtype) for x in (volume, tf_index)]
    return pl.pallas_call(
        functools.partial(opacity_kernel, slices, width // LANES, turns),
        out_shape=[part] * turns + held,
        in_specs=[pl.BlockSpec(memory_space=pltpu.HBM)] * 2 + [pl.BlockSpec(memory_space=pltpu.SMEM)],
        out_specs=[pl.BlockSpec(memory_space=pltpu.VMEM)] * (turns + 2),
        scratch_shapes=[pltpu.SemaphoreType.DMA((2, turns))],
        compiler_params=pltpu.CompilerParams(vmem_limit_bytes=FETCH_LIMIT),
        cost_estimate=pl.CostEstimate(
            flops=15 * volume.size, bytes_accessed=9 * volume.size, transcendentals=volume.size
        ),
        name="opacities",
    )(volume, tf_index, tf_opacity)


def colour_kernel(
    slices, tiles, vol, idx, after_ref, before_ref, colour_ref, opacity_ref, out_ref
):
    height = before_ref.shape[0]
    blocks = height // BLOCK
    lane = lax.broadcasted_iota(jnp.int32, (BLOCK, LANES), 1)
    first_lane, last_lane = lane == 0, lane == LANES - 1
    sublane = lax.broadcasted_iota(jnp.int32, (PAD, LANES), 0)
    first_row, last_row = sublane == 0, sublane == PAD - 1
    opacity_table = spread(opacity_ref)
    colour_tables = [spread(colour_ref, c) for c in range(3)]

    def shade(i):
        start = pl.multiple_of(i * BLOCK, BLOCK)
        rows = pl.ds(start, BLOCK)
        above = pl.ds(pl.multiple_of(jnp.maximum(start - PAD, 0), PAD), PAD)
        below = pl.ds(pl.multiple_of(jnp.minimum(start + BLOCK, height - PAD), PAD), PAD)
        for t in range(tiles):
            cols = pl.ds(t * LANES, LANES)
            halo = [ref[rows, cols].astype(jnp.float32) * (REACH / STEPS) for ref in (before_ref, after_ref)]
            centres = [halo[0]] + [vol[k, rows, cols] for k in range(slices)] + [halo[1]]
            transmit, sums = None, None
            for k in range(slices):
                centre = centres[k + 1]
                depth = centres[k + 2] - centres[k]
                upper = jnp.where(i > 0, vol[k, above, cols], 0.0)
                lower = jnp.where(i + 1 < blocks, vol[k, below, cols], 0.0)
                eights = [upper] + [centre[r : r + PAD] for r in range(0, BLOCK, PAD)] + [lower]
                across = jnp.concatenate(
                    [
                        pltpu.roll(jnp.where(first_row, eights[e + 1], eights[e]), PAD - 1, 0)
                        - pltpu.roll(jnp.where(last_row, eights[e - 1], eights[e]), 1, 0)
                        for e in range(1, len(eights) - 1)
                    ],
                    0,
                )
                beside_left = vol[k, rows, pl.ds((t - 1) * LANES, LANES)] if t > 0 else 0.0
                beside_right = vol[k, rows, pl.ds((t + 1) * LANES, LANES)] if t + 1 < tiles else 0.0
                left = pltpu.roll(jnp.where(last_lane, beside_left, centre), 1, 1)
                right = pltpu.roll(jnp.where(first_lane, beside_right, centre), LANES - 1, 1)
                along = right - left
                facing = jnp.abs((0.65 * 0.48) * depth + (0.65 * 0.6) * across + (0.65 * 0.64) * along)
                squares = depth * depth + across * across + along * along + 4.0
                shading = 0.35 + facing * lax.rsqrt(squares)
                index = idx[k, rows, cols]
                alpha = alpha_of(centre, index, opacity_table)
                shown = shading * alpha
                if transmit is not None:
                    shown = transmit * shown
                terms = [lookup(table, index) * shown for table in colour_tables]
                sums = terms if sums is None else [s + add for s, add in zip(sums, terms)]
                if k + 1 < slices:
                    transmit = 1.0 - alpha if transmit is None else transmit * (1.0 - alpha)
            for c in range(3):
                out_ref[i, c, :, cols] = sums[c].astype(jnp.bfloat16)

    @pl.loop(0, blocks)
    def _(i):
        shade(i)


def colours(volume, tf_index, before, after, tf_color, tf_opacity):
    slices, height, width = volume.shape
    blocks = height // BLOCK
    shape = (blocks, 3, BLOCK, width)
    return pl.pallas_call(
        functools.partial(colour_kernel, slices, width // LANES),
        out_shape=jax.ShapeDtypeStruct(shape, jnp.bfloat16),
        in_specs=[pl.BlockSpec(memory_space=pltpu.VMEM)] * 4 + [pl.BlockSpec(memory_space=pltpu.SMEM)] * 2,
        out_specs=pl.BlockSpec(memory_space=pltpu.VMEM),
        compiler_params=pltpu.CompilerParams(vmem_limit_bytes=LIMIT),
        cost_estimate=pl.CostEstimate(
            flops=50 * volume.size, bytes_accessed=40 * volume.size, transcendentals=2 * volume.size
        ),
        name="colours",
    )(volume, tf_index, after, before, tf_color, tf_opacity)


def regroup_kernel(turns, *refs):
    here = lax.rem(lax.axis_index("gz"), turns)
    for s, ref in enumerate(refs[:turns]):
        for m, out_ref in enumerate(refs[turns:]):
            out_ref[s] = ref[here ^ m]


def regroup(parts):
    turns = len(parts)
    return pl.pallas_call(
        functools.partial(regroup_kernel, turns),
        out_shape=[jax.ShapeDtypeStruct(parts[0].shape, parts[0].dtype)] * turns,
        in_specs=[pl.BlockSpec(memory_space=pltpu.VMEM)] * turns,
        out_specs=[pl.BlockSpec(memory_space=pltpu.VMEM)] * turns,
        compiler_params=pltpu.CompilerParams(vmem_limit_bytes=BLEND_LIMIT),
        name="regroup",
    )(*parts)


def blend_kernel(ranks, turns, order_ref, colour_ref, *rest):
    opacity_refs, (out_ref, place, opacity_ref) = rest[:turns], rest[turns:]
    device = lax.axis_index("gz")
    plane, member = device // turns, lax.rem(device, turns)
    for b in range(ranks):
        place[order_ref[b]] = b
    for m, ref in enumerate(opacity_refs):
        for s in range(turns):
            brick = lax.rem(plane + turns - s, turns) * turns + (member ^ m)
            opacity_ref[brick] = ref[s]
    for j in range(colour_ref.shape[3] // LANES):
        cols = pl.ds(j * LANES, LANES)
        canvas = (jnp.zeros((colour_ref.shape[2], LANES), jnp.float32),) * 4
        for rank in range(ranks):
            b = place[rank]
            clear = 1.0 - canvas[3]
            layers = [colour_ref[b, c, :, cols] for c in range(3)] + [opacity_ref[b, :, cols]]
            canvas = tuple(front + clear * back.astype(jnp.float32) for front, back in zip(canvas, layers))
        for c in range(4):
            out_ref[c, :, cols] = canvas[c]


def blend(order, colour, opacity_parts):
    ranks, channels, height, width = colour.shape
    turns = len(opacity_parts)
    return pl.pallas_call(
        functools.partial(blend_kernel, ranks, turns),
        out_shape=jax.ShapeDtypeStruct((4, height, width), jnp.float32),
        in_specs=[pl.BlockSpec(memory_space=pltpu.SMEM)] + [pl.BlockSpec(memory_space=pltpu.VMEM)] * (1 + turns),
        out_specs=pl.BlockSpec(memory_space=pltpu.VMEM),
        scratch_shapes=[pltpu.SMEM((ranks,), jnp.int32), pltpu.VMEM((ranks, height, width), colour.dtype)],
        compiler_params=pltpu.CompilerParams(vmem_limit_bytes=BLEND_LIMIT),
        name="blend",
    )(order, colour, *opacity_parts)


def blend_plain(order, colour, opacity):
    ranks = opacity.shape[0]
    place = jnp.zeros((ranks,), jnp.int32).at[order].set(jnp.arange(ranks, dtype=jnp.int32))
    layers = jnp.concatenate([colour, opacity[:, None]], 1)

    def step(canvas, b):
        layer = lax.dynamic_index_in_dim(layers, b, 0, keepdims=False).astype(jnp.float32)
        return canvas + (1.0 - canvas[3:4]) * layer, None

    return lax.scan(step, jnp.zeros(layers.shape[1:], jnp.float32), place)[0]


def by_owner(blocks_first, devices):
    blocks, width = blocks_first.shape[0], blocks_first.shape[-1]
    middle = blocks_first.shape[1:-2]
    if blocks == devices:
        return blocks_first
    each = devices // blocks
    split = blocks_first.reshape((blocks,) + middle + (each, BLOCK // each, width))
    moved = jnp.moveaxis(split, len(middle) + 1, 1)
    return moved.reshape((devices,) + middle + (BLOCK // each, width))


def exchange(x):
    return lax.all_to_all(x, "gz", split_axis=0, concat_axis=0, tiled=True)


def coded_kernel(pieces, volume_hbm, *rest):
    out_refs, (here, sems) = rest[:2], rest[2:]
    height = here.shape[1] // pieces
    copies = [
        pltpu.make_async_copy(
            volume_hbm.at[k, pl.ds(p * height, height), :], here.at[n, pl.ds(p * height, height), :], sems.at[n, p]
        )
        for n, k in enumerate([0, volume_hbm.shape[0] - 1])
        for p in range(pieces)
    ]
    for copy in copies:
        copy.start()
    for n, out_ref in enumerate(out_refs):
        for p in range(pieces):
            copies[n * pieces + p].wait()

            @pl.loop(0, height // BLOCK)
            def _(i):
                rows = pl.ds(pl.multiple_of(p * height + i * BLOCK, BLOCK), BLOCK)
                out_ref[rows, :] = jnp.round(here[n, rows, :] * (STEPS / REACH)).astype(jnp.int32).astype(jnp.int16)


def coded(volume):
    _, height, width = volume.shape
    part = jax.ShapeDtypeStruct((height, width), jnp.int16)
    return pl.pallas_call(
        functools.partial(coded_kernel, PLANES),
        out_shape=[part] * 2,
        in_specs=[pl.BlockSpec(memory_space=pltpu.HBM)],
        out_specs=[pl.BlockSpec(memory_space=pltpu.VMEM)] * 2,
        scratch_shapes=[pltpu.VMEM((2, height, width), volume.dtype), pltpu.SemaphoreType.DMA((2, PLANES))],
        compiler_params=pltpu.CompilerParams(vmem_limit_bytes=CODED_LIMIT),
        name="coded",
    )(volume)


def shards(volume, tf_index, tf_color, tf_opacity, order):
    devices = lax.axis_size("gz")
    slices, height, width = volume.shape
    up = [(i, i + 1) for i in range(devices - 1)]
    down = [(j, i) for i, j in up]
    initial, last = coded(volume)
    after = lax.ppermute(initial, "gz", down)
    before = lax.ppermute(last, "gz", up)
    turns = PLANES if devices == PLANES * PLANES and height // devices == BLOCK else 1
    own, *others, volume, tf_index = opacities(volume, tf_index, tf_opacity, turns)
    colour = by_owner(colours(volume, tf_index, before, after, tf_color, tf_opacity), devices)
    if turns == 1:
        return blend_plain(order, exchange(colour), exchange(by_owner(own, devices)))
    shifted = [
        lax.ppermute(part, "gz", [(i, (i + s * turns) % devices) for i in range(devices)])
        for s, part in enumerate(others, 1)
    ]
    shifted, colour = lax.optimization_barrier((shifted, colour))
    mine, *swapped = regroup([own] + shifted)
    swapped = [lax.ppermute(part, "gz", [(i, i ^ m) for i in range(devices)]) for m, part in enumerate(swapped, 1)]
    return blend(order, exchange(colour), [mine] + swapped)


def solution(mesh):
    placed = (P("gz", "frames", None), P("gz", "frames", None), P(), P(), P("frames"))
    return jax.shard_map(
        shards, mesh=mesh, in_specs=placed, out_specs=P("frames", "gz", None), check_vma=False
    )
```

```python
import functools

import jax
import jax.numpy as jnp
from jax import lax
from jax.experimental import pallas as pl
from jax.experimental.pallas import tpu as pltpu
from jax.sharding import PartitionSpec as P

REACH = 6.0
STEPS = 32767.0
BLOCK = 16
LANES = 128
WIDE = 256
PAD = 8
NT = 8
LIMIT = 24 * 1024 * 1024
FETCH_LIMIT = 43 * 1024 * 1024
CODED_LIMIT = 51 * 1024 * 1024
BLEND_LIMIT = 16 * 1024 * 1024
PLANES = 4


def spread(table_ref, *row):
    sublane = lax.broadcasted_iota(jnp.int32, (NT, LANES), 0)
    table = jnp.zeros((NT, LANES), jnp.float32)
    for m in range(NT):
        table = jnp.where(sublane == m, table_ref[(*row, m)], table)
    return table


def lookup(table, index):
    parts = [
        jnp.take_along_axis(table, index[r : r + NT], axis=0, mode="promise_in_bounds")
        for r in range(0, index.shape[0], NT)
    ]
    return jnp.concatenate(parts, 0)


def alpha_of(centre, index, table):
    return lookup(table, index) * (1.0 - jnp.exp(-centre * centre))


def opacity_kernel(slices, tiles, turns, volume_hbm, index_hbm, opacity_ref, *rest):
    out_refs, (vol, idx, sems) = rest[:turns], rest[turns:]
    height = vol.shape[1] // turns
    plane = lax.axis_index("gz") // (lax.axis_size("gz") // turns)
    bases = [pl.multiple_of(lax.rem(plane + turn, turns) * height, height) for turn in range(turns)]
    copies = []
    for turn, base in enumerate(bases):
        some = pl.ds(base, height)
        pair = [
            pltpu.make_async_copy(source.at[:, some, :], target.at[:, some, :], sems.at[kind, turn])
            for kind, (source, target) in enumerate([(volume_hbm, vol), (index_hbm, idx)])
        ]
        for copy in pair:
            copy.start()
        copies.append(pair)
    table = spread(opacity_ref)
    for base, pair, out_ref in zip(bases, copies, out_refs):
        for copy in pair:
            copy.wait()

        @pl.loop(0, height // BLOCK)
        def _(i):
            rows = pl.ds(pl.multiple_of(base + i * BLOCK, BLOCK), BLOCK)
            for t in range(tiles):
                cols = pl.ds(t * LANES, LANES)
                transmit = None
                for k in range(slices):
                    clear = 1.0 - alpha_of(vol[k, rows, cols], idx[k, rows, cols], table)
                    transmit = clear if transmit is None else transmit * clear
                out_ref[i, :, cols] = (1.0 - transmit).astype(jnp.bfloat16)


def opacities(volume, tf_index, tf_opacity, turns):
    slices, height, width = volume.shape
    part = jax.ShapeDtypeStruct((height // BLOCK // turns, BLOCK, width), jnp.bfloat16)
    held = [jax.ShapeDtypeStruct(x.shape, x.dtype) for x in (volume, tf_index)]
    return pl.pallas_call(
        functools.partial(opacity_kernel, slices, width // LANES, turns),
        out_shape=[part] * turns + held,
        in_specs=[pl.BlockSpec(memory_space=pltpu.HBM)] * 2 + [pl.BlockSpec(memory_space=pltpu.SMEM)],
        out_specs=[pl.BlockSpec(memory_space=pltpu.VMEM)] * (turns + 2),
        scratch_shapes=[pltpu.SemaphoreType.DMA((2, turns))],
        compiler_params=pltpu.CompilerParams(vmem_limit_bytes=FETCH_LIMIT),
        cost_estimate=pl.CostEstimate(
            flops=15 * volume.size, bytes_accessed=9 * volume.size, transcendentals=volume.size
        ),
        name="opacities",
    )(volume, tf_index, tf_opacity)


def colour_kernel(
    slices, tiles, vol, idx, after_ref, before_ref, colour_ref, opacity_ref, out_ref
):
    height = before_ref.shape[0]
    blocks = height // BLOCK
    lane = lax.broadcasted_iota(jnp.int32, (BLOCK, LANES), 1)
    first_lane, last_lane = lane == 0, lane == LANES - 1
    sublane = lax.broadcasted_iota(jnp.int32, (PAD, LANES), 0)
    first_row, last_row = sublane == 0, sublane == PAD - 1
    opacity_table = spread(opacity_ref)
    colour_tables = [spread(colour_ref, c) for c in range(3)]

    def shade(i):
        start = pl.multiple_of(i * BLOCK, BLOCK)
        rows = pl.ds(start, BLOCK)
        above = pl.ds(pl.multiple_of(jnp.maximum(start - PAD, 0), PAD), PAD)
        below = pl.ds(pl.multiple_of(jnp.minimum(start + BLOCK, height - PAD), PAD), PAD)
        for t in range(tiles):
            cols = pl.ds(t * LANES, LANES)
            halo = [ref[rows, cols].astype(jnp.float32) * (REACH / STEPS) for ref in (before_ref, after_ref)]
            centres = [halo[0]] + [vol[k, rows, cols] for k in range(slices)] + [halo[1]]
            transmit, sums = None, None
            for k in range(slices):
                centre = centres[k + 1]
                depth = centres[k + 2] - centres[k]
                upper = jnp.where(i > 0, vol[k, above, cols], 0.0)
                lower = jnp.where(i + 1 < blocks, vol[k, below, cols], 0.0)
                eights = [upper] + [centre[r : r + PAD] for r in range(0, BLOCK, PAD)] + [lower]
                across = jnp.concatenate(
                    [
                        pltpu.roll(jnp.where(first_row, eights[e + 1], eights[e]), PAD - 1, 0)
                        - pltpu.roll(jnp.where(last_row, eights[e - 1], eights[e]), 1, 0)
                        for e in range(1, len(eights) - 1)
                    ],
                    0,
                )
                beside_left = vol[k, rows, pl.ds((t - 1) * LANES, LANES)] if t > 0 else 0.0
                beside_right = vol[k, rows, pl.ds((t + 1) * LANES, LANES)] if t + 1 < tiles else 0.0
                left = pltpu.roll(jnp.where(last_lane, beside_left, centre), 1, 1)
                right = pltpu.roll(jnp.where(first_lane, beside_right, centre), LANES - 1, 1)
                along = right - left
                facing = jnp.abs((0.65 * 0.48) * depth + (0.65 * 0.6) * across + (0.65 * 0.64) * along)
                squares = depth * depth + across * across + along * along + 4.0
                shading = 0.35 + facing * lax.rsqrt(squares)
                index = idx[k, rows, cols]
                alpha = alpha_of(centre, index, opacity_table)
                shown = shading * alpha
                if transmit is not None:
                    shown = transmit * shown
                terms = [lookup(table, index) * shown for table in colour_tables]
                sums = terms if sums is None else [s + add for s, add in zip(sums, terms)]
                if k + 1 < slices:
                    transmit = 1.0 - alpha if transmit is None else transmit * (1.0 - alpha)
            for c in range(3):
                out_ref[i, c, :, cols] = sums[c].astype(jnp.bfloat16)

    @pl.loop(0, blocks)
    def _(i):
        shade(i)


def colours(volume, tf_index, before, after, tf_color, tf_opacity):
    slices, height, width = volume.shape
    blocks = height // BLOCK
    shape = (blocks, 3, BLOCK, width)
    return pl.pallas_call(
        functools.partial(colour_kernel, slices, width // LANES),
        out_shape=jax.ShapeDtypeStruct(shape, jnp.bfloat16),
        in_specs=[pl.BlockSpec(memory_space=pltpu.VMEM)] * 4 + [pl.BlockSpec(memory_space=pltpu.SMEM)] * 2,
        out_specs=pl.BlockSpec(memory_space=pltpu.VMEM),
        compiler_params=pltpu.CompilerParams(vmem_limit_bytes=LIMIT),
        cost_estimate=pl.CostEstimate(
            flops=50 * volume.size, bytes_accessed=40 * volume.size, transcendentals=2 * volume.size
        ),
        name="colours",
    )(volume, tf_index, after, before, tf_color, tf_opacity)


def regroup_kernel(turns, *refs):
    here = lax.rem(lax.axis_index("gz"), turns)
    for s, ref in enumerate(refs[:turns]):
        for m, out_ref in enumerate(refs[turns:]):
            out_ref[s] = ref[here ^ m]


def regroup(parts):
    turns = len(parts)
    return pl.pallas_call(
        functools.partial(regroup_kernel, turns),
        out_shape=[jax.ShapeDtypeStruct(parts[0].shape, parts[0].dtype)] * turns,
        in_specs=[pl.BlockSpec(memory_space=pltpu.VMEM)] * turns,
        out_specs=[pl.BlockSpec(memory_space=pltpu.VMEM)] * turns,
        compiler_params=pltpu.CompilerParams(vmem_limit_bytes=BLEND_LIMIT),
        name="regroup",
    )(*parts)


def blend_kernel(ranks, turns, order_ref, colour_ref, *rest):
    opacity_refs, (out_ref, place, opacity_ref) = rest[:turns], rest[turns:]
    device = lax.axis_index("gz")
    plane, member = device // turns, lax.rem(device, turns)
    for b in range(ranks):
        place[order_ref[b]] = b
    for m, ref in enumerate(opacity_refs):
        for s in range(turns):
            brick = lax.rem(plane + turns - s, turns) * turns + (member ^ m)
            opacity_ref[brick] = ref[s]
    for j in range(colour_ref.shape[3] // WIDE):
        cols = pl.ds(j * WIDE, WIDE)
        canvas = (jnp.zeros((colour_ref.shape[2], WIDE), jnp.float32),) * 4
        for rank in range(ranks):
            b = place[rank]
            clear = 1.0 - canvas[3]
            layers = [colour_ref[b, c, :, cols] for c in range(3)] + [opacity_ref[b, :, cols]]
            canvas = tuple(front + clear * back.astype(jnp.float32) for front, back in zip(canvas, layers))
        for c in range(4):
            out_ref[c, :, cols] = canvas[c]


def blend(order, colour, opacity_parts):
    ranks, channels, height, width = colour.shape
    turns = len(opacity_parts)
    return pl.pallas_call(
        functools.partial(blend_kernel, ranks, turns),
        out_shape=jax.ShapeDtypeStruct((4, height, width), jnp.float32),
        in_specs=[pl.BlockSpec(memory_space=pltpu.SMEM)] + [pl.BlockSpec(memory_space=pltpu.VMEM)] * (1 + turns),
        out_specs=pl.BlockSpec(memory_space=pltpu.VMEM),
        scratch_shapes=[pltpu.SMEM((ranks,), jnp.int32), pltpu.VMEM((ranks, height, width), colour.dtype)],
        compiler_params=pltpu.CompilerParams(vmem_limit_bytes=BLEND_LIMIT),
        name="blend",
    )(order, colour, *opacity_parts)


def blend_plain(order, colour, opacity):
    ranks = opacity.shape[0]
    place = jnp.zeros((ranks,), jnp.int32).at[order].set(jnp.arange(ranks, dtype=jnp.int32))
    layers = jnp.concatenate([colour, opacity[:, None]], 1)

    def step(canvas, b):
        layer = lax.dynamic_index_in_dim(layers, b, 0, keepdims=False).astype(jnp.float32)
        return canvas + (1.0 - canvas[3:4]) * layer, None

    return lax.scan(step, jnp.zeros(layers.shape[1:], jnp.float32), place)[0]


def by_owner(blocks_first, devices):
    blocks, width = blocks_first.shape[0], blocks_first.shape[-1]
    middle = blocks_first.shape[1:-2]
    if blocks == devices:
        return blocks_first
    each = devices // blocks
    split = blocks_first.reshape((blocks,) + middle + (each, BLOCK // each, width))
    moved = jnp.moveaxis(split, len(middle) + 1, 1)
    return moved.reshape((devices,) + middle + (BLOCK // each, width))


def exchange(x):
    return lax.all_to_all(x, "gz", split_axis=0, concat_axis=0, tiled=True)


def coded_kernel(pieces, volume_hbm, *rest):
    out_refs, (here, sems) = rest[:2], rest[2:]
    height = here.shape[1] // pieces
    copies = [
        pltpu.make_async_copy(
            volume_hbm.at[k, pl.ds(p * height, height), :], here.at[n, pl.ds(p * height, height), :], sems.at[n, p]
        )
        for n, k in enumerate([0, volume_hbm.shape[0] - 1])
        for p in range(pieces)
    ]
    for copy in copies:
        copy.start()
    for n, out_ref in enumerate(out_refs):
        for p in range(pieces):
            copies[n * pieces + p].wait()

            @pl.loop(0, height // BLOCK)
            def _(i):
                rows = pl.ds(pl.multiple_of(p * height + i * BLOCK, BLOCK), BLOCK)
                out_ref[rows, :] = jnp.round(here[n, rows, :] * (STEPS / REACH)).astype(jnp.int32).astype(jnp.int16)


def coded(volume):
    _, height, width = volume.shape
    part = jax.ShapeDtypeStruct((height, width), jnp.int16)
    return pl.pallas_call(
        functools.partial(coded_kernel, PLANES),
        out_shape=[part] * 2,
        in_specs=[pl.BlockSpec(memory_space=pltpu.HBM)],
        out_specs=[pl.BlockSpec(memory_space=pltpu.VMEM)] * 2,
        scratch_shapes=[pltpu.VMEM((2, height, width), volume.dtype), pltpu.SemaphoreType.DMA((2, PLANES))],
        compiler_params=pltpu.CompilerParams(vmem_limit_bytes=CODED_LIMIT),
        name="coded",
    )(volume)


def shards(volume, tf_index, tf_color, tf_opacity, order):
    devices = lax.axis_size("gz")
    slices, height, width = volume.shape
    up = [(i, i + 1) for i in range(devices - 1)]
    down = [(j, i) for i, j in up]
    initial, last = coded(volume)
    after = lax.ppermute(initial, "gz", down)
    before = lax.ppermute(last, "gz", up)
    turns = PLANES if devices == PLANES * PLANES and height // devices == BLOCK else 1
    own, *others, volume, tf_index = opacities(volume, tf_index, tf_opacity, turns)
    colour = by_owner(colours(volume, tf_index, before, after, tf_color, tf_opacity), devices)
    if turns == 1:
        return blend_plain(order, exchange(colour), exchange(by_owner(own, devices)))
    shifted = [
        lax.ppermute(part, "gz", [(i, (i + s * turns) % devices) for i in range(devices)])
        for s, part in enumerate(others, 1)
    ]
    shifted, colour = lax.optimization_barrier((shifted, colour))
    mine, *swapped = regroup([own] + shifted)
    swapped = [lax.ppermute(part, "gz", [(i, i ^ m) for i in range(devices)]) for m, part in enumerate(swapped, 1)]
    return blend(order, exchange(colour), [mine] + swapped)


def solution(mesh):
    placed = (P("gz", "frames", None), P("gz", "frames", None), P(), P(), P("frames"))
    return jax.shard_map(
        shards, mesh=mesh, in_specs=placed, out_specs=P("frames", "gz", None), check_vma=False
    )
```
